256 devices in a mesh: field: 4 (over x), cross: 64 (over y, z, core).
Axes of the slice: x: 4, y: 4, z: 8, core: 2. Of those that a mesh axis runs over, the one named last changes fastest.
Arguments:
- rhs: float32 [4, 64, 8192], P('field', None, 'cross'), may hold values from -12 to 12
- pivot_inverse: bfloat16 [4, 64, 64, 8192], P('field', None, None, 'cross'), as said below
- line_coupling: bfloat16 [4, 64, 64, 8192], P('field', None, None, 'cross'), as said below
- element_block: bfloat16 [4, 64, 64, 8192], P('field', None, None, 'cross'), as said below
- neighbours: int32 [8192, 4], P('cross'), may hold values from 0 to 8191, as said below
- face_type: int32 [8192, 4], P('cross'), may hold values from 0 to 2, as said below
Outputs:
- solution: float32 [4, 64, 8192], P('field', None, 'cross')
- residual: float32 [4, 64, 8192], P('field', None, 'cross')
- precond: float32 [4, 64, 8192], P('field', None, 'cross')
The draws below stay inside these ranges and needn't reach their ends.
Inputs may be any that keep to these rules, and one draw needn't show every extreme that they name: `neighbours`: the lines form a grid of 256 x 32; the lines of cross index c lie in grid columns c * 4 to (c + 1) * 4 - 1, in a scrambled order within the device, and a line's number is c * 128 + its slot. Faces 0 and 1 name the line one column down and up, faces 2 and 3 one row down and up; a face on the duct's wall names the line itself. Neighbours are mutual. `face_type`: 0 on faces between two lines, 1 (conducting wall) or 2 (insulating wall) on faces of the duct's wall, where neighbours names the line itself. `pivot_inverse`: symmetric with a dominant positive diagonal. `line_coupling`: together with element_block, the operator's line part is symmetric positive definite. `element_block`: symmetric with a dominant positive diagonal.
All inputs are finite; a program needn't handle non-finite values.
Results may differ from the reference program's by a relative error of at most 0.018.
Values may be sent and summed in bfloat16 or wider, within the bound.
No kernel may reach another device: no remote copies, remote signals or barrier semaphores. Data moves between devices by JAX's collectives and lax.ppermute only.
A program may use at most 128 MiB of HBM per device.

```python
import jax
import jax.numpy as jnp
from jax import lax

NODES = 64
SX = 4
NGY = 32
ITERS = 2
LINES_DEV = 128
NE = 4
NLINES = 8192


def line_layout(key):
    devices = NLINES // LINES_DEV
    keys = jax.random.split(key, devices)
    placed = jax.vmap(lambda one: jax.random.permutation(one, LINES_DEV))(keys).astype(jnp.int32)
    slot_of = jnp.argsort(placed, axis=1).astype(jnp.int32)
    device = jnp.arange(devices, dtype=jnp.int32)[:, None]
    column = placed // NGY
    rowpos = placed % NGY
    across = device * SX + column
    own_id = device * LINES_DEV + jnp.arange(LINES_DEV, dtype=jnp.int32)[None, :]
    columns_all = devices * SX

    def line_id(xpos, ypos):
        owner = xpos // SX
        return owner * LINES_DEV + slot_of[owner, xpos % SX * NGY + ypos]
    valid0 = across - 1 >= 0
    valid1 = across + 1 < columns_all
    valid2 = rowpos - 1 >= 0
    valid3 = rowpos + 1 < NGY
    near0 = jnp.where(valid0, line_id(jnp.maximum(across - 1, 0), rowpos), own_id)
    near1 = jnp.where(valid1, line_id(jnp.minimum(across + 1, columns_all - 1), rowpos), own_id)
    near2 = jnp.where(valid2, line_id(across, jnp.maximum(rowpos - 1, 0)), own_id)
    near3 = jnp.where(valid3, line_id(across, jnp.minimum(rowpos + 1, NGY - 1)), own_id)
    nears = jnp.stack([near0, near1, near2, near3], axis=-1).reshape(NLINES, 4)
    valids = jnp.stack([valid0, valid1, valid2, valid3], axis=-1).reshape(NLINES, 4)
    return (nears.astype(jnp.int32), valids)


def draw_neighbours(key, part):
    nears, valids = line_layout(key)
    return nears


def draw_face_type(key, part):
    nears, valids = line_layout(key)
    key = jax.random.fold_in(key, 7)
    kinds = jax.random.randint(key, (NLINES, 4), 1, 3).astype(jnp.int32)
    return jnp.where(valids, 0, kinds).astype(jnp.int32)


def symmetric_block(key, diagonal, spread):
    mixed = jax.random.uniform(key, (64, 64, NLINES), jnp.float32, -1.0, 1.0)
    mixed = 0.5 * (mixed + jnp.swapaxes(mixed, 0, 1))
    smaller = jnp.minimum(diagonal[:, None, :], diagonal[None, :, :])
    unit = jnp.eye(64, dtype=jnp.float32)[:, :, None]
    return unit * diagonal[:, None, :] + (1.0 - unit) * mixed * smaller * (spread / 63.0)


def draw_pivot_inverse(key, part):
    key = jax.random.fold_in(key, 11)
    share = 0.5

    def one_element(elem):
        sub = jax.random.split(jax.random.fold_in(key, elem), 4)
        slow = jax.random.uniform(sub[0], (64, NLINES)) < share
        fast_value = jnp.exp(jax.random.uniform(sub[1], (64, NLINES), jnp.float32, jnp.log(0.3), jnp.log(0.86)))
        slow_value = jax.random.uniform(sub[2], (64, NLINES), jnp.float32, 0.86, 0.94)
        diagonal = jnp.where(slow, slow_value, fast_value)
        return symmetric_block(sub[3], diagonal, 0.8).astype(jnp.bfloat16)
    return lax.map(one_element, jnp.arange(NE))


def draw_line_coupling(key, part):
    key = jax.random.fold_in(key, 13)

    def one_element(elem):
        sub = jax.random.split(jax.random.fold_in(key, elem), 2)
        diagonal = -jax.random.uniform(sub[0], (64, NLINES), jnp.float32, 0.9, 1.05)
        spread = jax.random.uniform(sub[1], (64, 64, NLINES), jnp.float32, -0.6 / 63.0, 0.6 / 63.0)
        unit = jnp.eye(64, dtype=jnp.float32)[:, :, None]
        return (unit * diagonal[:, None, :] + (1.0 - unit) * spread).astype(jnp.bfloat16)
    return lax.map(one_element, jnp.arange(NE))


def draw_element_block(key, part):
    key = jax.random.fold_in(key, 17)

    def one_element(elem):
        sub = jax.random.split(jax.random.fold_in(key, elem), 2)
        diagonal = jax.random.uniform(sub[0], (64, NLINES), jnp.float32, 6.0, 12.0)
        return symmetric_block(sub[1], diagonal, 0.4).astype(jnp.bfloat16)
    return lax.map(one_element, jnp.arange(NE))


def block_levels(key, extent, cuts, least, largest):
    def one(axis_at, shards_of):
        heights = jax.random.uniform(jax.random.fold_in(jax.random.fold_in(key, 6), axis_at), (shards_of,), jnp.float32, least / len(cuts), largest / len(cuts))
        return jnp.repeat(jnp.exp(heights), extent[axis_at] // shards_of).reshape((-1,) + (1,) * (len(extent) - axis_at - 1))

    level = one(*cuts[0])
    for cut in cuts[1:]:
        level = level * one(*cut)
    return level


def normal_values(stream_key, dims, width, reach, cuts=(), held_as=jnp.bfloat16):
    entries = width * jax.random.normal(stream_key, dims, jnp.float32)
    if cuts:
        entries = entries * block_levels(stream_key, dims, cuts, -0.22, 0.18)
    return jnp.clip(entries, -reach, reach).astype(held_as)


def setup_inputs(seed: int = 0) -> dict:
    streams_of = jax.random.split(jax.random.key(seed), 7)
    return {
        "rhs": normal_values(streams_of[0], (NE, NODES, NLINES), 2.0, 12.0, ((0, 4), (2, 64)), jnp.float32),
        "pivot_inverse": draw_pivot_inverse(jax.random.fold_in(streams_of[6], 71), 0),
        "line_coupling": draw_line_coupling(jax.random.fold_in(streams_of[6], 71), 0),
        "element_block": draw_element_block(jax.random.fold_in(streams_of[6], 71), 0),
        "neighbours": draw_neighbours(jax.random.fold_in(streams_of[6], 71), 0),
        "face_type": draw_face_type(jax.random.fold_in(streams_of[6], 71), 0),
    }


highest = lax.Precision.HIGHEST
penalty = 2.0


def apply_block(matrix, vector):
    return jnp.einsum('abl,bl->al', matrix.astype(jnp.float32), vector, precision=highest)


def apply_transpose(matrix, vector):
    return jnp.einsum('bal,bl->al', matrix.astype(jnp.float32), vector, precision=highest)


def operate(vector, element_block, line_coupling, neighbours, face_type):
    lifted = [apply_transpose(line_coupling[elem], vector[elem]) for elem in range(NE)]
    rows = []
    for elem in range(NE):
        total = apply_block(element_block[elem], vector[elem])
        if elem > 0:
            total = total + apply_block(line_coupling[elem], vector[elem - 1])
        if elem + 1 < NE:
            total = total + lifted[elem + 1]
        rows.append(total)
    line_part = jnp.stack(rows)
    cube = vector.reshape(NE, 4, 4, 4, NLINES)
    interior = (face_type == 0).astype(jnp.float32) * penalty
    own_weight = interior + (face_type == 1).astype(jnp.float32) * (2.0 * penalty)
    near0 = jnp.take(cube[:, 3], neighbours[:, 0], axis=3)
    near1 = jnp.take(cube[:, 0], neighbours[:, 1], axis=3)
    near2 = jnp.take(cube[:, :, 3], neighbours[:, 2], axis=3)
    near3 = jnp.take(cube[:, :, 0], neighbours[:, 3], axis=3)
    term0 = own_weight[:, 0] * cube[:, 0] - interior[:, 0] * near0
    term1 = own_weight[:, 1] * cube[:, 3] - interior[:, 1] * near1
    term2 = own_weight[:, 2] * cube[:, :, 0] - interior[:, 2] * near2
    term3 = own_weight[:, 3] * cube[:, :, 3] - interior[:, 3] * near3
    faces = jnp.zeros_like(cube)
    faces = faces.at[:, 0].add(term0).at[:, 3].add(term1)
    faces = faces.at[:, :, 0].add(term2).at[:, :, 3].add(term3)
    return line_part + faces.reshape(NE, 64, NLINES)


def precondition(residual, pivot_inverse, line_coupling):
    previous = jnp.zeros((64, NLINES), jnp.float32)
    forward_vals = []
    for elem in range(NE):
        previous = apply_block(pivot_inverse[elem], residual[elem] - apply_block(line_coupling[elem], previous))
        forward_vals.append(previous)
    carried = jnp.zeros((64, NLINES), jnp.float32)
    values = [None] * NE
    for elem in reversed(range(NE)):
        value = forward_vals[elem] - apply_block(pivot_inverse[elem], carried)
        values[elem] = value
        carried = apply_transpose(line_coupling[elem], value)
    return jnp.stack(values)


def reference(rhs, pivot_inverse, line_coupling, element_block, neighbours, face_type):
    solution = jnp.zeros_like(rhs)
    residual = rhs
    precond = precondition(residual, pivot_inverse, line_coupling)
    direction = precond
    rho = jnp.sum(residual * precond)
    for turn in range(ITERS):
        image = operate(direction, element_block, line_coupling, neighbours, face_type)
        alpha = rho / jnp.sum(direction * image)
        solution = solution + alpha * direction
        residual = residual - alpha * image
        precond = precondition(residual, pivot_inverse, line_coupling)
        if turn + 1 < ITERS:
            rho_next = jnp.sum(residual * precond)
            direction = precond + (rho_next / rho) * direction
            rho = rho_next
    return solution, residual, precond
```

```python
import functools

import jax
import jax.numpy as jnp
from jax import lax
from jax.experimental import pallas as pl
from jax.experimental.pallas import tpu as pltpu
from jax.sharding import PartitionSpec as P


SEGMENT = 32
BLOCK_ROWS = 1024
COUPLING, PIVOT, DIAGONAL, RESIDUAL = (0, 1024, 2048, 3072)
CHUNK_ROWS = 3072 + 48
VMEM_LIMIT = 48 * 1024 * 1024

f32 = jnp.float32
bf16 = jnp.bfloat16


def params():
    return pltpu.CompilerParams(vmem_limit_bytes=VMEM_LIMIT)


def segment_of(shape):
    return lax.broadcasted_iota(jnp.int32, shape, 1) >> 5


def row_of(shape):
    return lax.broadcasted_iota(jnp.int32, shape, 0)


def matmul(left, right):
    return jnp.dot(left, right, preferred_element_type=f32)


def three_parts(value):
    high = value.astype(bf16)
    rest = value - high.astype(f32)
    middle = rest.astype(bf16)
    low = (rest - middle.astype(f32)).astype(bf16)
    return high, middle, low


def pack_kernel(place, rhs, pivot, coupling, diagonal, neighbours, face_type, out0, out1, out2, out3, weights, order):
    me, cross = place[0], place[1]
    square = (128, 128)
    lane = lax.broadcasted_iota(jnp.int32, square, 1)
    slot = row_of(square)

    def step_down(face):
        near = neighbours[:, face : face + 1] - cross * 128
        return jnp.where((near == lane) & (lane != slot), 1.0, 0.0).astype(bf16)

    ones = jnp.ones(square, bf16)
    across = step_down(0)
    once = matmul(across, ones)
    twice = matmul(across, once.astype(bf16))
    column = once + twice + matmul(across, twice.astype(bf16))
    jump = step_down(2)
    row = matmul(jump, ones)
    for turn in range(5):
        row = row + matmul(jump, row.astype(bf16))
        if turn < 4:
            jump = matmul(jump, jump).astype(bf16)
    owner = jnp.where(cross % 2 == 0, column, 3.0 - column)
    position = (owner * 32.0 + row).astype(jnp.int32)

    segment = lane >> 5
    hits = [position == (((me + d) & 3) * 32 + (lane & 31)) for d in range(4)]
    for q in range(4):
        for d in range(4):
            order[q * 128 : (q + 1) * 128, d * 128 : (d + 1) * 128] = jnp.where(
                hits[d] & (segment == q), 1.0, 0.0
            ).astype(bf16)

    interior = jnp.where(face_type[...] == 0, 2.0, 0.0)
    own = interior + jnp.where(face_type[...] == 1, 4.0, 0.0)
    table = jnp.concatenate([own, interior, jnp.zeros((8, 128), f32)], axis=0).astype(bf16)
    placed = matmul(table, jnp.where(hits[0], 1.0, 0.0).astype(bf16))
    shape = (16, 128)
    seg, m = segment_of(shape), row_of(shape)
    masks = [seg == 0, seg == 3, m < 4, m >= 12]
    total = jnp.zeros(shape, f32)
    for face in range(4):
        total = total + jnp.where(masks[face], placed[face : face + 1], 0.0)
        weights[1 + face] = jnp.where(masks[face], placed[4 + face : 5 + face], 0.0)
    weights[0] = total

    outs = (out0, out1, out2, out3)
    sorting = order[...]

    def send(left, start, rows):
        result = matmul(left, sorting).astype(bf16)
        for d in range(4):
            outs[d][start : start + rows, :] = result[:, d * 128 : (d + 1) * 128]

    parts = []
    for part in three_parts(rhs[...]):
        parts.append(jnp.concatenate([part[16 * q : 16 * q + 16] for q in range(4)], axis=1))
    send(jnp.concatenate(parts, axis=0), RESIDUAL, 48)
    for block, start in ((coupling, COUPLING), (pivot, PIVOT), (diagonal, DIAGONAL)):
        left = jnp.concatenate(
            [block[:, 16 * q : 16 * q + 16, :].reshape(BLOCK_ROWS, 128) for q in range(4)], axis=1
        )
        send(left, start, BLOCK_ROWS)


def pack(place, rhs, pivot, coupling, diagonal, neighbours, face_type):
    chunk = jax.ShapeDtypeStruct((CHUNK_ROWS, 128), bf16)
    vmem = pl.BlockSpec(memory_space=pltpu.VMEM)
    return pl.pallas_call(
        pack_kernel,
        out_shape=[chunk] * 4 + [jax.ShapeDtypeStruct((5, 16, 128), f32), jax.ShapeDtypeStruct((512, 512), bf16)],
        in_specs=[pl.BlockSpec(memory_space=pltpu.SMEM)] + [vmem] * 6,
        out_specs=[vmem] * 6,
        compiler_params=params(),
        name="pack",
    )(place, rhs, pivot, coupling, diagonal, neighbours, face_type)


def to_packed(spread):
    seg = segment_of((16, 128))
    low = jnp.where(seg == 0, spread[0:16], spread[16:32])
    high = jnp.where(seg == 2, spread[32:48], spread[48:64])
    return jnp.where(seg < 2, low, high)


def to_spread(packed):
    seg = segment_of((16, 128))
    parts = []
    for q in range(4):
        part = jnp.where(seg == q, packed, 0.0)
        part = part + pltpu.roll(part, 32, 1)
        parts.append(part + pltpu.roll(part, 64, 1))
    return jnp.concatenate(parts, axis=0)


def transposed_times(blocks, elem, start, spread, row_ref):
    row_ref[...] = spread
    sums = [None] * 4
    for a in range(64):
        block = blocks[elem, start + 16 * a : start + 16 * a + 16, :].astype(f32)
        term = block * row_ref[a : a + 1, :]
        sums[a % 4] = term if sums[a % 4] is None else sums[a % 4] + term
    return (sums[0] + sums[1]) + (sums[2] + sums[3])


def times(blocks, elem, start, packed):
    block = blocks[elem, start : start + BLOCK_ROWS, :].astype(f32).reshape(64, 16, 128)
    total = jnp.sum(block * packed[None], axis=1)
    total = total + pltpu.roll(total, 32, 1)
    return total + pltpu.roll(total, 64, 1)


def fetch(place, received, blocks, sems):
    copies = [
        pltpu.make_async_copy(received[d], blocks.at[(place[0] - d) & 3], sems.at[d]) for d in range(4)
    ]
    for copy in copies:
        copy.start()
    for copy in copies:
        copy.wait()


def line_solve(residual, blocks, row_ref):
    forward = []
    for elem in range(4):
        right = to_spread(residual[elem])
        if elem > 0:
            right = right - times(blocks, elem, COUPLING, forward[-1])
        forward.append(transposed_times(blocks, elem, PIVOT, right, row_ref))
    values = [None] * 4
    carried = None
    for elem in reversed(range(4)):
        value = to_spread(forward[elem])
        if carried is not None:
            value = value - times(blocks, elem, PIVOT, carried)
        values[elem] = value
        if elem > 0:
            carried = transposed_times(blocks, elem, COUPLING, value, row_ref)
    return values


def send_faces(packed, upper, lower):
    seg = segment_of((16, 128))
    to_next, to_before = jnp.zeros((16, 128), f32), jnp.zeros((16, 128), f32)
    for elem in range(4):
        to_next = jnp.where(seg == elem, pltpu.roll(packed[elem], (32 * (elem + 1)) % 128, 1) if elem < 3 else packed[elem], to_next)
        to_before = jnp.where(seg == elem, pltpu.roll(packed[elem], 32 * elem, 1) if elem > 0 else packed[elem], to_before)
    upper[...] = to_next
    lower[...] = to_before


def line_apply(packed, blocks, weights, row_ref):
    spread = [to_spread(v) for v in packed]
    rows = []
    for elem in range(4):
        v = packed[elem]
        total = transposed_times(blocks, elem, DIAGONAL, spread[elem], row_ref)
        if elem > 0:
            total = total + to_packed(times(blocks, elem, COUPLING, packed[elem - 1]))
        if elem < 3:
            total = total + transposed_times(blocks, elem + 1, COUPLING, spread[elem + 1], row_ref)
        below = pltpu.roll(pltpu.roll(v, 4, 0), 1, 1)
        above = pltpu.roll(pltpu.roll(v, 12, 0), 127, 1)
        rows.append(total + weights[0] * v - weights[3] * below - weights[4] * above)
    return rows


def add_faces(partial, before, after, weights):
    rows = []
    for elem in range(4):
        left = before[...] if elem == 0 else pltpu.roll(before[...], 128 - 32 * elem, 1)
        right = after[...] if elem == 3 else pltpu.roll(after[...], 32 * (3 - elem), 1)
        rows.append(partial[elem] - weights[1] * left - weights[2] * right)
    return rows


def product_sum(first, second):
    total = first[0] * second[0]
    for elem in range(1, 4):
        total = total + first[elem] * second[elem]
    return jnp.sum(total, axis=0, keepdims=True)


def solve_kernel(place, r0, r1, r2, r3, residual, values, upper, lower, blocks, row_ref, sems):
    fetch(place, (r0, r1, r2, r3), blocks, sems)
    parts = []
    for elem in range(4):
        part = blocks[elem, RESIDUAL : RESIDUAL + 48, :].astype(f32)
        parts.append((part[0:16] + part[16:32]) + part[32:48])
        residual[elem] = parts[elem]
    packed = [to_packed(v) for v in line_solve(parts, blocks, row_ref)]
    for elem in range(4):
        values[elem] = packed[elem]
    send_faces(packed, upper, lower)


def apply_kernel(place, r0, r1, r2, r3, vector, weights, partial, blocks, row_ref, sems):
    fetch(place, (r0, r1, r2, r3), blocks, sems)
    rows = line_apply([vector[elem] for elem in range(4)], blocks, weights, row_ref)
    for elem in range(4):
        partial[elem] = rows[elem]


def join_solve_kernel(place, r0, r1, r2, r3, partial, before, after, weights, image, values, upper, lower, blocks, row_ref, sems):
    fetch(place, (r0, r1, r2, r3), blocks, sems)
    rows = add_faces(partial, before, after, weights)
    packed = [to_packed(v) for v in line_solve(rows, blocks, row_ref)]
    for elem in range(4):
        image[elem] = rows[elem]
        values[elem] = packed[elem]
    send_faces(packed, upper, lower)


def join_sums_kernel(partial, before, after, weights, r, z, w, s, image, sums):
    rows = add_faces(partial, before, after, weights)
    for elem in range(4):
        image[elem] = rows[elem]

    def values(ref):
        return [ref[elem] for elem in range(4)]

    z_, w_, s_ = values(z), values(w), values(s)
    products = [product_sum(values(r), z_), product_sum(z_, w_), product_sum(w_, s_), product_sum(s_, rows)]
    sums[...] = jnp.concatenate(products + [jnp.zeros((4, 128), f32)], axis=0)


def last_solve_kernel(place, r0, r1, r2, r3, z, w, s, t, back0, back1, back2, back3, blocks, row_ref, last, sems):
    fetch(place, (r0, r1, r2, r3), blocks, sems)
    packed = [to_packed(v) for v in line_solve([t[elem] for elem in range(4)], blocks, row_ref)]
    for elem in range(4):
        last[elem] = packed[elem]
    backs = (back0, back1, back2, back3)
    for d in range(4):
        elem = (place[0] + d) & 3
        for index, ref in enumerate((z, w, s, t, last)):
            backs[d][index] = ref[elem]


def final_kernel(sums, rhs, b0, b1, b2, b3, order, solution, residual, precond):
    vectors = [jnp.concatenate([b[index] for b in (b0, b3, b2, b1)], axis=1) for index in range(5)]
    z, w, s, t, u = vectors
    totals = jnp.sum(sums[...], axis=1, keepdims=True)
    rho, curve, second, third = (totals[k : k + 1, :] for k in range(4))
    alpha = rho / curve
    rho_next = rho - 2.0 * alpha * curve + alpha * alpha * second
    grown = 1.0 + rho_next / rho
    curve_next = grown * grown * curve - 2.0 * alpha * grown * second + alpha * alpha * third
    alpha_next = rho_next / curve_next
    first = alpha + alpha_next * grown
    other = alpha_next * alpha
    combos = [first * z - other * s, other * t - first * w, z - first * s + other * u]
    parts = [part for combo in combos for part in three_parts(combo)]
    moved = lax.dot_general(
        jnp.concatenate(parts, axis=0), order[...], (((1,), (1,)), ((), ())), preferred_element_type=f32
    )
    for index, ref in enumerate((solution, residual, precond)):
        rows = moved[48 * index : 48 * index + 48]
        value = (rows[0:16] + rows[16:32]) + rows[32:48]
        for q in range(4):
            part = value[:, 128 * q : 128 * q + 128]
            if index == 1:
                part = part + rhs[16 * q : 16 * q + 16, :]
            ref[16 * q : 16 * q + 16, :] = part


VMEM = pl.BlockSpec(memory_space=pltpu.VMEM)
SMEM = pl.BlockSpec(memory_space=pltpu.SMEM)
ANY = pl.BlockSpec(memory_space=pl.ANY)
FACE = jax.ShapeDtypeStruct((16, 128), f32)
VECTOR = jax.ShapeDtypeStruct((4, 16, 128), f32)
BASIS = jax.ShapeDtypeStruct((5, 16, 128), f32)


def with_blocks(kernel, place, received, arrays, outs, name, extra=()):
    return pl.pallas_call(
        kernel,
        out_shape=outs,
        in_specs=[SMEM] + [ANY] * 4 + [VMEM] * len(arrays),
        out_specs=[VMEM] * len(outs),
        scratch_shapes=[pltpu.VMEM((4, CHUNK_ROWS, 128), bf16), pltpu.VMEM((64, 128), f32)]
        + list(extra)
        + [pltpu.SemaphoreType.DMA((4,))],
        compiler_params=params(),
        name=name,
    )(place, *received, *arrays)


def plain(kernel, arrays, outs, name):
    return pl.pallas_call(
        kernel,
        out_shape=outs,
        in_specs=[VMEM] * len(arrays),
        out_specs=[VMEM] * len(outs),
        compiler_params=params(),
        name=name,
    )(*arrays)


def around(value, distance):
    count = lax.axis_size("field")
    return lax.ppermute(value, "field", [(i, (i + distance) % count) for i in range(count)])


def column_pairs(step):
    field, cross = lax.axis_size("field"), lax.axis_size("cross")
    device = {}
    for c in range(cross):
        for f in range(field):
            device[field * c + (f if c % 2 == 0 else field - 1 - f)] = f * cross + c
    count = field * cross
    return [(device[g], device[g + step]) for g in range(count) if 0 <= g + step < count]


def exchange(upper, lower):
    before = lax.ppermute(upper, ("field", "cross"), column_pairs(1))
    after = lax.ppermute(lower, ("field", "cross"), column_pairs(-1))
    return before, after


def total_of(value):
    cross = lax.axis_size("cross")
    for masks in ((1,), (2, 4, 6), (8,), (16, 32, 48)):
        moved = [
            lax.ppermute(value, "cross", [(i, i ^ mask) for i in range(cross)]) for mask in masks if mask < cross
        ]
        value = functools.reduce(jnp.add, moved, value)
    return functools.reduce(jnp.add, [around(value, d) for d in (1, 2, 3)], value)


def local(rhs, pivot_inverse, line_coupling, element_block, neighbours, face_type):
    place = jnp.stack([lax.axis_index("field"), lax.axis_index("cross")]).astype(jnp.int32)
    *chunks, weights, order = pack(
        place, rhs[0], pivot_inverse[0], line_coupling[0], element_block[0], neighbours, face_type.T
    )
    received = [chunks[0]] + [around(chunks[d], d) for d in (1, 2, 3)]
    r, z, upper, lower = with_blocks(solve_kernel, place, received, [], [VECTOR, VECTOR, FACE, FACE], "solve_first")
    before, after = exchange(upper, lower)
    (partial,) = with_blocks(apply_kernel, place, received, [z, weights], [VECTOR], "apply_first")
    w, s, upper, lower = with_blocks(
        join_solve_kernel, place, received, [partial, before, after, weights], [VECTOR, VECTOR, FACE, FACE], "solve_second"
    )
    before, after = exchange(upper, lower)
    (partial,) = with_blocks(apply_kernel, place, received, [s, weights], [VECTOR], "apply_second")
    t, sums = plain(
        join_sums_kernel,
        [partial, before, after, weights, r, z, w, s],
        [VECTOR, jax.ShapeDtypeStruct((8, 128), f32)],
        "sums",
    )
    sums = total_of(sums)
    backs = with_blocks(
        last_solve_kernel, place, received, [z, w, s, t], [BASIS] * 4, "solve_last", [pltpu.VMEM((4, 16, 128), f32)]
    )
    returned = [backs[0]] + [around(backs[d], d) for d in (1, 2, 3)]
    shape = jax.ShapeDtypeStruct((64, 128), f32)
    outs = plain(final_kernel, [sums, rhs[0], *returned, order], [shape] * 3, "final")
    return tuple(out[None] for out in outs)


def solution(mesh):
    placed = (
        P("field", None, "cross"),
        P("field", None, None, "cross"),
        P("field", None, None, "cross"),
        P("field", None, None, "cross"),
        P("cross", None),
        P("cross", None),
    )
    return jax.shard_map(
        local,
        mesh=mesh,
        in_specs=placed,
        out_specs=(P("field", None, "cross"), P("field", None, "cross"), P("field", None, "cross")),
        check_vma=False,
    )
```

```python
import jax
import jax.numpy as jnp
from jax import lax
from jax.experimental import pallas as pl
from jax.experimental.pallas import tpu as pltpu
from jax.sharding import PartitionSpec as P


BLOCK_ROWS = 1024
COUPLING, TRIANGLES, TRAIL = (0, 1024, 2048)
CHUNK_ROWS = 2048 + 64
PIVOT, DIAGONAL = (1024, 2048)
ELEMENT_ROWS = 3072
VMEM_LIMIT = 24 * 1024 * 1024

VMEM = pl.BlockSpec(memory_space=pltpu.VMEM)
HBM = pl.BlockSpec(memory_space=pltpu.HBM)

f32 = jnp.float32
bf16 = jnp.bfloat16


def params():
    return pltpu.CompilerParams(vmem_limit_bytes=VMEM_LIMIT)


def segment_of(shape):
    return lax.broadcasted_iota(jnp.int32, shape, 1) >> 5


def row_of(shape):
    return lax.broadcasted_iota(jnp.int32, shape, 0)


def matmul(left, right):
    return jnp.dot(left, right, preferred_element_type=f32)


def matmul_nt(left, right):
    return lax.dot_general(left, right, (((1,), (1,)), ((), ())), preferred_element_type=f32)


def three_parts(value):
    high = value.astype(bf16)
    rest = value - high.astype(f32)
    middle = rest.astype(bf16)
    low = (rest - middle.astype(f32)).astype(bf16)
    return high, middle, low


def pack_kernel(rhs, pivot, coupling, diagonal, neighbours, face_type, out0, out1, out2, out3, weights, order, *scratch):
    *held, sems = scratch
    copies = [
        pltpu.make_async_copy(source, target, sems.at[index])
        for index, (source, target) in enumerate(
            zip((neighbours, face_type, rhs, coupling, pivot, diagonal), held, strict=True)
        )
    ]
    for copy in copies:
        copy.start()
    neighbours, face_type, rhs, coupling, pivot, diagonal = held
    me, cross = lax.axis_index("field"), lax.axis_index("cross")
    square = (128, 128)
    lane = lax.broadcasted_iota(jnp.int32, square, 1)
    sub = row_of(square)
    copies[0].wait()

    def step_down(face):
        near = neighbours[face : face + 1, :] - cross * 128
        return jnp.where((near == sub) & (lane != sub), 1.0, 0.0).astype(bf16)

    ones = jnp.ones((16, 128), bf16)
    across = step_down(0)
    once = matmul(ones, across)
    twice = matmul(once.astype(bf16), across)
    column = once + twice + matmul(twice.astype(bf16), across)
    jump = step_down(2)
    row = matmul(ones, jump)
    for turn in range(5):
        row = row + matmul(row.astype(bf16), jump)
        if turn < 4:
            jump = matmul(jump, jump).astype(bf16)
    owner = jnp.where(cross % 2 == 0, column, 3.0 - column)
    position = (owner * 32.0 + row).astype(jnp.int32)[0:1]

    segment = sub >> 5
    hits = [position == (((me + d) & 3) * 32 + (sub & 31)) for d in range(4)]
    for q in range(4):
        for d in range(4):
            order[d * 128 : (d + 1) * 128, q * 128 : (q + 1) * 128] = jnp.where(
                hits[d] & (segment == q), 1.0, 0.0
            ).astype(bf16)

    outs = (out0, out1, out2, out3)
    sorting = order[...]

    def send(left, start, rows):
        result = matmul_nt(left, sorting).astype(bf16)
        for d in range(4):
            outs[d][start : start + rows, :] = result[:, d * 128 : (d + 1) * 128]

    copies[3].wait()
    left = [coupling[:, 16 * q : 16 * q + 16, :].reshape(BLOCK_ROWS, 128) for q in range(4)]
    send(jnp.concatenate(left, axis=1), COUPLING, BLOCK_ROWS)

    copies[4].wait()
    copies[5].wait()
    corner = (16, 16, 128)
    major, minor = lax.broadcasted_iota(jnp.int32, corner, 0), lax.broadcasted_iota(jnp.int32, corner, 1)
    left, trail = [], []
    for q in range(4):
        here = slice(16 * q, 16 * q + 16)
        own, other = pivot[here, here, :].astype(f32), diagonal[here, here, :].astype(f32)
        mixed = jnp.where(minor <= major, own, other).astype(bf16)
        parts = [mixed]
        if q > 0:
            parts = [diagonal[0 : 16 * q, here, :]] + parts
        if q < 3:
            parts = parts + [pivot[16 * q + 16 : 64, here, :]]
        left.append(jnp.concatenate(parts, axis=0).reshape(BLOCK_ROWS, 128))
        trail.append(jnp.sum(jnp.where(minor == major, other, 0.0), axis=0).astype(bf16))
    send(jnp.concatenate(left, axis=1), TRIANGLES, BLOCK_ROWS)

    copies[2].wait()
    rows = [jnp.concatenate(trail, axis=1)]
    for part in three_parts(rhs[...]):
        rows.append(jnp.concatenate([part[16 * q : 16 * q + 16] for q in range(4)], axis=1))
    send(jnp.concatenate(rows, axis=0), TRAIL, 64)

    copies[1].wait()
    interior = jnp.where(face_type[...] == 0, 2.0, 0.0)
    own = interior + jnp.where(face_type[...] == 1, 4.0, 0.0)
    table = jnp.concatenate([own, interior, jnp.zeros((8, 128), f32)], axis=0).astype(bf16)
    placed = matmul_nt(table, jnp.where(hits[0], 1.0, 0.0).astype(bf16))
    shape = (16, 128)
    seg, m = segment_of(shape), row_of(shape)
    masks = [seg == 0, seg == 3, m < 4, m >= 12]
    total = jnp.zeros(shape, f32)
    for face in range(4):
        total = total + jnp.where(masks[face], placed[face : face + 1], 0.0)
        weights[1 + face] = jnp.where(masks[face], placed[4 + face : 5 + face], 0.0)
    weights[0] = total


def pack(rhs, pivot, coupling, diagonal, neighbours, face_type):
    chunk = jax.ShapeDtypeStruct((CHUNK_ROWS, 128), bf16)
    held = [pltpu.VMEM((4, 128), jnp.int32)] * 2 + [pltpu.VMEM((64, 128), f32)] + [pltpu.VMEM((64, 64, 128), bf16)] * 3
    return pl.pallas_call(
        pack_kernel,
        out_shape=[chunk] * 4 + [jax.ShapeDtypeStruct((5, 16, 128), f32), jax.ShapeDtypeStruct((512, 512), bf16)],
        in_specs=[HBM] * 6,
        out_specs=[VMEM] * 6,
        scratch_shapes=held + [pltpu.SemaphoreType.DMA((6,))],
        compiler_params=params(),
        name="pack",
    )(*(pltpu.with_memory_space_constraint(x, pltpu.HBM) for x in (rhs, pivot, coupling, diagonal, neighbours, face_type)))


def to_packed(spread):
    seg = segment_of((16, 128))
    low = jnp.where(seg == 0, spread[0:16], spread[16:32])
    high = jnp.where(seg == 2, spread[32:48], spread[48:64])
    return jnp.where(seg < 2, low, high)


def to_spread(packed):
    seg = segment_of((16, 128))
    parts = []
    for q in range(4):
        part = jnp.where(seg == q, packed, 0.0)
        part = part + pltpu.roll(part, 32, 1)
        parts.append(part + pltpu.roll(part, 64, 1))
    return jnp.concatenate(parts, axis=0)


def transposed_times(blocks, elem, start, spread, row_ref):
    row_ref[...] = spread
    sums = [None] * 4
    for a in range(64):
        block = blocks[elem, start + 16 * a : start + 16 * a + 16, :].astype(f32)
        term = block * row_ref[a : a + 1, :]
        sums[a % 4] = term if sums[a % 4] is None else sums[a % 4] + term
    return (sums[0] + sums[1]) + (sums[2] + sums[3])


def times(blocks, elem, start, packed):
    block = blocks[elem, start : start + BLOCK_ROWS, :].astype(f32).reshape(64, 16, 128)
    total = jnp.sum(block * packed[None], axis=1)
    total = total + pltpu.roll(total, 32, 1)
    return total + pltpu.roll(total, 64, 1)


def turn_segments(rows):
    seg = segment_of(rows[0].shape)
    rows = list(rows)
    for width, low in ((2, seg < 2), (1, (seg & 1) == 0)):
        for j in range(4):
            if j & width:
                continue
            x, y = rows[j], rows[j + width]
            rows[j] = jnp.where(low, x, pltpu.roll(y, 32 * width, 1))
            rows[j + width] = jnp.where(low, pltpu.roll(x, 128 - 32 * width, 1), y)
    return rows


def unpack_triangles(triangles, trail, blocks, elem):
    shape = (16, 128)
    seg, m = segment_of(shape), row_of(shape)
    turned = []
    for q in range(4):
        block = triangles[256 * q : 256 * q + 256, :].astype(f32).reshape(16, 16, 128)
        turned.append(jnp.swapaxes(block, 0, 1))
    for k in range(16):
        across = turn_segments([turned[q][k] for q in range(4)])
        for q in range(4):
            a = 16 * q + k
            here = triangles[16 * a : 16 * a + 16, :].astype(f32)
            below = (seg < q) | ((seg == q) & (m <= k))
            diagonal = jnp.where((seg == q) & (m == k), trail, jnp.where(below, across[q], here))
            blocks[elem, PIVOT + 16 * a : PIVOT + 16 * a + 16, :] = jnp.where(below, here, across[q]).astype(bf16)
            blocks[elem, DIAGONAL + 16 * a : DIAGONAL + 16 * a + 16, :] = diagonal.astype(bf16)


def line_solve(residual, blocks, row_ref):
    forward = []
    for elem in range(4):
        right = to_spread(residual[elem])
        if elem > 0:
            right = right - times(blocks, elem, COUPLING, forward[-1])
        forward.append(transposed_times(blocks, elem, PIVOT, right, row_ref))
    values = [None] * 4
    carried = None
    for elem in reversed(range(4)):
        value = to_spread(forward[elem])
        if carried is not None:
            value = value - times(blocks, elem, PIVOT, carried)
        values[elem] = value
        if elem > 0:
            carried = transposed_times(blocks, elem, COUPLING, value, row_ref)
    return values


def send_faces(packed, upper, lower):
    seg = segment_of((16, 128))
    to_next, to_before = jnp.zeros((16, 128), f32), jnp.zeros((16, 128), f32)
    for elem in range(4):
        to_next = jnp.where(seg == elem, pltpu.roll(packed[elem], (32 * (elem + 1)) % 128, 1) if elem < 3 else packed[elem], to_next)
        to_before = jnp.where(seg == elem, pltpu.roll(packed[elem], 32 * elem, 1) if elem > 0 else packed[elem], to_before)
    upper[...] = to_next
    lower[...] = to_before


def line_apply(packed, blocks, weights, row_ref):
    spread = [to_spread(v) for v in packed]
    rows = []
    for elem in range(4):
        v = packed[elem]
        total = transposed_times(blocks, elem, DIAGONAL, spread[elem], row_ref)
        if elem > 0:
            total = total + to_packed(times(blocks, elem, COUPLING, packed[elem - 1]))
        if elem < 3:
            total = total + transposed_times(blocks, elem + 1, COUPLING, spread[elem + 1], row_ref)
        below = pltpu.roll(pltpu.roll(v, 4, 0), 1, 1)
        above = pltpu.roll(pltpu.roll(v, 12, 0), 127, 1)
        rows.append(total + weights[0] * v - weights[3] * below - weights[4] * above)
    return rows


def add_faces(partial, before, after, weights):
    rows = []
    for elem in range(4):
        left = before[...] if elem == 0 else pltpu.roll(before[...], 128 - 32 * elem, 1)
        right = after[...] if elem == 3 else pltpu.roll(after[...], 32 * (3 - elem), 1)
        rows.append(partial[elem] - weights[1] * left - weights[2] * right)
    return rows


def product_sum(first, second):
    total = first[0] * second[0]
    for elem in range(1, 4):
        total = total + first[elem] * second[elem]
    return jnp.sum(total, axis=0, keepdims=True)


def solve_kernel(c0, c1, c2, c3, blocks, residual, values, upper, lower, triangles, row_ref, sems):
    me = lax.axis_index("field")
    copies = []
    for d, source in enumerate((c0, c1, c2, c3)):
        elem = (me - d) & 3
        pairs = (
            (source.at[TRIANGLES:CHUNK_ROWS, :], triangles.at[elem]),
            (source.at[0:BLOCK_ROWS, :], blocks.at[elem, 0:BLOCK_ROWS, :]),
        )
        copies.append([pltpu.make_async_copy(*pair, sems.at[2 * d + k]) for k, pair in enumerate(pairs)])
    for group in copies:
        for copy in group:
            copy.start()
    for group in copies:
        for copy in group:
            copy.wait()
    parts = []
    for elem in range(4):
        trail = triangles[elem, BLOCK_ROWS : BLOCK_ROWS + 64, :].astype(f32)
        parts.append((trail[16:32] + trail[32:48]) + trail[48:64])
        residual[elem] = parts[elem]
        unpack_triangles(triangles.at[elem], trail[0:16], blocks, elem)
    packed = [to_packed(v) for v in line_solve(parts, blocks, row_ref)]
    for elem in range(4):
        values[elem] = packed[elem]
    send_faces(packed, upper, lower)


def apply_kernel(blocks, vector, weights, partial, row_ref):
    rows = line_apply([vector[elem] for elem in range(4)], blocks, weights, row_ref)
    for elem in range(4):
        partial[elem] = rows[elem]


def join_solve_kernel(blocks, partial, before, after, weights, image, values, upper, lower, row_ref):
    rows = add_faces(partial, before, after, weights)
    packed = [to_packed(v) for v in line_solve(rows, blocks, row_ref)]
    for elem in range(4):
        image[elem] = rows[elem]
        values[elem] = packed[elem]
    send_faces(packed, upper, lower)


def last_solve_kernel(blocks, partial, before, after, weights, r, z, w, s, back0, back1, back2, back3, row_ref, t, u):
    rows = add_faces(partial, before, after, weights)
    packed = [to_packed(v) for v in line_solve(rows, blocks, row_ref)]
    for elem in range(4):
        t[elem] = rows[elem]
        u[elem] = packed[elem]

    def values(ref):
        return [ref[elem] for elem in range(4)]

    z_, w_, s_ = values(z), values(w), values(s)
    seg = segment_of((1, 128))
    sums = jnp.zeros((1, 128), f32)
    for index, pair in enumerate(((values(r), z_), (z_, w_), (w_, s_), (s_, rows))):
        total = product_sum(*pair)
        total = total + pltpu.roll(total, 32, 1)
        total = total + pltpu.roll(total, 64, 1)
        sums = jnp.where(seg == index, total, sums)
    me = lax.axis_index("field")
    for d, back in enumerate((back0, back1, back2, back3)):
        elem = (me + d) & 3
        for index, ref in enumerate((z, w, s, t, u)):
            back[16 * index : 16 * index + 16, :] = ref[elem]
        back[80:88, :] = jnp.broadcast_to(sums, (8, 128))


def final_kernel(sums, rhs, b0, b1, b2, b3, order, solution, residual, precond):
    backs = (b0, b3, b2, b1)
    z, w, s, t, u = (
        jnp.concatenate([b[16 * index : 16 * index + 16, :] for b in backs], axis=1) for index in range(5)
    )
    total = jnp.sum(sums[...], axis=0)
    totals = [jnp.sum(total[:, 32 * k : 32 * k + 32], axis=1, keepdims=True) for k in range(4)]
    rho, curve, second, third = totals
    alpha = rho / curve
    rho_next = rho - 2.0 * alpha * curve + alpha * alpha * second
    grown = 1.0 + rho_next / rho
    curve_next = grown * grown * curve - 2.0 * alpha * grown * second + alpha * alpha * third
    alpha_next = rho_next / curve_next
    first = alpha + alpha_next * grown
    other = alpha_next * alpha
    combos = [first * z - other * s, other * t - first * w, z - first * s + other * u]
    parts = [part for combo in combos for part in three_parts(combo)]
    moved = matmul(jnp.concatenate(parts, axis=0), order[...])
    for index, ref in enumerate((solution, residual, precond)):
        rows = moved[48 * index : 48 * index + 48]
        value = (rows[0:16] + rows[16:32]) + rows[32:48]
        for q in range(4):
            part = value[:, 128 * q : 128 * q + 128]
            if index == 1:
                part = part + rhs[16 * q : 16 * q + 16, :]
            ref[16 * q : 16 * q + 16, :] = part


FACE = jax.ShapeDtypeStruct((16, 128), f32)
VECTOR = jax.ShapeDtypeStruct((4, 16, 128), f32)
BACK = jax.ShapeDtypeStruct((88, 128), f32)
BLOCKS = jax.ShapeDtypeStruct((4, ELEMENT_ROWS, 128), bf16)


def kernel(body, arrays, outs, name, spec=VMEM, scratch=()):
    return pl.pallas_call(
        body,
        out_shape=outs,
        in_specs=[spec] * len(arrays),
        out_specs=[VMEM] * len(outs),
        scratch_shapes=list(scratch),
        compiler_params=params(),
        name=name,
    )(*arrays)


def around(value, distance):
    count = lax.axis_size("field")
    return lax.ppermute(value, "field", [(i, (i + distance) % count) for i in range(count)])


def column_pairs(step):
    field, cross = lax.axis_size("field"), lax.axis_size("cross")
    device = {}
    for c in range(cross):
        for f in range(field):
            device[field * c + (f if c % 2 == 0 else field - 1 - f)] = f * cross + c
    count = field * cross
    return [(device[g], device[g + step]) for g in range(count) if 0 <= g + step < count]


def exchange(upper, lower):
    before = lax.ppermute(upper, ("field", "cross"), column_pairs(1))
    after = lax.ppermute(lower, ("field", "cross"), column_pairs(-1))
    return before, after


def local(rhs, pivot_inverse, line_coupling, element_block, neighbours, face_type):
    *chunks, weights, order = pack(
        rhs[0], pivot_inverse[0], line_coupling[0], element_block[0], neighbours.T, face_type.T
    )
    received = [chunks[0]] + [around(chunks[d], d) for d in (1, 2, 3)]
    spread = pltpu.VMEM((64, 128), f32)
    triangles = pltpu.VMEM((4, CHUNK_ROWS - TRIANGLES, 128), bf16)
    blocks, r, z, upper, lower = kernel(
        solve_kernel,
        received,
        [BLOCKS, VECTOR, VECTOR, FACE, FACE],
        "solve_first",
        pl.BlockSpec(memory_space=pl.ANY),
        [triangles, spread, pltpu.SemaphoreType.DMA((8,))],
    )
    before, after = exchange(upper, lower)
    (partial,) = kernel(apply_kernel, [blocks, z, weights], [VECTOR], "apply_first", scratch=[spread])
    w, s, upper, lower = kernel(
        join_solve_kernel,
        [blocks, partial, before, after, weights],
        [VECTOR, VECTOR, FACE, FACE],
        "solve_second",
        scratch=[spread],
    )
    before, after = exchange(upper, lower)
    (partial,) = kernel(apply_kernel, [blocks, s, weights], [VECTOR], "apply_second", scratch=[spread])
    backs = kernel(
        last_solve_kernel,
        [blocks, partial, before, after, weights, r, z, w, s],
        [BACK] * 4,
        "solve_last",
        scratch=[spread, pltpu.VMEM((4, 16, 128), f32), pltpu.VMEM((4, 16, 128), f32)],
    )
    returned = [backs[0]] + [around(backs[d], d) for d in (1, 2, 3)]
    row = (returned[0][80:81] + returned[1][80:81]) + (returned[2][80:81] + returned[3][80:81])
    rows = jnp.broadcast_to(row[None], (lax.axis_size("cross"), 1, 128))
    sums = lax.all_to_all(rows, "cross", 0, 0)
    shape = jax.ShapeDtypeStruct((64, 128), f32)
    outs = kernel(final_kernel, [sums, rhs[0], *returned, order], [shape] * 3, "final")
    return tuple(out[None] for out in outs)


def solution(mesh):
    placed = (
        P("field", None, "cross"),
        P("field", None, None, "cross"),
        P("field", None, None, "cross"),
        P("field", None, None, "cross"),
        P("cross", None),
        P("cross", None),
    )
    return jax.shard_map(
        local,
        mesh=mesh,
        in_specs=placed,
        out_specs=(P("field", None, "cross"), P("field", None, "cross"), P("field", None, "cross")),
        check_vma=False,
    )
```

```python
import functools

import jax
import jax.numpy as jnp
from jax import lax
from jax.experimental import pallas as pl
from jax.experimental.pallas import tpu as pltpu
from jax.sharding import PartitionSpec as P


BLOCK_ROWS = 1024
COUPLING, TRIANGLES, TRAIL = (0, 1024, 2048)
CHUNK_ROWS = 2048 + 64
PIVOT, DIAGONAL = (1024, 2048)
ELEMENT_ROWS = 3072
VMEM_LIMIT = 24 * 1024 * 1024

VMEM = pl.BlockSpec(memory_space=pltpu.VMEM)
HBM = pl.BlockSpec(memory_space=pltpu.HBM)

f32 = jnp.float32
bf16 = jnp.bfloat16


def params():
    return pltpu.CompilerParams(vmem_limit_bytes=VMEM_LIMIT)


def segment_of(shape):
    return lax.broadcasted_iota(jnp.int32, shape, 1) >> 5


def row_of(shape):
    return lax.broadcasted_iota(jnp.int32, shape, 0)


def matmul(left, right):
    return jnp.dot(left, right, preferred_element_type=f32)


def matmul_nt(left, right):
    return lax.dot_general(left, right, (((1,), (1,)), ((), ())), preferred_element_type=f32)


def three_parts(value):
    high = value.astype(bf16)
    rest = value - high.astype(f32)
    middle = rest.astype(bf16)
    low = (rest - middle.astype(f32)).astype(bf16)
    return high, middle, low


def start_fetch(sources, targets, sems):
    copies = [pltpu.make_async_copy(*pair, sems.at[i]) for i, pair in enumerate(zip(sources, targets, strict=True))]
    for copy in copies:
        copy.start()
    return copies


def send(left, sorting, outs, start, rows):
    result = matmul_nt(left, sorting).astype(bf16)
    for d in range(4):
        outs[d][start : start + rows, :] = result[:, d * 128 : (d + 1) * 128]


def pack_kernel(neighbours, face_type, rhs, coupling, pivot, diagonal, out0, out1, out2, out3, weights, order, *scratch):
    *held, sems = scratch
    copies = start_fetch((neighbours, face_type, rhs, coupling, pivot, diagonal), held, sems)
    neighbours, face_type, rhs, coupling, pivot, diagonal = held
    me, cross = lax.axis_index("field"), lax.axis_index("cross")
    square = (128, 128)
    lane = lax.broadcasted_iota(jnp.int32, square, 1)
    sub = row_of(square)
    copies[0].wait()

    def step_down(face):
        near = neighbours[face : face + 1, :] - cross * 128
        return jnp.where((near == sub) & (lane != sub), 1.0, 0.0).astype(bf16)

    ones = jnp.ones((16, 128), bf16)
    across = step_down(0)
    once = matmul(ones, across)
    twice = matmul(once.astype(bf16), across)
    column = once + twice + matmul(twice.astype(bf16), across)
    jump = step_down(2)
    row = matmul(ones, jump)
    for turn in range(5):
        row = row + matmul(row.astype(bf16), jump)
        if turn < 4:
            jump = matmul(jump, jump).astype(bf16)
    owner = jnp.where(cross % 2 == 0, column, 3.0 - column)
    position = (owner * 32.0 + row).astype(jnp.int32)[0:1]

    segment = sub >> 5
    hits = [position == (((me + d) & 3) * 32 + (sub & 31)) for d in range(4)]
    for q in range(4):
        for d in range(4):
            order[d * 128 : (d + 1) * 128, q * 128 : (q + 1) * 128] = jnp.where(
                hits[d] & (segment == q), 1.0, 0.0
            ).astype(bf16)

    outs, sorting = (out0, out1, out2, out3), order[...]
    copies[3].wait()
    left = [coupling[:, 16 * q : 16 * q + 16, :].reshape(BLOCK_ROWS, 128) for q in range(4)]
    send(jnp.concatenate(left, axis=1), sorting, outs, COUPLING, BLOCK_ROWS)

    for copy in (copies[2], copies[4], copies[5]):
        copy.wait()
    corner = (16, 16, 128)
    major, minor = lax.broadcasted_iota(jnp.int32, corner, 0), lax.broadcasted_iota(jnp.int32, corner, 1)
    left, trail = [], []
    for q in range(4):
        here = slice(16 * q, 16 * q + 16)
        own, other = pivot[here, here, :].astype(f32), diagonal[here, here, :].astype(f32)
        parts = [jnp.where(minor <= major, own, other).astype(bf16)]
        if q > 0:
            parts = [diagonal[0 : 16 * q, here, :]] + parts
        if q < 3:
            parts = parts + [pivot[16 * q + 16 : 64, here, :]]
        left.append(jnp.concatenate(parts, axis=0).reshape(BLOCK_ROWS, 128))
        trail.append(jnp.sum(jnp.where(minor == major, other, 0.0), axis=0).astype(bf16))
    send(jnp.concatenate(left, axis=1), sorting, outs, TRIANGLES, BLOCK_ROWS)
    rows = [jnp.concatenate(trail, axis=1)]
    for part in three_parts(rhs[...]):
        rows.append(jnp.concatenate([part[16 * q : 16 * q + 16] for q in range(4)], axis=1))
    send(jnp.concatenate(rows, axis=0), sorting, outs, TRAIL, 64)

    copies[1].wait()
    interior = jnp.where(face_type[...] == 0, 2.0, 0.0)
    own = interior + jnp.where(face_type[...] == 1, 4.0, 0.0)
    table = jnp.concatenate([own, interior, jnp.zeros((8, 128), f32)], axis=0).astype(bf16)
    placed = matmul_nt(table, jnp.where(hits[0], 1.0, 0.0).astype(bf16))
    shape = (16, 128)
    seg, m = segment_of(shape), row_of(shape)
    masks = [seg == 0, seg == 3, m < 4, m >= 12]
    total = jnp.zeros(shape, f32)
    for face in range(4):
        total = total + jnp.where(masks[face], placed[face : face + 1], 0.0)
        weights[1 + face] = jnp.where(masks[face], placed[4 + face : 5 + face], 0.0)
    weights[0] = total


def in_hbm(*arrays):
    return [pltpu.with_memory_space_constraint(array, pltpu.HBM) for array in arrays]


def to_packed(spread):
    seg = segment_of((16, 128))
    low = jnp.where(seg == 0, spread[0:16], spread[16:32])
    high = jnp.where(seg == 2, spread[32:48], spread[48:64])
    return jnp.where(seg < 2, low, high)


def to_spread(packed):
    seg = segment_of((16, 128))
    rolled = [packed] + [pltpu.roll(packed, 32 * k, 1) for k in (1, 2, 3)]
    parts = []
    for q in range(4):
        low = jnp.where(seg == 0, rolled[-q % 4], rolled[(1 - q) % 4])
        high = jnp.where(seg == 2, rolled[(2 - q) % 4], rolled[(3 - q) % 4])
        parts.append(jnp.where(seg < 2, low, high))
    return jnp.concatenate(parts, axis=0)


def over_segments(value):
    return (value + pltpu.roll(value, 32, 1)) + (pltpu.roll(value, 64, 1) + pltpu.roll(value, 96, 1))


def transposed_times(blocks, elem, start, spread, row_ref):
    row_ref[...] = spread
    sums = [None] * 4
    for a in range(64):
        term = blocks[elem, start + 16 * a : start + 16 * a + 16, :].astype(f32) * row_ref[a : a + 1, :]
        sums[a % 4] = term if sums[a % 4] is None else sums[a % 4] + term
    return (sums[0] + sums[1]) + (sums[2] + sums[3])


def times(blocks, elem, start, packed):
    block = blocks[elem, start : start + BLOCK_ROWS, :].astype(f32).reshape(64, 16, 128)
    return over_segments(jnp.sum(block * packed[None], axis=1))


def turn_segments(rows):
    seg = segment_of(rows[0].shape)
    rows = list(rows)
    for width, low in ((2, seg < 2), (1, (seg & 1) == 0)):
        for j in range(4):
            if j & width:
                continue
            x, y = rows[j], rows[j + width]
            rows[j] = jnp.where(low, x, pltpu.roll(y, 32 * width, 1))
            rows[j + width] = jnp.where(low, pltpu.roll(x, 128 - 32 * width, 1), y)
    return rows


def unpack(chunk, blocks, residual, elem, wide):
    shape = (16, 128)
    seg, m = segment_of(shape), row_of(shape)
    blocks[elem, 0:BLOCK_ROWS, :] = chunk[COUPLING : COUPLING + BLOCK_ROWS, :]
    wide[...] = chunk[TRIANGLES : TRIANGLES + BLOCK_ROWS, :].astype(f32)
    trail = chunk[TRAIL : TRAIL + 64, :].astype(f32)
    residual[elem] = (trail[16:32] + trail[32:48]) + trail[48:64]
    for k in range(16):
        across = turn_segments([wide[pl.ds(256 * q + k, 16, stride=16), :] for q in range(4)])
        for q in range(4):
            a = 16 * q + k
            here = wide[16 * a : 16 * a + 16, :]
            below = (seg < q) | ((seg == q) & (m <= k))
            diagonal = jnp.where((seg == q) & (m == k), trail[0:16], jnp.where(below, across[q], here))
            blocks[elem, PIVOT + 16 * a : PIVOT + 16 * a + 16, :] = jnp.where(below, here, across[q]).astype(bf16)
            blocks[elem, DIAGONAL + 16 * a : DIAGONAL + 16 * a + 16, :] = diagonal.astype(bf16)


def line_solve(residual, blocks, row_ref):
    forward = []
    for elem in range(4):
        right = to_spread(residual[elem])
        if elem > 0:
            right = right - times(blocks, elem, COUPLING, forward[-1])
        forward.append(transposed_times(blocks, elem, PIVOT, right, row_ref))
    values = [None] * 4
    carried = None
    for elem in reversed(range(4)):
        value = to_spread(forward[elem])
        if carried is not None:
            value = value - times(blocks, elem, PIVOT, carried)
        values[elem] = value
        if elem > 0:
            carried = transposed_times(blocks, elem, COUPLING, value, row_ref)
    return values


def send_faces(packed, upper, lower):
    seg = segment_of((16, 128))
    to_next, to_before = jnp.zeros((16, 128), f32), jnp.zeros((16, 128), f32)
    for elem in range(4):
        to_next = jnp.where(seg == elem, pltpu.roll(packed[elem], (32 * (elem + 1)) % 128, 1) if elem < 3 else packed[elem], to_next)
        to_before = jnp.where(seg == elem, pltpu.roll(packed[elem], 32 * elem, 1) if elem > 0 else packed[elem], to_before)
    upper[...] = to_next
    lower[...] = to_before


def line_apply(packed, blocks, weights, row_ref):
    spread = [to_spread(v) for v in packed]
    rows = []
    for elem in range(4):
        v = packed[elem]
        total = transposed_times(blocks, elem, DIAGONAL, spread[elem], row_ref)
        if elem > 0:
            total = total + to_packed(times(blocks, elem, COUPLING, packed[elem - 1]))
        if elem < 3:
            total = total + transposed_times(blocks, elem + 1, COUPLING, spread[elem + 1], row_ref)
        below = pltpu.roll(pltpu.roll(v, 4, 0), 1, 1)
        above = pltpu.roll(pltpu.roll(v, 12, 0), 127, 1)
        rows.append(total + weights[0] * v - weights[3] * below - weights[4] * above)
    return rows


def add_faces(partial, before, after, weights):
    rows = []
    for elem in range(4):
        left = before[...] if elem == 0 else pltpu.roll(before[...], 128 - 32 * elem, 1)
        right = after[...] if elem == 3 else pltpu.roll(after[...], 32 * (3 - elem), 1)
        rows.append(partial[elem] - weights[1] * left - weights[2] * right)
    return rows


def product_sum(first, second):
    total = first[0] * second[0]
    for elem in range(1, 4):
        total = total + first[elem] * second[elem]
    return jnp.sum(total, axis=0, keepdims=True)


def unpack_kernel(distance, *refs):
    *_, chunk, blocks, residual, wide = refs
    unpack(chunk, blocks, residual, (lax.axis_index("field") - distance) & 3, wide)


def solve_kernel(blocks_before, residual_before, chunk, blocks, residual, values, upper, lower, row_ref, wide):
    unpack(chunk, blocks, residual, (lax.axis_index("field") - 2) & 3, wide)
    packed = [to_packed(v) for v in line_solve([residual[elem] for elem in range(4)], blocks, row_ref)]
    for elem in range(4):
        values[elem] = packed[elem]
    send_faces(packed, upper, lower)


def apply_kernel(blocks, vector, weights, partial, row_ref):
    rows = line_apply([vector[elem] for elem in range(4)], blocks, weights, row_ref)
    for elem in range(4):
        partial[elem] = rows[elem]


def join_solve_kernel(blocks, partial, before, after, weights, image, values, upper, lower, row_ref):
    rows = add_faces(partial, before, after, weights)
    packed = [to_packed(v) for v in line_solve(rows, blocks, row_ref)]
    for elem in range(4):
        image[elem] = rows[elem]
        values[elem] = packed[elem]
    send_faces(packed, upper, lower)


def last_solve_kernel(blocks, partial, before, after, weights, r, z, w, s, back0, back1, back2, back3, row_ref, t, u):
    rows = add_faces(partial, before, after, weights)
    packed = [to_packed(v) for v in line_solve(rows, blocks, row_ref)]
    for elem in range(4):
        t[elem] = rows[elem]
        u[elem] = packed[elem]

    def values(ref):
        return [ref[elem] for elem in range(4)]

    z_, w_, s_ = values(z), values(w), values(s)
    seg = segment_of((1, 128))
    sums = jnp.zeros((1, 128), f32)
    for index, pair in enumerate(((values(r), z_), (z_, w_), (w_, s_), (s_, rows))):
        total = product_sum(*pair)
        total = total + pltpu.roll(total, 32, 1)
        total = total + pltpu.roll(total, 64, 1)
        sums = jnp.where(seg == index, total, sums)
    me = lax.axis_index("field")
    for d, back in enumerate((back0, back1, back2, back3)):
        elem = (me + d) & 3
        for index, ref in enumerate((z, w, s, t, u)):
            back[16 * index : 16 * index + 16, :] = ref[elem]
        back[80:88, :] = jnp.broadcast_to(sums, (8, 128))


def final_kernel(sums, rhs, b0, b1, b2, b3, order, solution, residual, precond):
    backs = (b0, b3, b2, b1)
    z, w, s, t, u = (
        jnp.concatenate([b[16 * index : 16 * index + 16, :] for b in backs], axis=1) for index in range(5)
    )
    total = jnp.sum(sums[...], axis=0)
    totals = [jnp.sum(total[:, 32 * k : 32 * k + 32], axis=1, keepdims=True) for k in range(4)]
    rho, curve, second, third = totals
    alpha = rho / curve
    rho_next = rho - 2.0 * alpha * curve + alpha * alpha * second
    grown = 1.0 + rho_next / rho
    curve_next = grown * grown * curve - 2.0 * alpha * grown * second + alpha * alpha * third
    alpha_next = rho_next / curve_next
    first = alpha + alpha_next * grown
    other = alpha_next * alpha
    combos = [first * z - other * s, other * t - first * w, z - first * s + other * u]
    parts = [part for combo in combos for part in three_parts(combo)]
    moved = matmul(jnp.concatenate(parts, axis=0), order[...])
    for index, ref in enumerate((solution, residual, precond)):
        rows = moved[48 * index : 48 * index + 48]
        value = (rows[0:16] + rows[16:32]) + rows[32:48]
        for q in range(4):
            part = value[:, 128 * q : 128 * q + 128]
            if index == 1:
                part = part + rhs[16 * q : 16 * q + 16, :]
            ref[16 * q : 16 * q + 16, :] = part


FACE = jax.ShapeDtypeStruct((16, 128), f32)
VECTOR = jax.ShapeDtypeStruct((4, 16, 128), f32)
BACK = jax.ShapeDtypeStruct((88, 128), f32)
BLOCKS = jax.ShapeDtypeStruct((4, ELEMENT_ROWS, 128), bf16)


def kernel(body, arrays, outs, name, spec=VMEM, scratch=(), aliases=None):
    return pl.pallas_call(
        body,
        out_shape=outs,
        in_specs=spec if isinstance(spec, list) else [spec] * len(arrays),
        out_specs=[VMEM] * len(outs),
        scratch_shapes=list(scratch),
        input_output_aliases=aliases or {},
        compiler_params=params(),
        name=name,
    )(*arrays)


def around(value, distance):
    count = lax.axis_size("field")
    return lax.ppermute(value, "field", [(i, (i + distance) % count) for i in range(count)])


def column_pairs(step):
    field, cross = lax.axis_size("field"), lax.axis_size("cross")
    device = {}
    for c in range(cross):
        for f in range(field):
            device[field * c + (f if c % 2 == 0 else field - 1 - f)] = f * cross + c
    count = field * cross
    return [(device[g], device[g + step]) for g in range(count) if 0 <= g + step < count]


def exchange(upper, lower):
    before = lax.ppermute(upper, ("field", "cross"), column_pairs(1))
    after = lax.ppermute(lower, ("field", "cross"), column_pairs(-1))
    return before, after


def local(rhs, pivot_inverse, line_coupling, element_block, neighbours, face_type):
    matrix, small = pltpu.VMEM((64, 64, 128), bf16), pltpu.VMEM((4, 128), jnp.int32)
    spread, wide = pltpu.VMEM((64, 128), f32), pltpu.VMEM((BLOCK_ROWS, 128), f32)
    *chunks, weights, order = kernel(
        pack_kernel,
        in_hbm(neighbours.T, face_type.T, rhs[0], line_coupling[0], pivot_inverse[0], element_block[0]),
        [jax.ShapeDtypeStruct((CHUNK_ROWS, 128), bf16)] * 4
        + [jax.ShapeDtypeStruct((5, 16, 128), f32), jax.ShapeDtypeStruct((512, 512), bf16)],
        "pack",
        HBM,
        [small, small, pltpu.VMEM((64, 128), f32), matrix, matrix, matrix, pltpu.SemaphoreType.DMA((6,))],
    )
    held = []
    arrived = {d: around(chunks[d], d) if d else chunks[0] for d in (0, 1, 3, 2)}
    for d in (0, 1, 3):
        held = kernel(
            functools.partial(unpack_kernel, d),
            [*held, arrived[d]],
            [BLOCKS, VECTOR],
            f"unpack_{d}",
            scratch=[wide],
            aliases={0: 0, 1: 1} if held else None,
        )
    blocks, r, z, upper, lower = kernel(
        solve_kernel,
        [*held, arrived[2]],
        [BLOCKS, VECTOR, VECTOR, FACE, FACE],
        "solve_first",
        scratch=[spread, wide],
        aliases={0: 0, 1: 1},
    )
    before, after = exchange(upper, lower)
    (partial,) = kernel(apply_kernel, [blocks, z, weights], [VECTOR], "apply_first", scratch=[spread])
    w, s, upper, lower = kernel(
        join_solve_kernel,
        [blocks, partial, before, after, weights],
        [VECTOR, VECTOR, FACE, FACE],
        "solve_second",
        scratch=[spread],
    )
    before, after = exchange(upper, lower)
    (partial,) = kernel(apply_kernel, [blocks, s, weights], [VECTOR], "apply_second", scratch=[spread])
    backs = kernel(
        last_solve_kernel,
        [blocks, partial, before, after, weights, r, z, w, s],
        [BACK] * 4,
        "solve_last",
        scratch=[spread, pltpu.VMEM((4, 16, 128), f32), pltpu.VMEM((4, 16, 128), f32)],
    )
    returned = [backs[0]] + [around(backs[d], d) for d in (1, 2, 3)]
    row = (returned[0][80:81] + returned[1][80:81]) + (returned[2][80:81] + returned[3][80:81])
    rows = jnp.broadcast_to(row[None], (lax.axis_size("cross"), 1, 128))
    sums = lax.all_to_all(rows, "cross", 0, 0)
    shape = jax.ShapeDtypeStruct((64, 128), f32)
    outs = kernel(final_kernel, [sums, rhs[0], *returned, order], [shape] * 3, "final")
    return tuple(out[None] for out in outs)


def solution(mesh):
    placed = (
        P("field", None, "cross"),
        P("field", None, None, "cross"),
        P("field", None, None, "cross"),
        P("field", None, None, "cross"),
        P("cross", None),
        P("cross", None),
    )
    return jax.shard_map(
        local,
        mesh=mesh,
        in_specs=placed,
        out_specs=(P("field", None, "cross"), P("field", None, "cross"), P("field", None, "cross")),
        check_vma=False,
    )
```

```python
import functools

import jax
import jax.numpy as jnp
from jax import lax
from jax.experimental import pallas as pl
from jax.experimental.pallas import tpu as pltpu
from jax.sharding import PartitionSpec as P


BLOCK_ROWS = 1024
COUPLING, WIDE, SHORT, CORNER, RESIDUAL = (0, 1024, 1280, 1408, 1664)
FIRST_ROWS = 1664 + 48
SECOND_WIDE, SECOND_SHORT, SECOND_DIAGONAL = (0, 256, 384)
SECOND_ROWS = 384 + 16
PIVOT = 1024
ELEMENT_ROWS = 2048
VMEM_LIMIT = 24 * 1024 * 1024

VMEM = pl.BlockSpec(memory_space=pltpu.VMEM)
HBM = pl.BlockSpec(memory_space=pltpu.HBM)

f32 = jnp.float32
bf16 = jnp.bfloat16


def params():
    return pltpu.CompilerParams(vmem_limit_bytes=VMEM_LIMIT)


def segment_of(shape):
    return lax.broadcasted_iota(jnp.int32, shape, 1) >> 5


def row_of(shape):
    return lax.broadcasted_iota(jnp.int32, shape, 0)


def matmul(left, right):
    return jnp.dot(left, right, preferred_element_type=f32)


def matmul_nt(left, right):
    return lax.dot_general(left, right, (((1,), (1,)), ((), ())), preferred_element_type=f32)


def three_parts(value):
    high = value.astype(bf16)
    rest = value - high.astype(f32)
    middle = rest.astype(bf16)
    low = (rest - middle.astype(f32)).astype(bf16)
    return high, middle, low


def start_fetch(sources, targets, sems):
    copies = [pltpu.make_async_copy(*pair, sems.at[i]) for i, pair in enumerate(zip(sources, targets, strict=True))]
    for copy in copies:
        copy.start()
    return copies


def send(left, sorting, outs, start, rows):
    result = matmul_nt(left, sorting).astype(bf16)
    for d in range(4):
        outs[d][start : start + rows, :] = result[:, d * 128 : (d + 1) * 128]


def parts_below(block):
    def part(rows, column):
        return block[rows, 16 * column : 16 * column + 16, :].reshape(-1, 128)

    last, upper, lower = slice(48, 64), slice(32, 40), slice(40, 48)
    wide = [part(last, 0), part(last, 1), part(last, 2), part(slice(16, 32), 0)]
    short = [part(upper, 0), part(upper, 1), part(lower, 0), part(lower, 1)]
    return [jnp.concatenate(wide, axis=1), jnp.concatenate(short, axis=1)]


def corner_orders():
    shape = (16, 16, 128)
    return lax.broadcasted_iota(jnp.int32, shape, 0), lax.broadcasted_iota(jnp.int32, shape, 1)


def pack_first_kernel(
    neighbours, face_type, rhs, coupling, pivot, diagonal, out0, out1, out2, out3, weights, order, *scratch
):
    *held, sems = scratch
    sources = [neighbours, face_type, rhs, coupling, pivot]
    targets = list(held[:5])
    for q in range(4):
        here = slice(16 * q, 16 * q + 16)
        sources.append(diagonal.at[here, here, :])
        targets.append(held[5].at[q])
    copies = start_fetch(sources, targets, sems)
    neighbours, face_type, rhs, coupling, pivot, corners = held
    me, cross = lax.axis_index("field"), lax.axis_index("cross")
    square = (128, 128)
    lane = lax.broadcasted_iota(jnp.int32, square, 1)
    sub = row_of(square)
    copies[0].wait()

    def step_down(face):
        near = neighbours[face : face + 1, :] - cross * 128
        return jnp.where((near == sub) & (lane != sub), 1.0, 0.0).astype(bf16)

    ones = jnp.ones((16, 128), bf16)
    across = step_down(0)
    once = matmul(ones, across)
    twice = matmul(once.astype(bf16), across)
    column = once + twice + matmul(twice.astype(bf16), across)
    jump = step_down(2)
    row = matmul(ones, jump)
    for turn in range(5):
        row = row + matmul(row.astype(bf16), jump)
        if turn < 4:
            jump = matmul(jump, jump).astype(bf16)
    owner = jnp.where(cross % 2 == 0, column, 3.0 - column)
    position = (owner * 32.0 + row).astype(jnp.int32)[0:1]

    segment = sub >> 5
    hits = [position == (((me + d) & 3) * 32 + (sub & 31)) for d in range(4)]
    for q in range(4):
        for d in range(4):
            order[d * 128 : (d + 1) * 128, q * 128 : (q + 1) * 128] = jnp.where(
                hits[d] & (segment == q), 1.0, 0.0
            ).astype(bf16)

    outs, sorting = (out0, out1, out2, out3), order[...]
    copies[3].wait()
    left = [coupling[:, 16 * q : 16 * q + 16, :].reshape(BLOCK_ROWS, 128) for q in range(4)]
    send(jnp.concatenate(left, axis=1), sorting, outs, COUPLING, BLOCK_ROWS)

    for copy in (copies[2], *copies[4:]):
        copy.wait()
    major, minor = corner_orders()
    shared = []
    for q in range(4):
        here = slice(16 * q, 16 * q + 16)
        own, other = pivot[here, here, :].astype(f32), corners[q].astype(f32)
        shared.append(jnp.where(minor <= major, own, other).astype(bf16).reshape(256, 128))
    rows = parts_below(pivot) + [jnp.concatenate(shared, axis=1)]
    for part in three_parts(rhs[...]):
        rows.append(jnp.concatenate([part[16 * q : 16 * q + 16] for q in range(4)], axis=1))
    send(jnp.concatenate(rows, axis=0), sorting, outs, WIDE, FIRST_ROWS - WIDE)

    copies[1].wait()
    interior = jnp.where(face_type[...] == 0, 2.0, 0.0)
    own = interior + jnp.where(face_type[...] == 1, 4.0, 0.0)
    table = jnp.concatenate([own, interior, jnp.zeros((8, 128), f32)], axis=0).astype(bf16)
    placed = matmul_nt(table, jnp.where(hits[0], 1.0, 0.0).astype(bf16))
    shape = (16, 128)
    seg, m = segment_of(shape), row_of(shape)
    masks = [seg == 0, seg == 3, m < 4, m >= 12]
    total = jnp.zeros(shape, f32)
    for face in range(4):
        total = total + jnp.where(masks[face], placed[face : face + 1], 0.0)
        weights[1 + face] = jnp.where(masks[face], placed[4 + face : 5 + face], 0.0)
    weights[0] = total


def pack_second_kernel(diagonal, order, after, out0, out1, out2, out3, held, sems):
    (copy,) = start_fetch([diagonal], [held], sems)
    copy.wait()
    major, minor = corner_orders()
    trail = []
    for q in range(4):
        here = slice(16 * q, 16 * q + 16)
        trail.append(jnp.sum(jnp.where(minor == major, held[here, here, :].astype(f32), 0.0), axis=0).astype(bf16))
    rows = parts_below(held) + [jnp.concatenate(trail, axis=1)]
    send(jnp.concatenate(rows, axis=0), order[...], (out0, out1, out2, out3), 0, SECOND_ROWS)


def in_hbm(*arrays):
    return [pltpu.with_memory_space_constraint(array, pltpu.HBM) for array in arrays]


def to_packed(spread):
    seg = segment_of((16, 128))
    low = jnp.where(seg == 0, spread[0:16], spread[16:32])
    high = jnp.where(seg == 2, spread[32:48], spread[48:64])
    return jnp.where(seg < 2, low, high)


def to_spread(packed):
    seg = segment_of((16, 128))
    rolled = [packed] + [pltpu.roll(packed, 32 * k, 1) for k in (1, 2, 3)]
    parts = []
    for q in range(4):
        low = jnp.where(seg == 0, rolled[-q % 4], rolled[(1 - q) % 4])
        high = jnp.where(seg == 2, rolled[(2 - q) % 4], rolled[(3 - q) % 4])
        parts.append(jnp.where(seg < 2, low, high))
    return jnp.concatenate(parts, axis=0)


def over_segments(value):
    return (value + pltpu.roll(value, 32, 1)) + (pltpu.roll(value, 64, 1) + pltpu.roll(value, 96, 1))


def transposed_times(blocks, elem, start, spread, row_ref):
    row_ref[...] = spread
    sums = [None] * 4
    for a in range(64):
        term = blocks[elem, start + 16 * a : start + 16 * a + 16, :].astype(f32) * row_ref[a : a + 1, :]
        sums[a % 4] = term if sums[a % 4] is None else sums[a % 4] + term
    return (sums[0] + sums[1]) + (sums[2] + sums[3])


def times(blocks, elem, start, packed):
    block = blocks[elem, start : start + BLOCK_ROWS, :].astype(f32).reshape(64, 16, 128)
    return over_segments(jnp.sum(block * packed[None], axis=1))


def turn_segments(rows):
    seg = segment_of(rows[0].shape)
    rows = list(rows)
    for width, low in ((2, seg < 2), (1, (seg & 1) == 0)):
        for j in range(4):
            if j & width:
                continue
            x, y = rows[j], rows[j + width]
            rows[j] = jnp.where(low, x, pltpu.roll(y, 32 * width, 1))
            rows[j + width] = jnp.where(low, pltpu.roll(x, 128 - 32 * width, 1), y)
    return rows


def spread_parts(wide, parts, corner):
    seg = segment_of((16, 128))
    for k in range(16):
        diagonal = corner[16 * k : 16 * k + 16, :].astype(f32)
        last = parts[16 * k : 16 * k + 16, :].astype(f32)
        third = parts[256 + 16 * (k % 8) : 272 + 16 * (k % 8), :].astype(f32)
        if k >= 8:
            third = pltpu.roll(third, 64, 1)
        wide[16 * k : 16 * k + 16, :] = diagonal
        wide[256 + 16 * k : 272 + 16 * k, :] = jnp.where(seg == 0, pltpu.roll(last, 32, 1), diagonal)
        wide[512 + 16 * k : 528 + 16 * k, :] = jnp.where(seg == 2, diagonal, third)
        wide[768 + 16 * k : 784 + 16 * k, :] = jnp.where(seg == 3, diagonal, last)


def unpack_pivot(chunk, blocks, residual, elem, wide):
    shape = (16, 128)
    seg, m = segment_of(shape), row_of(shape)
    blocks[elem, 0:BLOCK_ROWS, :] = chunk[COUPLING : COUPLING + BLOCK_ROWS, :]
    part = chunk[RESIDUAL : RESIDUAL + 48, :].astype(f32)
    residual[elem] = (part[0:16] + part[16:32]) + part[32:48]
    spread_parts(wide, chunk.at[WIDE:CORNER, :], chunk.at[CORNER:RESIDUAL, :])
    for k in range(16):
        across = turn_segments([wide[pl.ds(256 * q + k, 16, stride=16), :] for q in range(4)])
        for q in range(4):
            a = 16 * q + k
            below = (seg < q) | ((seg == q) & (m <= k))
            value = jnp.where(below, wide[16 * a : 16 * a + 16, :], across[q])
            blocks[elem, PIVOT + 16 * a : PIVOT + 16 * a + 16, :] = value.astype(bf16)


def unpack_diagonal(first, second, diagonals, elem, wide):
    shape = (16, 128)
    seg, m = segment_of(shape), row_of(shape)
    trail = second[SECOND_DIAGONAL:SECOND_ROWS, :].astype(f32)
    spread_parts(wide, second.at[0:SECOND_DIAGONAL, :], first.at[CORNER:RESIDUAL, :])
    for k in range(16):
        across = turn_segments([wide[pl.ds(256 * q + k, 16, stride=16), :] for q in range(4)])
        for q in range(4):
            a = 16 * q + k
            here = (seg < q) | ((seg == q) & (m > k))
            value = jnp.where(here, wide[16 * a : 16 * a + 16, :], across[q])
            value = jnp.where((seg == q) & (m == k), trail, value)
            diagonals[elem, 16 * a : 16 * a + 16, :] = value.astype(bf16)


def line_solve(residual, blocks, row_ref):
    forward = []
    for elem in range(4):
        right = to_spread(residual[elem])
        if elem > 0:
            right = right - times(blocks, elem, COUPLING, forward[-1])
        forward.append(transposed_times(blocks, elem, PIVOT, right, row_ref))
    values = [None] * 4
    carried = None
    for elem in reversed(range(4)):
        value = to_spread(forward[elem])
        if carried is not None:
            value = value - times(blocks, elem, PIVOT, carried)
        values[elem] = value
        if elem > 0:
            carried = transposed_times(blocks, elem, COUPLING, value, row_ref)
    return values


def is_even_column():
    return (lax.axis_index("field") + lax.axis_index("cross")) % 2 == 0


def send_faces(packed, inner, outer):
    seg = segment_of((16, 128))
    to_next, to_before = packed[3], packed[0]
    for elem in range(3):
        to_next = jnp.where(seg == elem, pltpu.roll(packed[elem], 32 * (elem + 1), 1), to_next)
        to_before = jnp.where(seg == elem + 1, pltpu.roll(packed[elem + 1], 32 * (elem + 1), 1), to_before)
    even = is_even_column()
    inner[...] = jnp.where(even, to_next, to_before)
    outer[...] = jnp.where(even, to_before, to_next)


def line_apply(packed, blocks, diagonals, weights, row_ref):
    spread = [to_spread(v) for v in packed]
    rows = []
    for elem in range(4):
        v = packed[elem]
        total = transposed_times(diagonals, elem, 0, spread[elem], row_ref)
        if elem > 0:
            total = total + to_packed(times(blocks, elem, COUPLING, packed[elem - 1]))
        if elem < 3:
            total = total + transposed_times(blocks, elem + 1, COUPLING, spread[elem + 1], row_ref)
        below = pltpu.roll(pltpu.roll(v, 4, 0), 1, 1)
        above = pltpu.roll(pltpu.roll(v, 12, 0), 127, 1)
        rows.append(total + weights[0] * v - weights[3] * below - weights[4] * above)
    return rows


def add_faces(partial, inner, outer, weights):
    even = is_even_column()
    before = jnp.where(even, outer[...], inner[...])
    after = jnp.where(even, inner[...], outer[...])
    rows = []
    for elem in range(4):
        left = before if elem == 0 else pltpu.roll(before, 128 - 32 * elem, 1)
        right = after if elem == 3 else pltpu.roll(after, 32 * (3 - elem), 1)
        rows.append(partial[elem] - weights[1] * left - weights[2] * right)
    return rows


def product_sum(first, second):
    total = first[0] * second[0]
    for elem in range(1, 4):
        total = total + first[elem] * second[elem]
    return jnp.sum(total, axis=0, keepdims=True)


def unpack_kernel(distance, *refs):
    *_, chunk, blocks, residual, wide = refs
    unpack_pivot(chunk, blocks, residual, (lax.axis_index("field") - distance) & 3, wide)


def solve_kernel(blocks_before, residual_before, chunk, blocks, residual, values, inner_out, outer_out, row_ref, wide):
    unpack_pivot(chunk, blocks, residual, (lax.axis_index("field") - 2) & 3, wide)
    packed = [to_packed(v) for v in line_solve([residual[elem] for elem in range(4)], blocks, row_ref)]
    for elem in range(4):
        values[elem] = packed[elem]
    send_faces(packed, inner_out, outer_out)


def unpack_second_kernel(distance, *refs):
    *_, first, second, diagonals, wide = refs
    unpack_diagonal(first, second, diagonals, (lax.axis_index("field") - distance) & 3, wide)


def apply_kernel(blocks, diagonals, vector, weights, partial, row_ref):
    rows = line_apply([vector[elem] for elem in range(4)], blocks, diagonals, weights, row_ref)
    for elem in range(4):
        partial[elem] = rows[elem]


def join_solve_kernel(blocks, partial, inner, outer, weights, image, values, inner_out, outer_out, row_ref):
    rows = add_faces(partial, inner, outer, weights)
    packed = [to_packed(v) for v in line_solve(rows, blocks, row_ref)]
    for elem in range(4):
        image[elem] = rows[elem]
        values[elem] = packed[elem]
    send_faces(packed, inner_out, outer_out)


def last_solve_kernel(blocks, partial, inner, outer, weights, r, z, w, s, back0, back1, back2, back3, row_ref, t, u):
    rows = add_faces(partial, inner, outer, weights)
    packed = [to_packed(v) for v in line_solve(rows, blocks, row_ref)]
    for elem in range(4):
        t[elem] = rows[elem]
        u[elem] = packed[elem]

    def values(ref):
        return [ref[elem] for elem in range(4)]

    z_, w_, s_ = values(z), values(w), values(s)
    seg = segment_of((1, 128))
    sums = jnp.zeros((1, 128), f32)
    for index, pair in enumerate(((values(r), z_), (z_, w_), (w_, s_), (s_, rows))):
        total = product_sum(*pair)
        total = total + pltpu.roll(total, 32, 1)
        total = total + pltpu.roll(total, 64, 1)
        sums = jnp.where(seg == index, total, sums)
    me = lax.axis_index("field")
    for d, back in enumerate((back0, back1, back2, back3)):
        elem = (me + d) & 3
        for index, ref in enumerate((z, w, s, t, u)):
            back[16 * index : 16 * index + 16, :] = ref[elem]
        back[80:88, :] = jnp.broadcast_to(sums, (8, 128))


def final_kernel(sums, rhs, b0, b1, b2, b3, order, solution, residual, precond):
    backs = (b0, b3, b2, b1)
    z, w, s, t, u = (
        jnp.concatenate([b[16 * index : 16 * index + 16, :] for b in backs], axis=1) for index in range(5)
    )
    total = jnp.sum(sums[...], axis=0)
    totals = [jnp.sum(total[:, 32 * k : 32 * k + 32], axis=1, keepdims=True) for k in range(4)]
    rho, curve, second, third = totals
    alpha = rho / curve
    rho_next = rho - 2.0 * alpha * curve + alpha * alpha * second
    grown = 1.0 + rho_next / rho
    curve_next = grown * grown * curve - 2.0 * alpha * grown * second + alpha * alpha * third
    alpha_next = rho_next / curve_next
    first = alpha + alpha_next * grown
    other = alpha_next * alpha
    combos = [first * z - other * s, other * t - first * w, z - first * s + other * u]
    parts = [part for combo in combos for part in three_parts(combo)]
    moved = matmul(jnp.concatenate(parts, axis=0), order[...])
    for index, ref in enumerate((solution, residual, precond)):
        rows = moved[48 * index : 48 * index + 48]
        value = (rows[0:16] + rows[16:32]) + rows[32:48]
        for q in range(4):
            part = value[:, 128 * q : 128 * q + 128]
            if index == 1:
                part = part + rhs[16 * q : 16 * q + 16, :]
            ref[16 * q : 16 * q + 16, :] = part


FACE = jax.ShapeDtypeStruct((16, 128), f32)
VECTOR = jax.ShapeDtypeStruct((4, 16, 128), f32)
BACK = jax.ShapeDtypeStruct((88, 128), f32)
BLOCKS = jax.ShapeDtypeStruct((4, ELEMENT_ROWS, 128), bf16)
DIAGONALS = jax.ShapeDtypeStruct((4, BLOCK_ROWS, 128), bf16)


def kernel(body, arrays, outs, name, spec=VMEM, scratch=(), aliases=None):
    return pl.pallas_call(
        body,
        out_shape=outs,
        in_specs=spec if isinstance(spec, list) else [spec] * len(arrays),
        out_specs=[VMEM] * len(outs),
        scratch_shapes=list(scratch),
        input_output_aliases=aliases or {},
        compiler_params=params(),
        name=name,
    )(*arrays)


def around(value, distance):
    count = lax.axis_size("field")
    return lax.ppermute(value, "field", [(i, (i + distance) % count) for i in range(count)])


def column_swaps(first):
    field, cross = lax.axis_size("field"), lax.axis_size("cross")
    device = {}
    for c in range(cross):
        for f in range(field):
            device[field * c + (f if c % 2 == 0 else field - 1 - f)] = f * cross + c
    pairs = [(device[g], device[g + 1]) for g in range(first, field * cross - 1, 2)]
    return pairs + [(b, a) for a, b in pairs]


def exchange(inner, outer):
    return [lax.ppermute(faces, ("field", "cross"), column_swaps(first)) for first, faces in enumerate((inner, outer))]


def local(rhs, pivot_inverse, line_coupling, element_block, neighbours, face_type):
    matrix, small = pltpu.VMEM((64, 64, 128), bf16), pltpu.VMEM((4, 128), jnp.int32)
    spread, wide = pltpu.VMEM((64, 128), f32), pltpu.VMEM((BLOCK_ROWS, 128), f32)
    fetches = 9
    *chunks, weights, order = kernel(
        pack_first_kernel,
        in_hbm(neighbours.T, face_type.T, rhs[0], line_coupling[0], pivot_inverse[0], element_block[0]),
        [jax.ShapeDtypeStruct((FIRST_ROWS, 128), bf16)] * 4
        + [jax.ShapeDtypeStruct((5, 16, 128), f32), jax.ShapeDtypeStruct((512, 512), bf16)],
        "pack_first",
        HBM,
        [small, small, pltpu.VMEM((64, 128), f32), matrix, matrix, pltpu.VMEM((4, 16, 16, 128), bf16)]
        + [pltpu.SemaphoreType.DMA((fetches,))],
    )
    held = []
    first = {d: around(chunks[d], d) if d else chunks[0] for d in (0, 1, 3, 2)}
    for d in (0, 1, 3):
        held = kernel(
            functools.partial(unpack_kernel, d),
            [*held, *(diagonals if d == 3 else []), first[d]],
            [BLOCKS, VECTOR],
            f"unpack_{d}",
            scratch=[wide],
            aliases={0: 0, 1: 1} if held else None,
        )
        if d == 1:
            chunks = kernel(
                pack_second_kernel,
                in_hbm(element_block[0]) + [order, held[1]],
                [jax.ShapeDtypeStruct((SECOND_ROWS, 128), bf16)] * 4,
                "pack_second",
                [HBM, VMEM, VMEM],
                [matrix, pltpu.SemaphoreType.DMA((1,))],
            )
            second = {d: around(chunks[d], d) if d else chunks[0] for d in (0, 1, 3, 2)}
            diagonals = kernel(
                functools.partial(unpack_second_kernel, 0), [first[0], second[0]], [DIAGONALS], "unpack_second_0", scratch=[wide]
            )
    blocks, r, z, inner, outer = kernel(
        solve_kernel,
        [*held, first[2]],
        [BLOCKS, VECTOR, VECTOR, FACE, FACE],
        "solve_first",
        scratch=[spread, wide],
        aliases={0: 0, 1: 1},
    )
    inner, outer = exchange(inner, outer)
    for d in (1, 3, 2):
        diagonals = kernel(
            functools.partial(unpack_second_kernel, d),
            [*diagonals, first[d], second[d]],
            [DIAGONALS],
            f"unpack_second_{d}",
            scratch=[wide],
            aliases={0: 0},
        )
    (partial,) = kernel(apply_kernel, [blocks, *diagonals, z, weights], [VECTOR], "apply_first", scratch=[spread])
    w, s, inner, outer = kernel(
        join_solve_kernel,
        [blocks, partial, inner, outer, weights],
        [VECTOR, VECTOR, FACE, FACE],
        "solve_second",
        scratch=[spread],
    )
    inner, outer = exchange(inner, outer)
    (partial,) = kernel(apply_kernel, [blocks, *diagonals, s, weights], [VECTOR], "apply_second", scratch=[spread])
    backs = kernel(
        last_solve_kernel,
        [blocks, partial, inner, outer, weights, r, z, w, s],
        [BACK] * 4,
        "solve_last",
        scratch=[spread, pltpu.VMEM((4, 16, 128), f32), pltpu.VMEM((4, 16, 128), f32)],
    )
    returned = [backs[0]] + [around(backs[d], d) for d in (1, 2, 3)]
    row = (returned[0][80:81] + returned[1][80:81]) + (returned[2][80:81] + returned[3][80:81])
    rows = jnp.broadcast_to(row[None], (lax.axis_size("cross"), 1, 128))
    sums = lax.all_to_all(rows, "cross", 0, 0)
    shape = jax.ShapeDtypeStruct((64, 128), f32)
    outs = kernel(final_kernel, [sums, rhs[0], *returned, order], [shape] * 3, "final")
    return tuple(out[None] for out in outs)


def solution(mesh):
    placed = (
        P("field", None, "cross"),
        P("field", None, None, "cross"),
        P("field", None, None, "cross"),
        P("field", None, None, "cross"),
        P("cross", None),
        P("cross", None),
    )
    return jax.shard_map(
        local,
        mesh=mesh,
        in_specs=placed,
        out_specs=(P("field", None, "cross"), P("field", None, "cross"), P("field", None, "cross")),
        check_vma=False,
    )
```

```python
import functools

import jax
import jax.numpy as jnp
from jax import lax
from jax.experimental import pallas as pl
from jax.experimental.pallas import tpu as pltpu
from jax.sharding import PartitionSpec as P


BLOCK_ROWS = 1024
COUPLING, WIDE, SHORT, CORNER, EDGE, RESIDUAL = (0, 1024, 1280, 1408, 1536, 1552)
FIRST_ROWS = 1552 + 32
SECOND_ROWS = RESIDUAL - WIDE
PIVOT = 1024
ELEMENT_ROWS = 2048
VMEM_LIMIT = 24 * 1024 * 1024

VMEM = pl.BlockSpec(memory_space=pltpu.VMEM)
HBM = pl.BlockSpec(memory_space=pltpu.HBM)

f32 = jnp.float32
bf16 = jnp.bfloat16


def params():
    return pltpu.CompilerParams(vmem_limit_bytes=VMEM_LIMIT)


def segment_of(shape):
    return lax.broadcasted_iota(jnp.int32, shape, 1) >> 5


def row_of(shape):
    return lax.broadcasted_iota(jnp.int32, shape, 0)


def matmul(left, right):
    return jnp.dot(left, right, preferred_element_type=f32)


def matmul_nt(left, right):
    return lax.dot_general(left, right, (((1,), (1,)), ((), ())), preferred_element_type=f32)


def bf16_parts(value, count):
    parts = []
    for _ in range(count):
        parts.append(value.astype(bf16))
        value = value - parts[-1].astype(f32)
    return parts


def start_fetch(sources, targets, sems):
    copies = [pltpu.make_async_copy(*pair, sems.at[i]) for i, pair in enumerate(zip(sources, targets, strict=True))]
    for copy in copies:
        copy.start()
    return copies


def send(left, sorting, outs, start, rows):
    result = matmul_nt(left, sorting).astype(bf16)
    for d in range(4):
        outs[d][start : start + rows, :] = result[:, d * 128 : (d + 1) * 128]


def parts_of(block):
    def part(rows, column):
        return block[rows, 16 * column : 16 * column + 16, :].reshape(-1, 128)

    last, upper, lower = slice(48, 64), slice(32, 40), slice(40, 48)
    wide = [part(last, 0), part(last, 1), part(last, 2), part(slice(16, 32), 0)]
    short = [part(upper, 0), part(upper, 1), part(lower, 0), part(lower, 1)]
    shape = (16, 16, 128)
    major, minor = lax.broadcasted_iota(jnp.int32, shape, 0), lax.broadcasted_iota(jnp.int32, shape, 1)
    corner, edge = [], []
    for q in (0, 2):
        one, other = (
            block[16 * k : 16 * k + 16, 16 * k : 16 * k + 16, :].astype(f32) for k in (q, q + 1)
        )
        pair = jnp.where(minor <= major, one, other).astype(bf16)
        corner += [pair[0:8].reshape(128, 128), pair[8:16].reshape(128, 128)]
        edge += [jnp.zeros((16, 128), bf16), jnp.sum(jnp.where(minor == major, other, 0.0), axis=0).astype(bf16)]
    return [jnp.concatenate(parts, axis=1) for parts in (wide, short, corner, edge)]


def pack_first_kernel(
    neighbours, face_type, rhs, coupling, pivot, out0, out1, out2, out3, weights, order, *scratch
):
    *held, sems = scratch
    copies = start_fetch((neighbours, face_type, rhs, coupling, pivot), held, sems)
    neighbours, face_type, rhs, coupling, pivot = held
    me, cross = lax.axis_index("field"), lax.axis_index("cross")
    square = (128, 128)
    lane = lax.broadcasted_iota(jnp.int32, square, 1)
    sub = row_of(square)
    copies[0].wait()

    def step_down(face):
        near = neighbours[face : face + 1, :] - cross * 128
        return jnp.where((near == sub) & (lane != sub), 1.0, 0.0).astype(bf16)

    ones = jnp.ones((16, 128), bf16)
    across = step_down(0)
    once = matmul(ones, across)
    twice = matmul(once.astype(bf16), across)
    column = once + twice + matmul(twice.astype(bf16), across)
    jump = step_down(2)
    row = matmul(ones, jump)
    for turn in range(5):
        row = row + matmul(row.astype(bf16), jump)
        if turn < 4:
            jump = matmul(jump, jump).astype(bf16)
    owner = jnp.where(cross % 2 == 0, column, 3.0 - column)
    position = (owner * 32.0 + row).astype(jnp.int32)[0:1]

    segment = sub >> 5
    hits = [position == (((me + d) & 3) * 32 + (sub & 31)) for d in range(4)]
    for q in range(4):
        for d in range(4):
            order[d * 128 : (d + 1) * 128, q * 128 : (q + 1) * 128] = jnp.where(
                hits[d] & (segment == q), 1.0, 0.0
            ).astype(bf16)

    outs, sorting = (out0, out1, out2, out3), order[...]
    copies[3].wait()
    left = [coupling[:, 16 * q : 16 * q + 16, :].reshape(BLOCK_ROWS, 128) for q in range(4)]
    send(jnp.concatenate(left, axis=1), sorting, outs, COUPLING, BLOCK_ROWS)

    copies[2].wait()
    copies[4].wait()
    rows = parts_of(pivot)
    for part in bf16_parts(rhs[...], 2):
        rows.append(jnp.concatenate([part[16 * q : 16 * q + 16] for q in range(4)], axis=1))
    send(jnp.concatenate(rows, axis=0), sorting, outs, WIDE, FIRST_ROWS - WIDE)

    copies[1].wait()
    interior = jnp.where(face_type[...] == 0, 2.0, 0.0)
    own = interior + jnp.where(face_type[...] == 1, 4.0, 0.0)
    table = jnp.concatenate([own, interior, jnp.zeros((8, 128), f32)], axis=0).astype(bf16)
    placed = matmul_nt(table, jnp.where(hits[0], 1.0, 0.0).astype(bf16))
    shape = (16, 128)
    seg, m = segment_of(shape), row_of(shape)
    masks = [seg == 0, seg == 3, m < 4, m >= 12]
    total = jnp.zeros(shape, f32)
    for face in range(4):
        total = total + jnp.where(masks[face], placed[face : face + 1], 0.0)
        weights[1 + face] = jnp.where(masks[face], placed[4 + face : 5 + face], 0.0)
    weights[0] = total


def pack_second_kernel(diagonal, order, after, out0, out1, out2, out3, held, sems):
    (copy,) = start_fetch([diagonal], [held], sems)
    copy.wait()
    send(jnp.concatenate(parts_of(held), axis=0), order[...], (out0, out1, out2, out3), 0, SECOND_ROWS)


def in_hbm(*arrays):
    return [pltpu.with_memory_space_constraint(array, pltpu.HBM) for array in arrays]


def to_packed(spread):
    seg = segment_of((16, 128))
    low = jnp.where(seg == 0, spread[0:16], spread[16:32])
    high = jnp.where(seg == 2, spread[32:48], spread[48:64])
    return jnp.where(seg < 2, low, high)


def to_spread(packed):
    seg = segment_of((16, 128))
    rolled = [packed] + [pltpu.roll(packed, 32 * k, 1) for k in (1, 2, 3)]
    parts = []
    for q in range(4):
        low = jnp.where(seg == 0, rolled[-q % 4], rolled[(1 - q) % 4])
        high = jnp.where(seg == 2, rolled[(2 - q) % 4], rolled[(3 - q) % 4])
        parts.append(jnp.where(seg < 2, low, high))
    return jnp.concatenate(parts, axis=0)


def over_segments(value):
    return (value + pltpu.roll(value, 32, 1)) + (pltpu.roll(value, 64, 1) + pltpu.roll(value, 96, 1))


def transposed_times(blocks, elem, start, spread, row_ref):
    row_ref[...] = spread
    sums = [None] * 4
    for a in range(64):
        term = blocks[elem, start + 16 * a : start + 16 * a + 16, :].astype(f32) * row_ref[a : a + 1, :]
        sums[a % 4] = term if sums[a % 4] is None else sums[a % 4] + term
    return (sums[0] + sums[1]) + (sums[2] + sums[3])


def times(blocks, elem, start, packed):
    block = blocks[elem, start : start + BLOCK_ROWS, :].astype(f32).reshape(64, 16, 128)
    return over_segments(jnp.sum(block * packed[None], axis=1))


def turn_segments(rows):
    seg = segment_of(rows[0].shape)
    rows = list(rows)
    for width, low in ((2, seg < 2), (1, (seg & 1) == 0)):
        for j in range(4):
            if j & width:
                continue
            x, y = rows[j], rows[j + width]
            rows[j] = jnp.where(low, x, pltpu.roll(y, 32 * width, 1))
            rows[j + width] = jnp.where(low, pltpu.roll(x, 128 - 32 * width, 1), y)
    return rows


def corner_row(parts, k):
    odd = segment_of((16, 128)) % 2 == 1
    start = CORNER - WIDE + 16 * (k % 8)
    row = parts[start : start + 16, :].astype(f32)
    if k < 8:
        return jnp.where(odd, pltpu.roll(row, 32, 1), row)
    return jnp.where(odd, row, pltpu.roll(row, 96, 1))


def unpack(chunk, blocks, residual, elem, wide):
    shape = (16, 128)
    seg, m = segment_of(shape), row_of(shape)
    blocks[elem, 0:BLOCK_ROWS, :] = chunk[COUPLING : COUPLING + BLOCK_ROWS, :]
    residual[elem] = chunk[RESIDUAL : RESIDUAL + 16, :].astype(f32) + chunk[RESIDUAL + 16 : RESIDUAL + 32, :].astype(f32)
    parts = chunk.at[WIDE:RESIDUAL, :]
    for k in range(16):
        corner = corner_row(parts, k)
        last = parts[16 * k : 16 * k + 16, :].astype(f32)
        third = parts[256 + 16 * (k % 8) : 272 + 16 * (k % 8), :].astype(f32)
        if k >= 8:
            third = pltpu.roll(third, 64, 1)
        wide[16 * k : 16 * k + 16, :] = corner
        wide[256 + 16 * k : 272 + 16 * k, :] = jnp.where(seg == 0, pltpu.roll(last, 32, 1), corner)
        wide[512 + 16 * k : 528 + 16 * k, :] = jnp.where(seg == 2, corner, third)
        wide[768 + 16 * k : 784 + 16 * k, :] = jnp.where(seg == 3, corner, last)
    edge = chunk[EDGE : EDGE + 16, :].astype(f32)
    for k in range(16):
        turned = turn_segments([wide[pl.ds(256 * q + k, 16, stride=16), :] for q in range(4)])
        for q in range(4):
            a = 16 * q + k
            here = (seg < q) | ((seg == q) & ((m <= k) if q % 2 == 0 else (m > k)))
            value = jnp.where(here, wide[16 * a : 16 * a + 16, :], turned[q])
            if q % 2 == 1:
                value = jnp.where((seg == q) & (m == k), edge, value)
            blocks[elem, PIVOT + 16 * a : PIVOT + 16 * a + 16, :] = value.astype(bf16)


def diagonal_times(parts, packed):
    shape = (16, 128)
    seg, m = segment_of(shape), row_of(shape)
    spread = to_spread(packed)
    v0, v1, v2, v3 = (spread[16 * q : 16 * q + 16] for q in range(4))

    def both_ways(block, count, across, along):
        down = [block[k] * across[k : k + 1] for k in range(count)]
        while len(down) > 1:
            down = [x + y for x, y in zip(down[::2], down[1::2], strict=True)]
        return down[0], jnp.sum(block * along[None], axis=1)

    odd = seg % 2 == 1
    diagonal = parts[EDGE - WIDE : EDGE - WIDE + 16, :].astype(f32)
    corner = []
    for k in range(16):
        row = corner_row(parts, k)
        diagonal = jnp.where((m == k) & ~odd, row, diagonal)
        corner.append(jnp.where(jnp.where(odd, m - k, k - m) > 0, row, 0.0))
    down, right = both_ways(jnp.concatenate(corner, axis=0).reshape(16, 16, 128), 16, packed, packed)
    total = down + right + diagonal * packed
    wide = parts[0 : SHORT - WIDE, :].astype(f32).reshape(16, 16, 128)
    down, right = both_ways(wide, 16, jnp.where(seg == 3, v1, v3), jnp.where(seg == 3, v0, packed))
    total = total + jnp.where(seg < 3, down, 0.0) + jnp.where(seg == 0, pltpu.roll(down, 32, 1), 0.0)
    turned = [pltpu.roll(right, 32 * k, 1) for k in (1, 2, 3)]
    total = total + jnp.where(seg == 3, (turned[0] + turned[1]) + turned[2], jnp.where(seg == 1, turned[1], 0.0))
    short = parts[SHORT - WIDE : CORNER - WIDE, :].astype(f32).reshape(8, 16, 128)
    down, right = both_ways(short, 8, jnp.where(seg[0:8] < 2, v2[0:8], v2[8:16]), jnp.where(odd, v1, v0))
    total = total + jnp.where(seg < 2, down + pltpu.roll(down, 64, 1), 0.0)
    upper = pltpu.roll(right, 64, 1) + pltpu.roll(right, 32, 1)
    lower = right + pltpu.roll(right, 96, 1)
    return total + jnp.where(seg == 2, jnp.concatenate([upper, lower], axis=0), 0.0)


def line_solve(residual, blocks, row_ref):
    forward = []
    for elem in range(4):
        right = to_spread(residual[elem])
        if elem > 0:
            right = right - times(blocks, elem, COUPLING, forward[-1])
        forward.append(transposed_times(blocks, elem, PIVOT, right, row_ref))
    values = [None] * 4
    carried = None
    for elem in reversed(range(4)):
        value = to_spread(forward[elem])
        if carried is not None:
            value = value - times(blocks, elem, PIVOT, carried)
        values[elem] = value
        if elem > 0:
            carried = transposed_times(blocks, elem, COUPLING, value, row_ref)
    return values


def is_even_column():
    return (lax.axis_index("field") + lax.axis_index("cross")) % 2 == 0


def send_faces(packed, inner, outer):
    seg = segment_of((16, 128))
    to_next, to_before = packed[3], packed[0]
    for elem in range(3):
        to_next = jnp.where(seg == elem, pltpu.roll(packed[elem], 32 * (elem + 1), 1), to_next)
        to_before = jnp.where(seg == elem + 1, pltpu.roll(packed[elem + 1], 32 * (elem + 1), 1), to_before)
    even = is_even_column()
    inner[...] = jnp.where(even, to_next, to_before)
    outer[...] = jnp.where(even, to_before, to_next)


def line_apply(packed, blocks, products, weights, row_ref):
    spread = [to_spread(v) for v in packed]
    rows = []
    for elem in range(4):
        v = packed[elem]
        total = products[elem]
        if elem > 0:
            total = total + to_packed(times(blocks, elem, COUPLING, packed[elem - 1]))
        if elem < 3:
            total = total + transposed_times(blocks, elem + 1, COUPLING, spread[elem + 1], row_ref)
        below = pltpu.roll(pltpu.roll(v, 4, 0), 1, 1)
        above = pltpu.roll(pltpu.roll(v, 12, 0), 127, 1)
        rows.append(total + weights[0] * v - weights[3] * below - weights[4] * above)
    return rows


def add_faces(partial, inner, outer, weights):
    even = is_even_column()
    before = jnp.where(even, outer[...], inner[...])
    after = jnp.where(even, inner[...], outer[...])
    rows = []
    for elem in range(4):
        left = before if elem == 0 else pltpu.roll(before, 128 - 32 * elem, 1)
        right = after if elem == 3 else pltpu.roll(after, 32 * (3 - elem), 1)
        rows.append(partial[elem] - weights[1] * left - weights[2] * right)
    return rows


def product_sum(first, second):
    total = first[0] * second[0]
    for elem in range(1, 4):
        total = total + first[elem] * second[elem]
    return jnp.sum(total, axis=0, keepdims=True)


def unpack_kernel(distance, *refs):
    *_, chunk, blocks, residual, wide = refs
    unpack(chunk, blocks, residual, (lax.axis_index("field") - distance) & 3, wide)


def solve_kernel(blocks_before, residual_before, chunk, blocks, residual, values, inner_out, outer_out, row_ref, wide):
    unpack(chunk, blocks, residual, (lax.axis_index("field") - 2) & 3, wide)
    packed = [to_packed(v) for v in line_solve([residual[elem] for elem in range(4)], blocks, row_ref)]
    for elem in range(4):
        values[elem] = packed[elem]
    send_faces(packed, inner_out, outer_out)


def apply_kernel(blocks, p0, p1, p2, p3, vector, weights, partial, row_ref, products):
    me = lax.axis_index("field")
    for d, parts in enumerate((p0, p1, p2, p3)):
        elem = (me - d) & 3
        products[elem] = diagonal_times(parts, vector[elem])
    rows = line_apply([vector[elem] for elem in range(4)], blocks, products, weights, row_ref)
    for elem in range(4):
        partial[elem] = rows[elem]


def join_solve_kernel(blocks, partial, inner, outer, weights, image, values, inner_out, outer_out, row_ref):
    rows = add_faces(partial, inner, outer, weights)
    packed = [to_packed(v) for v in line_solve(rows, blocks, row_ref)]
    for elem in range(4):
        image[elem] = rows[elem]
        values[elem] = packed[elem]
    send_faces(packed, inner_out, outer_out)


def last_solve_kernel(blocks, partial, inner, outer, weights, r, z, w, s, back0, back1, back2, back3, row_ref, t, u):
    rows = add_faces(partial, inner, outer, weights)
    packed = [to_packed(v) for v in line_solve(rows, blocks, row_ref)]
    for elem in range(4):
        t[elem] = rows[elem]
        u[elem] = packed[elem]

    def values(ref):
        return [ref[elem] for elem in range(4)]

    z_, w_, s_ = values(z), values(w), values(s)
    seg = segment_of((1, 128))
    sums = jnp.zeros((1, 128), f32)
    for index, pair in enumerate(((values(r), z_), (z_, w_), (w_, s_), (s_, rows))):
        total = product_sum(*pair)
        total = total + pltpu.roll(total, 32, 1)
        total = total + pltpu.roll(total, 64, 1)
        sums = jnp.where(seg == index, total, sums)
    me = lax.axis_index("field")
    for d, back in enumerate((back0, back1, back2, back3)):
        elem = (me + d) & 3
        for index, ref in enumerate((z, w, s, t, u)):
            back[16 * index : 16 * index + 16, :] = ref[elem]
        back[80:88, :] = jnp.broadcast_to(sums, (8, 128))


def final_kernel(sums, rhs, b0, b1, b2, b3, order, solution, residual, precond):
    backs = (b0, b3, b2, b1)
    z, w, s, t, u = (
        jnp.concatenate([b[16 * index : 16 * index + 16, :] for b in backs], axis=1) for index in range(5)
    )
    total = jnp.sum(sums[...], axis=0)
    totals = [jnp.sum(total[:, 32 * k : 32 * k + 32], axis=1, keepdims=True) for k in range(4)]
    rho, curve, second, third = totals
    alpha = rho / curve
    rho_next = rho - 2.0 * alpha * curve + alpha * alpha * second
    grown = 1.0 + rho_next / rho
    curve_next = grown * grown * curve - 2.0 * alpha * grown * second + alpha * alpha * third
    alpha_next = rho_next / curve_next
    first = alpha + alpha_next * grown
    other = alpha_next * alpha
    combos = [first * z - other * s, other * t - first * w, z - first * s + other * u]
    parts = [part for combo in combos for part in bf16_parts(combo, 3)]
    moved = matmul(jnp.concatenate(parts, axis=0), order[...])
    for index, ref in enumerate((solution, residual, precond)):
        rows = moved[48 * index : 48 * index + 48]
        value = (rows[0:16] + rows[16:32]) + rows[32:48]
        for q in range(4):
            part = value[:, 128 * q : 128 * q + 128]
            if index == 1:
                part = part + rhs[16 * q : 16 * q + 16, :]
            ref[16 * q : 16 * q + 16, :] = part


FACE = jax.ShapeDtypeStruct((16, 128), f32)
VECTOR = jax.ShapeDtypeStruct((4, 16, 128), f32)
BACK = jax.ShapeDtypeStruct((88, 128), f32)
BLOCKS = jax.ShapeDtypeStruct((4, ELEMENT_ROWS, 128), bf16)


def kernel(body, arrays, outs, name, spec=VMEM, scratch=(), aliases=None):
    return pl.pallas_call(
        body,
        out_shape=outs,
        in_specs=spec if isinstance(spec, list) else [spec] * len(arrays),
        out_specs=[VMEM] * len(outs),
        scratch_shapes=list(scratch),
        input_output_aliases=aliases or {},
        compiler_params=params(),
        name=name,
    )(*arrays)


def around(value, distance):
    count = lax.axis_size("field")
    return lax.ppermute(value, "field", [(i, (i + distance) % count) for i in range(count)])


def column_swaps(first):
    field, cross = lax.axis_size("field"), lax.axis_size("cross")
    device = {}
    for c in range(cross):
        for f in range(field):
            device[field * c + (f if c % 2 == 0 else field - 1 - f)] = f * cross + c
    pairs = [(device[g], device[g + 1]) for g in range(first, field * cross - 1, 2)]
    return pairs + [(b, a) for a, b in pairs]


def exchange(inner, outer):
    return [lax.ppermute(faces, ("field", "cross"), column_swaps(first)) for first, faces in enumerate((inner, outer))]


def local(rhs, pivot_inverse, line_coupling, element_block, neighbours, face_type):
    matrix, small = pltpu.VMEM((64, 64, 128), bf16), pltpu.VMEM((4, 128), jnp.int32)
    spread, wide = pltpu.VMEM((64, 128), f32), pltpu.VMEM((BLOCK_ROWS, 128), f32)
    *chunks, weights, order = kernel(
        pack_first_kernel,
        in_hbm(neighbours.T, face_type.T, rhs[0], line_coupling[0], pivot_inverse[0]),
        [jax.ShapeDtypeStruct((FIRST_ROWS, 128), bf16)] * 4
        + [jax.ShapeDtypeStruct((5, 16, 128), f32), jax.ShapeDtypeStruct((512, 512), bf16)],
        "pack_first",
        HBM,
        [small, small, pltpu.VMEM((64, 128), f32), matrix, matrix, pltpu.SemaphoreType.DMA((5,))],
    )
    held = []
    first = {d: around(chunks[d], d) if d else chunks[0] for d in (0, 1, 3, 2)}
    for d in (0, 1, 3):
        held = kernel(
            functools.partial(unpack_kernel, d),
            [*held, first[d]],
            [BLOCKS, VECTOR],
            f"unpack_{d}",
            scratch=[wide],
            aliases={0: 0, 1: 1} if held else None,
        )
        if d == 1:
            chunks = kernel(
                pack_second_kernel,
                in_hbm(element_block[0]) + [order, held[1]],
                [jax.ShapeDtypeStruct((SECOND_ROWS, 128), bf16)] * 4,
                "pack_second",
                [HBM, VMEM, VMEM],
                [matrix, pltpu.SemaphoreType.DMA((1,))],
            )
            second = {d: around(chunks[d], d) if d else chunks[0] for d in (0, 1, 3, 2)}
    blocks, r, z, inner, outer = kernel(
        solve_kernel,
        [*held, first[2]],
        [BLOCKS, VECTOR, VECTOR, FACE, FACE],
        "solve_first",
        scratch=[spread, wide],
        aliases={0: 0, 1: 1},
    )
    inner, outer = exchange(inner, outer)
    parts = [second[d] for d in range(4)]
    products = pltpu.VMEM((4, 16, 128), f32)
    (partial,) = kernel(apply_kernel, [blocks, *parts, z, weights], [VECTOR], "apply_first", scratch=[spread, products])
    w, s, inner, outer = kernel(
        join_solve_kernel,
        [blocks, partial, inner, outer, weights],
        [VECTOR, VECTOR, FACE, FACE],
        "solve_second",
        scratch=[spread],
    )
    inner, outer = exchange(inner, outer)
    (partial,) = kernel(apply_kernel, [blocks, *parts, s, weights], [VECTOR], "apply_second", scratch=[spread, products])
    backs = kernel(
        last_solve_kernel,
        [blocks, partial, inner, outer, weights, r, z, w, s],
        [BACK] * 4,
        "solve_last",
        scratch=[spread, pltpu.VMEM((4, 16, 128), f32), pltpu.VMEM((4, 16, 128), f32)],
    )
    returned = [backs[0]] + [around(backs[d], d) for d in (1, 2, 3)]
    row = (returned[0][80:81] + returned[1][80:81]) + (returned[2][80:81] + returned[3][80:81])
    rows = jnp.broadcast_to(row[None], (lax.axis_size("cross"), 1, 128))
    sums = lax.all_to_all(rows, "cross", 0, 0)
    shape = jax.ShapeDtypeStruct((64, 128), f32)
    outs = kernel(final_kernel, [sums, rhs[0], *returned, order], [shape] * 3, "final")
    return tuple(out[None] for out in outs)


def solution(mesh):
    placed = (
        P("field", None, "cross"),
        P("field", None, None, "cross"),
        P("field", None, None, "cross"),
        P("field", None, None, "cross"),
        P("cross", None),
        P("cross", None),
    )
    return jax.shard_map(
        local,
        mesh=mesh,
        in_specs=placed,
        out_specs=(P("field", None, "cross"), P("field", None, "cross"), P("field", None, "cross")),
        check_vma=False,
    )
```

```python
import functools

import jax
import jax.numpy as jnp
from jax import lax
from jax.experimental import pallas as pl
from jax.experimental.pallas import tpu as pltpu
from jax.sharding import PartitionSpec as P


BLOCK_ROWS = 1024
COUPLING, WIDE, SHORT, CORNER, EDGE, RESIDUAL = (0, 1024, 1280, 1408, 1536, 1552)
FIRST_ROWS = 1552 + 32
SECOND_ROWS = RESIDUAL - WIDE
PIVOT = 1024
ELEMENT_ROWS = 2048
VMEM_LIMIT = 24 * 1024 * 1024

VMEM = pl.BlockSpec(memory_space=pltpu.VMEM)
HBM = pl.BlockSpec(memory_space=pltpu.HBM)

f32 = jnp.float32
bf16 = jnp.bfloat16


def params():
    return pltpu.CompilerParams(vmem_limit_bytes=VMEM_LIMIT)


def segment_of(shape):
    return lax.broadcasted_iota(jnp.int32, shape, 1) >> 5


def row_of(shape):
    return lax.broadcasted_iota(jnp.int32, shape, 0)


def matmul(left, right):
    return jnp.dot(left, right, preferred_element_type=f32)


def matmul_nt(left, right):
    return lax.dot_general(left, right, (((1,), (1,)), ((), ())), preferred_element_type=f32)


def bf16_parts(value, count):
    parts = []
    for _ in range(count):
        parts.append(value.astype(bf16))
        value = value - parts[-1].astype(f32)
    return parts


def start_fetch(sources, targets, sems):
    copies = [pltpu.make_async_copy(*pair, sems.at[i]) for i, pair in enumerate(zip(sources, targets, strict=True))]
    for copy in copies:
        copy.start()
    return copies


def send(left, sorting, outs, start, rows):
    result = matmul_nt(left, sorting).astype(bf16)
    for d in range(4):
        outs[d][start : start + rows, :] = result[:, d * 128 : (d + 1) * 128]


def parts_of(block):
    def part(rows, column):
        return block[rows, 16 * column : 16 * column + 16, :].reshape(-1, 128)

    last, upper, lower = slice(48, 64), slice(32, 40), slice(40, 48)
    wide = [part(last, 0), part(last, 1), part(last, 2), part(slice(16, 32), 0)]
    short = [part(upper, 0), part(upper, 1), part(lower, 0), part(lower, 1)]
    shape = (16, 16, 128)
    major, minor = lax.broadcasted_iota(jnp.int32, shape, 0), lax.broadcasted_iota(jnp.int32, shape, 1)
    corner, edge = [], []
    for q in (0, 2):
        one, other = (
            block[16 * k : 16 * k + 16, 16 * k : 16 * k + 16, :].astype(f32) for k in (q, q + 1)
        )
        pair = jnp.where(minor <= major, one, other).astype(bf16)
        corner += [pair[0:8].reshape(128, 128), pair[8:16].reshape(128, 128)]
        edge += [jnp.zeros((16, 128), bf16), jnp.sum(jnp.where(minor == major, other, 0.0), axis=0).astype(bf16)]
    return [jnp.concatenate(parts, axis=1) for parts in (wide, short, corner, edge)]


def pack_first_kernel(
    neighbours, face_type, rhs, coupling, pivot, out0, out1, out2, out3, weights, order, rhs_out, *scratch
):
    *held, sems = scratch
    copies = start_fetch((neighbours, face_type, rhs, coupling, pivot), held, sems)
    neighbours, face_type, rhs, coupling, pivot = held
    me, cross = lax.axis_index("field"), lax.axis_index("cross")
    square = (128, 128)
    lane = lax.broadcasted_iota(jnp.int32, square, 1)
    sub = row_of(square)
    copies[0].wait()

    def step_down(face):
        near = neighbours[face : face + 1, :] - cross * 128
        return jnp.where((near == sub) & (lane != sub), 1.0, 0.0).astype(bf16)

    ones = jnp.ones((16, 128), bf16)
    across = step_down(0)
    once = matmul(ones, across)
    twice = matmul(once.astype(bf16), across)
    column = once + twice + matmul(twice.astype(bf16), across)
    jump = step_down(2)
    row = matmul(ones, jump)
    for turn in range(5):
        row = row + matmul(row.astype(bf16), jump)
        if turn < 4:
            jump = matmul(jump, jump).astype(bf16)
    owner = jnp.where(cross % 2 == 0, column, 3.0 - column)
    position = (owner * 32.0 + row).astype(jnp.int32)[0:1]

    segment = sub >> 5
    hits = [position == (((me + d) & 3) * 32 + (sub & 31)) for d in range(4)]
    for q in range(4):
        for d in range(4):
            order[d * 128 : (d + 1) * 128, q * 128 : (q + 1) * 128] = jnp.where(
                hits[d] & (segment == q), 1.0, 0.0
            ).astype(bf16)

    outs, sorting = (out0, out1, out2, out3), order[...]
    copies[3].wait()
    left = [coupling[:, 16 * q : 16 * q + 16, :].reshape(BLOCK_ROWS, 128) for q in range(4)]
    send(jnp.concatenate(left, axis=1), sorting, outs, COUPLING, BLOCK_ROWS)

    copies[2].wait()
    copies[4].wait()
    rhs_out[...] = rhs[...]
    rows = parts_of(pivot)
    for part in bf16_parts(rhs[...], 2):
        rows.append(jnp.concatenate([part[16 * q : 16 * q + 16] for q in range(4)], axis=1))
    send(jnp.concatenate(rows, axis=0), sorting, outs, WIDE, FIRST_ROWS - WIDE)

    copies[1].wait()
    interior = jnp.where(face_type[...] == 0, 2.0, 0.0)
    own = interior + jnp.where(face_type[...] == 1, 4.0, 0.0)
    table = jnp.concatenate([own, interior, jnp.zeros((8, 128), f32)], axis=0).astype(bf16)
    placed = matmul_nt(table, jnp.where(hits[0], 1.0, 0.0).astype(bf16))
    shape = (16, 128)
    seg, m = segment_of(shape), row_of(shape)
    masks = [seg == 0, seg == 3, m < 4, m >= 12]
    total = jnp.zeros(shape, f32)
    for face in range(4):
        total = total + jnp.where(masks[face], placed[face : face + 1], 0.0)
        weights[1 + face] = jnp.where(masks[face], placed[4 + face : 5 + face], 0.0)
    weights[0] = total


def pack_second_kernel(diagonal, order, after, out0, out1, out2, out3, held, sems):
    (copy,) = start_fetch([diagonal], [held], sems)
    copy.wait()
    send(jnp.concatenate(parts_of(held), axis=0), order[...], (out0, out1, out2, out3), 0, SECOND_ROWS)


def in_hbm(*arrays):
    return [pltpu.with_memory_space_constraint(array, pltpu.HBM) for array in arrays]


def to_packed(spread):
    seg = segment_of((16, 128))
    low = jnp.where(seg == 0, spread[0:16], spread[16:32])
    high = jnp.where(seg == 2, spread[32:48], spread[48:64])
    return jnp.where(seg < 2, low, high)


def to_spread(packed):
    seg = segment_of((16, 128))
    rolled = [packed] + [pltpu.roll(packed, 32 * k, 1) for k in (1, 2, 3)]
    parts = []
    for q in range(4):
        low = jnp.where(seg == 0, rolled[-q % 4], rolled[(1 - q) % 4])
        high = jnp.where(seg == 2, rolled[(2 - q) % 4], rolled[(3 - q) % 4])
        parts.append(jnp.where(seg < 2, low, high))
    return jnp.concatenate(parts, axis=0)


def over_segments(value):
    return (value + pltpu.roll(value, 32, 1)) + (pltpu.roll(value, 64, 1) + pltpu.roll(value, 96, 1))


def transposed_times(blocks, elem, start, spread, row_ref):
    row_ref[...] = spread
    sums = [None] * 4
    for a in range(64):
        term = blocks[elem, start + 16 * a : start + 16 * a + 16, :].astype(f32) * row_ref[a : a + 1, :]
        sums[a % 4] = term if sums[a % 4] is None else sums[a % 4] + term
    return (sums[0] + sums[1]) + (sums[2] + sums[3])


def times(blocks, elem, start, packed):
    block = blocks[elem, start : start + BLOCK_ROWS, :].astype(f32).reshape(64, 16, 128)
    return over_segments(jnp.sum(block * packed[None], axis=1))


def turn_segments(rows):
    seg = segment_of(rows[0].shape)
    rows = list(rows)
    for width, low in ((2, seg < 2), (1, (seg & 1) == 0)):
        for j in range(4):
            if j & width:
                continue
            x, y = rows[j], rows[j + width]
            rows[j] = jnp.where(low, x, pltpu.roll(y, 32 * width, 1))
            rows[j + width] = jnp.where(low, pltpu.roll(x, 128 - 32 * width, 1), y)
    return rows


def corner_row(parts, k):
    odd = segment_of((16, 128)) % 2 == 1
    start = CORNER - WIDE + 16 * (k % 8)
    row = parts[start : start + 16, :].astype(f32)
    if k < 8:
        return jnp.where(odd, pltpu.roll(row, 32, 1), row)
    return jnp.where(odd, row, pltpu.roll(row, 96, 1))


def unpack(chunk, blocks, residual, elem, wide):
    shape = (16, 128)
    seg, m = segment_of(shape), row_of(shape)
    blocks[elem, 0:BLOCK_ROWS, :] = chunk[COUPLING : COUPLING + BLOCK_ROWS, :]
    residual[elem] = chunk[RESIDUAL : RESIDUAL + 16, :].astype(f32) + chunk[RESIDUAL + 16 : RESIDUAL + 32, :].astype(f32)
    parts = chunk.at[WIDE:RESIDUAL, :]
    for k in range(16):
        corner = corner_row(parts, k)
        last = parts[16 * k : 16 * k + 16, :].astype(f32)
        third = parts[256 + 16 * (k % 8) : 272 + 16 * (k % 8), :].astype(f32)
        if k >= 8:
            third = pltpu.roll(third, 64, 1)
        wide[16 * k : 16 * k + 16, :] = corner
        wide[256 + 16 * k : 272 + 16 * k, :] = jnp.where(seg == 0, pltpu.roll(last, 32, 1), corner)
        wide[512 + 16 * k : 528 + 16 * k, :] = jnp.where(seg == 2, corner, third)
        wide[768 + 16 * k : 784 + 16 * k, :] = jnp.where(seg == 3, corner, last)
    edge = chunk[EDGE : EDGE + 16, :].astype(f32)
    for k in range(16):
        turned = turn_segments([wide[pl.ds(256 * q + k, 16, stride=16), :] for q in range(4)])
        for q in range(4):
            a = 16 * q + k
            here = (seg < q) | ((seg == q) & ((m <= k) if q % 2 == 0 else (m > k)))
            value = jnp.where(here, wide[16 * a : 16 * a + 16, :], turned[q])
            if q % 2 == 1:
                value = jnp.where((seg == q) & (m == k), edge, value)
            blocks[elem, PIVOT + 16 * a : PIVOT + 16 * a + 16, :] = value.astype(bf16)


def diagonal_times(parts, packed):
    shape = (16, 128)
    seg, m = segment_of(shape), row_of(shape)
    spread = to_spread(packed)
    v0, v1, v2, v3 = (spread[16 * q : 16 * q + 16] for q in range(4))

    def both_ways(block, count, across, along):
        down = [block[k] * across[k : k + 1] for k in range(count)]
        while len(down) > 1:
            down = [x + y for x, y in zip(down[::2], down[1::2], strict=True)]
        return down[0], jnp.sum(block * along[None], axis=1)

    odd = seg % 2 == 1
    diagonal = parts[EDGE - WIDE : EDGE - WIDE + 16, :].astype(f32)
    corner = []
    for k in range(16):
        row = corner_row(parts, k)
        diagonal = jnp.where((m == k) & ~odd, row, diagonal)
        corner.append(jnp.where(jnp.where(odd, m - k, k - m) > 0, row, 0.0))
    down, right = both_ways(jnp.concatenate(corner, axis=0).reshape(16, 16, 128), 16, packed, packed)
    total = down + right + diagonal * packed
    wide = parts[0 : SHORT - WIDE, :].astype(f32).reshape(16, 16, 128)
    down, right = both_ways(wide, 16, jnp.where(seg == 3, v1, v3), jnp.where(seg == 3, v0, packed))
    total = total + jnp.where(seg < 3, down, 0.0) + jnp.where(seg == 0, pltpu.roll(down, 32, 1), 0.0)
    turned = [pltpu.roll(right, 32 * k, 1) for k in (1, 2, 3)]
    total = total + jnp.where(seg == 3, (turned[0] + turned[1]) + turned[2], jnp.where(seg == 1, turned[1], 0.0))
    short = parts[SHORT - WIDE : CORNER - WIDE, :].astype(f32).reshape(8, 16, 128)
    down, right = both_ways(short, 8, jnp.where(seg[0:8] < 2, v2[0:8], v2[8:16]), jnp.where(odd, v1, v0))
    total = total + jnp.where(seg < 2, down + pltpu.roll(down, 64, 1), 0.0)
    upper = pltpu.roll(right, 64, 1) + pltpu.roll(right, 32, 1)
    lower = right + pltpu.roll(right, 96, 1)
    return total + jnp.where(seg == 2, jnp.concatenate([upper, lower], axis=0), 0.0)


def line_solve(residual, blocks, row_ref):
    forward = []
    for elem in range(4):
        right = to_spread(residual[elem])
        if elem > 0:
            right = right - times(blocks, elem, COUPLING, forward[-1])
        forward.append(transposed_times(blocks, elem, PIVOT, right, row_ref))
    values = [None] * 4
    carried = None
    for elem in reversed(range(4)):
        value = to_spread(forward[elem])
        if carried is not None:
            value = value - times(blocks, elem, PIVOT, carried)
        values[elem] = value
        if elem > 0:
            carried = transposed_times(blocks, elem, COUPLING, value, row_ref)
    return values


def is_even_column():
    return (lax.axis_index("field") + lax.axis_index("cross")) % 2 == 0


def send_faces(packed, inner, outer):
    seg = segment_of((16, 128))
    to_next, to_before = packed[3], packed[0]
    for elem in range(3):
        to_next = jnp.where(seg == elem, pltpu.roll(packed[elem], 32 * (elem + 1), 1), to_next)
        to_before = jnp.where(seg == elem + 1, pltpu.roll(packed[elem + 1], 32 * (elem + 1), 1), to_before)
    even = is_even_column()
    inner[...] = jnp.where(even, to_next, to_before)
    outer[...] = jnp.where(even, to_before, to_next)


def line_apply(packed, blocks, products, weights, row_ref):
    spread = [to_spread(v) for v in packed]
    rows = []
    for elem in range(4):
        v = packed[elem]
        total = products[elem]
        if elem > 0:
            total = total + to_packed(times(blocks, elem, COUPLING, packed[elem - 1]))
        if elem < 3:
            total = total + transposed_times(blocks, elem + 1, COUPLING, spread[elem + 1], row_ref)
        below = pltpu.roll(pltpu.roll(v, 4, 0), 1, 1)
        above = pltpu.roll(pltpu.roll(v, 12, 0), 127, 1)
        rows.append(total + weights[0] * v - weights[3] * below - weights[4] * above)
    return rows


def add_faces(partial, inner, outer, weights):
    even = is_even_column()
    before = jnp.where(even, outer[...], inner[...])
    after = jnp.where(even, inner[...], outer[...])
    rows = []
    for elem in range(4):
        left = before if elem == 0 else pltpu.roll(before, 128 - 32 * elem, 1)
        right = after if elem == 3 else pltpu.roll(after, 32 * (3 - elem), 1)
        rows.append(partial[elem] - weights[1] * left - weights[2] * right)
    return rows


def product_sum(first, second):
    total = first[0] * second[0]
    for elem in range(1, 4):
        total = total + first[elem] * second[elem]
    return jnp.sum(total, axis=0, keepdims=True)


def unpack_kernel(distance, *refs):
    *_, chunk, blocks, residual, wide = refs
    unpack(chunk, blocks, residual, (lax.axis_index("field") - distance) & 3, wide)


def solve_kernel(blocks_before, residual_before, chunk, blocks, residual, values, inner_out, outer_out, row_ref, wide):
    unpack(chunk, blocks, residual, (lax.axis_index("field") - 2) & 3, wide)
    packed = [to_packed(v) for v in line_solve([residual[elem] for elem in range(4)], blocks, row_ref)]
    for elem in range(4):
        values[elem] = packed[elem]
    send_faces(packed, inner_out, outer_out)


def apply_kernel(blocks, p0, p1, p2, p3, vector, weights, partial, row_ref, products):
    me = lax.axis_index("field")
    for d, parts in enumerate((p0, p1, p2, p3)):
        elem = (me - d) & 3
        products[elem] = diagonal_times(parts, vector[elem])
    rows = line_apply([vector[elem] for elem in range(4)], blocks, products, weights, row_ref)
    for elem in range(4):
        partial[elem] = rows[elem]


def join_solve_kernel(blocks, partial, inner, outer, weights, image, values, inner_out, outer_out, row_ref):
    rows = add_faces(partial, inner, outer, weights)
    packed = [to_packed(v) for v in line_solve(rows, blocks, row_ref)]
    for elem in range(4):
        image[elem] = rows[elem]
        values[elem] = packed[elem]
    send_faces(packed, inner_out, outer_out)


def sums_kernel(partial, inner, outer, weights, r, z, w, s, image, sums):
    rows = add_faces(partial, inner, outer, weights)

    def values(ref):
        return [ref[elem] for elem in range(4)]

    z_, w_, s_ = values(z), values(w), values(s)
    seg = segment_of((1, 128))
    total = jnp.zeros((1, 128), f32)
    for index, pair in enumerate(((values(r), z_), (z_, w_), (w_, s_), (s_, rows))):
        total = jnp.where(seg == index, over_segments(product_sum(*pair)), total)
    for elem in range(4):
        image[elem] = rows[elem]
    sums[...] = jnp.broadcast_to(total, sums.shape)


def fold_kernel(rows, total):
    total[...] = jnp.broadcast_to(jnp.sum(rows[...], axis=0), total.shape)


def last_solve_kernel(blocks, z, w, s, t, back0, back1, back2, back3, row_ref, u):
    packed = [to_packed(v) for v in line_solve([t[elem] for elem in range(4)], blocks, row_ref)]
    for elem in range(4):
        u[elem] = packed[elem]
    me = lax.axis_index("field")
    for d, back in enumerate((back0, back1, back2, back3)):
        elem = (me + d) & 3
        for index, ref in enumerate((z, w, s, t, u)):
            back[16 * index : 16 * index + 16, :] = ref[elem]


def final_kernel(s0, s1, s2, s3, rhs, b0, b1, b2, b3, order, solution, residual, precond):
    backs = (b0, b3, b2, b1)
    z, w, s, t, u = (
        jnp.concatenate([b[16 * index : 16 * index + 16, :] for b in backs], axis=1) for index in range(5)
    )
    total = ((s0[...] + s1[...]) + (s2[...] + s3[...]))[0:1]
    totals = [jnp.sum(total[:, 32 * k : 32 * k + 32], axis=1, keepdims=True) for k in range(4)]
    rho, curve, second, third = totals
    alpha = rho / curve
    rho_next = rho - 2.0 * alpha * curve + alpha * alpha * second
    grown = 1.0 + rho_next / rho
    curve_next = grown * grown * curve - 2.0 * alpha * grown * second + alpha * alpha * third
    alpha_next = rho_next / curve_next
    first = alpha + alpha_next * grown
    other = alpha_next * alpha
    combos = [first * z - other * s, other * t - first * w, z - first * s + other * u]
    parts = [part for combo in combos for part in bf16_parts(combo, 3)]
    moved = matmul(jnp.concatenate(parts, axis=0), order[...])
    for index, ref in enumerate((solution, residual, precond)):
        rows = moved[48 * index : 48 * index + 48]
        value = (rows[0:16] + rows[16:32]) + rows[32:48]
        for q in range(4):
            part = value[:, 128 * q : 128 * q + 128]
            if index == 1:
                part = part + rhs[16 * q : 16 * q + 16, :]
            ref[16 * q : 16 * q + 16, :] = part


FACE = jax.ShapeDtypeStruct((16, 128), f32)
VECTOR = jax.ShapeDtypeStruct((4, 16, 128), f32)
BACK = jax.ShapeDtypeStruct((80, 128), f32)
BLOCKS = jax.ShapeDtypeStruct((4, ELEMENT_ROWS, 128), bf16)


def kernel(body, arrays, outs, name, spec=VMEM, scratch=(), aliases=None):
    return pl.pallas_call(
        body,
        out_shape=outs,
        in_specs=spec if isinstance(spec, list) else [spec] * len(arrays),
        out_specs=[VMEM] * len(outs),
        scratch_shapes=list(scratch),
        input_output_aliases=aliases or {},
        compiler_params=params(),
        name=name,
    )(*arrays)


def around(value, distance):
    count = lax.axis_size("field")
    return lax.ppermute(value, "field", [(i, (i + distance) % count) for i in range(count)])


def column_swaps(first):
    field, cross = lax.axis_size("field"), lax.axis_size("cross")
    device = {}
    for c in range(cross):
        for f in range(field):
            device[field * c + (f if c % 2 == 0 else field - 1 - f)] = f * cross + c
    pairs = [(device[g], device[g + 1]) for g in range(first, field * cross - 1, 2)]
    return pairs + [(b, a) for a, b in pairs]


def exchange(inner, outer):
    return [lax.ppermute(faces, ("field", "cross"), column_swaps(first)) for first, faces in enumerate((inner, outer))]


def local(rhs, pivot_inverse, line_coupling, element_block, neighbours, face_type):
    matrix, small = pltpu.VMEM((64, 64, 128), bf16), pltpu.VMEM((4, 128), jnp.int32)
    spread, wide = pltpu.VMEM((64, 128), f32), pltpu.VMEM((BLOCK_ROWS, 128), f32)
    shape = jax.ShapeDtypeStruct((64, 128), f32)
    *chunks, weights, order, rhs_here = kernel(
        pack_first_kernel,
        in_hbm(neighbours.T, face_type.T, rhs[0], line_coupling[0], pivot_inverse[0]),
        [jax.ShapeDtypeStruct((FIRST_ROWS, 128), bf16)] * 4
        + [jax.ShapeDtypeStruct((5, 16, 128), f32), jax.ShapeDtypeStruct((512, 512), bf16), shape],
        "pack_first",
        HBM,
        [small, small, pltpu.VMEM((64, 128), f32), matrix, matrix, pltpu.SemaphoreType.DMA((5,))],
    )
    held = []
    first = {d: around(chunks[d], d) if d else chunks[0] for d in (0, 1, 3, 2)}
    for d in (0, 1, 3):
        held = kernel(
            functools.partial(unpack_kernel, d),
            [*held, first[d]],
            [BLOCKS, VECTOR],
            f"unpack_{d}",
            scratch=[wide],
            aliases={0: 0, 1: 1} if held else None,
        )
        if d == 1:
            chunks = kernel(
                pack_second_kernel,
                in_hbm(element_block[0]) + [order, held[1]],
                [jax.ShapeDtypeStruct((SECOND_ROWS, 128), bf16)] * 4,
                "pack_second",
                [HBM, VMEM, VMEM],
                [matrix, pltpu.SemaphoreType.DMA((1,))],
            )
            second = {d: around(chunks[d], d) if d else chunks[0] for d in (0, 1, 3, 2)}
    blocks, r, z, inner, outer = kernel(
        solve_kernel,
        [*held, first[2]],
        [BLOCKS, VECTOR, VECTOR, FACE, FACE],
        "solve_first",
        scratch=[spread, wide],
        aliases={0: 0, 1: 1},
    )
    inner, outer = exchange(inner, outer)
    parts = [second[d] for d in range(4)]
    products = pltpu.VMEM((4, 16, 128), f32)
    (partial,) = kernel(apply_kernel, [blocks, *parts, z, weights], [VECTOR], "apply_first", scratch=[spread, products])
    w, s, inner, outer = kernel(
        join_solve_kernel,
        [blocks, partial, inner, outer, weights],
        [VECTOR, VECTOR, FACE, FACE],
        "solve_second",
        scratch=[spread],
    )
    inner, outer = exchange(inner, outer)
    (partial,) = kernel(apply_kernel, [blocks, *parts, s, weights], [VECTOR], "apply_second", scratch=[spread, products])
    count = lax.axis_size("cross")
    t, rows = kernel(
        sums_kernel,
        [partial, inner, outer, weights, r, z, w, s],
        [VECTOR, jax.ShapeDtypeStruct((count, 128), f32)],
        "sums",
    )
    rows = lax.all_to_all(rows.reshape(count, 1, 128), "cross", 0, 0)
    backs = kernel(
        last_solve_kernel, [blocks, z, w, s, t], [BACK] * 4, "solve_last", scratch=[spread, pltpu.VMEM((4, 16, 128), f32)]
    )
    returned = [backs[0]] + [around(backs[d], d) for d in (1, 2, 3)]
    (total,) = kernel(fold_kernel, [rows], [jax.ShapeDtypeStruct((8, 128), f32)], "fold")
    totals = [total] + [around(total, d) for d in (1, 2, 3)]
    outs = kernel(final_kernel, [*totals, rhs_here, *returned, order], [shape] * 3, "final")
    return tuple(out[None] for out in outs)


def solution(mesh):
    placed = (
        P("field", None, "cross"),
        P("field", None, None, "cross"),
        P("field", None, None, "cross"),
        P("field", None, None, "cross"),
        P("cross", None),
        P("cross", None),
    )
    return jax.shard_map(
        local,
        mesh=mesh,
        in_specs=placed,
        out_specs=(P("field", None, "cross"), P("field", None, "cross"), P("field", None, "cross")),
        check_vma=False,
    )
```

```python
import jax
import jax.numpy as jnp
from jax import lax
from jax.experimental import pallas as pl
from jax.experimental.pallas import tpu as pltpu
from jax.sharding import PartitionSpec as P


BLOCK_ROWS = 1024
COUPLING, WIDE, SHORT, CORNER, EDGE, RESIDUAL = (0, 1024, 1280, 1408, 1536, 1552)
FIRST_ROWS = 1552 + 32
SECOND_ROWS = RESIDUAL - WIDE
PIVOT = 1024
ELEMENT_ROWS = 2048
VMEM_LIMIT = 24 * 1024 * 1024

VMEM = pl.BlockSpec(memory_space=pltpu.VMEM)
HBM = pl.BlockSpec(memory_space=pltpu.HBM)

f32 = jnp.float32
bf16 = jnp.bfloat16


def params():
    return pltpu.CompilerParams(vmem_limit_bytes=VMEM_LIMIT)


def segment_of(shape):
    return lax.broadcasted_iota(jnp.int32, shape, 1) >> 5


def row_of(shape):
    return lax.broadcasted_iota(jnp.int32, shape, 0)


def matmul(left, right):
    return jnp.dot(left, right, preferred_element_type=f32)


def matmul_nt(left, right):
    return lax.dot_general(left, right, (((1,), (1,)), ((), ())), preferred_element_type=f32)


def bf16_parts(value, count):
    parts = []
    for _ in range(count):
        parts.append(value.astype(bf16))
        value = value - parts[-1].astype(f32)
    return parts


def start_fetch(sources, targets, sems):
    copies = [pltpu.make_async_copy(*pair, sems.at[i]) for i, pair in enumerate(zip(sources, targets, strict=True))]
    for copy in copies:
        copy.start()
    return copies


def send(left, sorting, outs, start, rows):
    result = matmul_nt(left, sorting).astype(bf16)
    for d in range(4):
        outs[d][start : start + rows, :] = result[:, d * 128 : (d + 1) * 128]


def hits_of(position, distance, line):
    return position == ((lax.axis_index("field") + distance) & 3) * 32 + line


def sorting_matrix(position):
    sub = row_of((128, 128))
    rows = []
    for d in range(4):
        hit = hits_of(position, d, sub & 31)
        rows.append(jnp.concatenate([jnp.where(hit & ((sub >> 5) == q), 1.0, 0.0) for q in range(4)], axis=1))
    return jnp.concatenate(rows, axis=0).astype(bf16)


def parts_of(block):
    def part(rows, column):
        return block[rows, 16 * column : 16 * column + 16, :].reshape(-1, 128)

    last, upper, lower = slice(48, 64), slice(32, 40), slice(40, 48)
    wide = [part(last, 0), part(last, 1), part(last, 2), part(slice(16, 32), 0)]
    short = [part(upper, 0), part(upper, 1), part(lower, 0), part(lower, 1)]
    shape = (16, 16, 128)
    major, minor = lax.broadcasted_iota(jnp.int32, shape, 0), lax.broadcasted_iota(jnp.int32, shape, 1)
    corner, edge = [], []
    for q in (0, 2):
        one, other = (
            block[16 * k : 16 * k + 16, 16 * k : 16 * k + 16, :].astype(f32) for k in (q, q + 1)
        )
        pair = jnp.where(minor <= major, one, other).astype(bf16)
        corner += [pair[0:8].reshape(128, 128), pair[8:16].reshape(128, 128)]
        edge += [jnp.zeros((16, 128), bf16), jnp.sum(jnp.where(minor == major, other, 0.0), axis=0).astype(bf16)]
    return [jnp.concatenate(parts, axis=1) for parts in (wide, short, corner, edge)]


def pack_first_kernel(neighbours, rhs, coupling, pivot, out0, out1, out2, out3, place, rhs_out, *scratch):
    *held, sems = scratch
    copies = start_fetch((neighbours, rhs, coupling, pivot), held, sems)
    neighbours, rhs, coupling, pivot = held
    cross = lax.axis_index("cross")
    square = (128, 128)
    lane = lax.broadcasted_iota(jnp.int32, square, 1)
    sub = row_of(square)
    copies[0].wait()

    def step_down(face):
        near = neighbours[face : face + 1, :] - cross * 128
        return jnp.where((near == sub) & (lane != sub), 1.0, 0.0).astype(bf16)

    ones = jnp.ones((16, 128), bf16)
    across = step_down(0)
    once = matmul(ones, across)
    twice = matmul(once.astype(bf16), across)
    column = once + twice + matmul(twice.astype(bf16), across)
    jump = step_down(2)
    row = matmul(ones, jump)
    for turn in range(5):
        row = row + matmul(row.astype(bf16), jump)
        if turn < 4:
            jump = matmul(jump, jump).astype(bf16)
    owner = jnp.where(cross % 2 == 0, column, 3.0 - column)
    position = (owner * 32.0 + row).astype(jnp.int32)[0:1]

    place[...] = jnp.broadcast_to(position, place.shape)

    sorting = sorting_matrix(position)
    outs = (out0, out1, out2, out3)
    copies[2].wait()
    left = [coupling[:, 16 * q : 16 * q + 16, :].reshape(BLOCK_ROWS, 128) for q in range(4)]
    send(jnp.concatenate(left, axis=1), sorting, outs, COUPLING, BLOCK_ROWS)

    copies[1].wait()
    copies[3].wait()
    rhs_out[...] = rhs[...]
    rows = parts_of(pivot)
    for part in bf16_parts(rhs[...], 2):
        rows.append(jnp.concatenate([part[16 * q : 16 * q + 16] for q in range(4)], axis=1))
    send(jnp.concatenate(rows, axis=0), sorting, outs, WIDE, FIRST_ROWS - WIDE)


def pack_second_kernel(diagonal, face_type, place, after, out0, out1, out2, out3, weights, order, held, faces, sems):
    copies = start_fetch((diagonal, face_type), (held, faces), sems)
    sub = row_of((128, 128))
    position = place[0:1, :]
    order[...] = sorting_matrix(position)
    copies[0].wait()
    send(jnp.concatenate(parts_of(held), axis=0), order[...], (out0, out1, out2, out3), 0, SECOND_ROWS)

    copies[1].wait()
    interior = jnp.where(faces[...] == 0, 2.0, 0.0)
    own = interior + jnp.where(faces[...] == 1, 4.0, 0.0)
    table = jnp.concatenate([own, interior, jnp.zeros((8, 128), f32)], axis=0).astype(bf16)
    placed = matmul_nt(table, jnp.where(hits_of(position, 0, sub & 31), 1.0, 0.0).astype(bf16))
    shape = (16, 128)
    seg, m = segment_of(shape), row_of(shape)
    masks = [seg == 0, seg == 3, m < 4, m >= 12]
    total = jnp.zeros(shape, f32)
    for face in range(4):
        total = total + jnp.where(masks[face], placed[face : face + 1], 0.0)
        weights[1 + face] = jnp.where(masks[face], placed[4 + face : 5 + face], 0.0)
    weights[0] = total


def in_hbm(*arrays):
    return [pltpu.with_memory_space_constraint(array, pltpu.HBM) for array in arrays]


def to_packed(spread):
    seg = segment_of((16, 128))
    low = jnp.where(seg == 0, spread[0:16], spread[16:32])
    high = jnp.where(seg == 2, spread[32:48], spread[48:64])
    return jnp.where(seg < 2, low, high)


def to_spread(packed):
    seg = segment_of((16, 128))
    rolled = [packed] + [pltpu.roll(packed, 32 * k, 1) for k in (1, 2, 3)]
    parts = []
    for q in range(4):
        low = jnp.where(seg == 0, rolled[-q % 4], rolled[(1 - q) % 4])
        high = jnp.where(seg == 2, rolled[(2 - q) % 4], rolled[(3 - q) % 4])
        parts.append(jnp.where(seg < 2, low, high))
    return jnp.concatenate(parts, axis=0)


def over_segments(value):
    return (value + pltpu.roll(value, 32, 1)) + (pltpu.roll(value, 64, 1) + pltpu.roll(value, 96, 1))


def transposed_times(blocks, elem, start, spread, row_ref):
    row_ref[...] = spread
    sums = [None] * 4
    for a in range(64):
        term = blocks[elem, start + 16 * a : start + 16 * a + 16, :].astype(f32) * row_ref[a : a + 1, :]
        sums[a % 4] = term if sums[a % 4] is None else sums[a % 4] + term
    return (sums[0] + sums[1]) + (sums[2] + sums[3])


def times(blocks, elem, start, packed):
    block = blocks[elem, start : start + BLOCK_ROWS, :].astype(f32).reshape(64, 16, 128)
    return over_segments(jnp.sum(block * packed[None], axis=1))


def turn_segments(rows):
    seg = segment_of(rows[0].shape)
    rows = list(rows)
    for width, low in ((2, seg < 2), (1, (seg & 1) == 0)):
        for j in range(4):
            if j & width:
                continue
            x, y = rows[j], rows[j + width]
            rows[j] = jnp.where(low, x, pltpu.roll(y, 32 * width, 1))
            rows[j + width] = jnp.where(low, pltpu.roll(x, 128 - 32 * width, 1), y)
    return rows


def corner_row(read, k):
    odd = segment_of((16, 128)) % 2 == 1
    start = CORNER - WIDE + 16 * (k % 8)
    row = read(start, 16)
    if k < 8:
        return jnp.where(odd, pltpu.roll(row, 32, 1), row)
    return jnp.where(odd, row, pltpu.roll(row, 96, 1))


def unpack(chunk, blocks, wide):
    shape = (16, 128)
    seg, m = segment_of(shape), row_of(shape)

    def read(start, rows):
        return chunk[start : start + rows, :].astype(f32)

    blocks[0:BLOCK_ROWS, :] = chunk[COUPLING : COUPLING + BLOCK_ROWS, :]
    for k in range(16):
        corner = corner_row(lambda start, rows: read(WIDE + start, rows), k)
        last = read(WIDE + 16 * k, 16)
        third = read(SHORT + 16 * (k % 8), 16)
        if k >= 8:
            third = pltpu.roll(third, 64, 1)
        wide[16 * k : 16 * k + 16, :] = corner
        wide[256 + 16 * k : 272 + 16 * k, :] = jnp.where(seg == 0, pltpu.roll(last, 32, 1), corner)
        wide[512 + 16 * k : 528 + 16 * k, :] = jnp.where(seg == 2, corner, third)
        wide[768 + 16 * k : 784 + 16 * k, :] = jnp.where(seg == 3, corner, last)
    edge = read(EDGE, 16)
    for k in range(16):
        turned = turn_segments([wide[pl.ds(256 * q + k, 16, stride=16), :] for q in range(4)])
        for q in range(4):
            a = 16 * q + k
            here = (seg < q) | ((seg == q) & ((m <= k) if q % 2 == 0 else (m > k)))
            value = jnp.where(here, wide[16 * a : 16 * a + 16, :], turned[q])
            if q % 2 == 1:
                value = jnp.where((seg == q) & (m == k), edge, value)
            blocks[PIVOT + 16 * a : PIVOT + 16 * a + 16, :] = value.astype(bf16)
    return read(RESIDUAL, 16) + read(RESIDUAL + 16, 16)


def diagonal_times(parts, packed):
    shape = (16, 128)
    seg, m = segment_of(shape), row_of(shape)
    spread = to_spread(packed)
    v0, v1, v2, v3 = (spread[16 * q : 16 * q + 16] for q in range(4))

    def both_ways(block, count, across, along):
        down = [block[k] * across[k : k + 1] for k in range(count)]
        while len(down) > 1:
            down = [x + y for x, y in zip(down[::2], down[1::2], strict=True)]
        return down[0], jnp.sum(block * along[None], axis=1)

    odd = seg % 2 == 1
    diagonal = parts[EDGE - WIDE : EDGE - WIDE + 16, :].astype(f32)
    corner = []
    for k in range(16):
        row = corner_row(lambda start, rows: parts[start : start + rows, :].astype(f32), k)
        diagonal = jnp.where((m == k) & ~odd, row, diagonal)
        corner.append(jnp.where(jnp.where(odd, m - k, k - m) > 0, row, 0.0))
    down, right = both_ways(jnp.concatenate(corner, axis=0).reshape(16, 16, 128), 16, packed, packed)
    total = down + right + diagonal * packed
    wide = parts[0 : SHORT - WIDE, :].astype(f32).reshape(16, 16, 128)
    down, right = both_ways(wide, 16, jnp.where(seg == 3, v1, v3), jnp.where(seg == 3, v0, packed))
    total = total + jnp.where(seg < 3, down, 0.0) + jnp.where(seg == 0, pltpu.roll(down, 32, 1), 0.0)
    turned = [pltpu.roll(right, 32 * k, 1) for k in (1, 2, 3)]
    total = total + jnp.where(seg == 3, (turned[0] + turned[1]) + turned[2], jnp.where(seg == 1, turned[1], 0.0))
    short = parts[SHORT - WIDE : CORNER - WIDE, :].astype(f32).reshape(8, 16, 128)
    down, right = both_ways(short, 8, jnp.where(seg[0:8] < 2, v2[0:8], v2[8:16]), jnp.where(odd, v1, v0))
    total = total + jnp.where(seg < 2, down + pltpu.roll(down, 64, 1), 0.0)
    upper = pltpu.roll(right, 64, 1) + pltpu.roll(right, 32, 1)
    lower = right + pltpu.roll(right, 96, 1)
    return total + jnp.where(seg == 2, jnp.concatenate([upper, lower], axis=0), 0.0)


def line_solve(residual, blocks, row_ref):
    forward = []
    for elem in range(4):
        right = to_spread(residual[elem])
        if elem > 0:
            right = right - times(blocks, elem, COUPLING, forward[-1])
        forward.append(transposed_times(blocks, elem, PIVOT, right, row_ref))
    values = [None] * 4
    carried = None
    for elem in reversed(range(4)):
        value = to_spread(forward[elem])
        if carried is not None:
            value = value - times(blocks, elem, PIVOT, carried)
        values[elem] = value
        if elem > 0:
            carried = transposed_times(blocks, elem, COUPLING, value, row_ref)
    return values


def is_even_column():
    return (lax.axis_index("field") + lax.axis_index("cross")) % 2 == 0


def send_faces(packed, inner, outer):
    seg = segment_of((16, 128))
    to_next, to_before = packed[3], packed[0]
    for elem in range(3):
        to_next = jnp.where(seg == elem, pltpu.roll(packed[elem], 32 * (elem + 1), 1), to_next)
        to_before = jnp.where(seg == elem + 1, pltpu.roll(packed[elem + 1], 32 * (elem + 1), 1), to_before)
    even = is_even_column()
    inner[...] = jnp.where(even, to_next, to_before)
    outer[...] = jnp.where(even, to_before, to_next)


def line_apply(packed, blocks, products, weights, row_ref):
    spread = [to_spread(v) for v in packed]
    rows = []
    for elem in range(4):
        v = packed[elem]
        total = products[elem]
        if elem > 0:
            total = total + to_packed(times(blocks, elem, COUPLING, packed[elem - 1]))
        if elem < 3:
            total = total + transposed_times(blocks, elem + 1, COUPLING, spread[elem + 1], row_ref)
        below = pltpu.roll(pltpu.roll(v, 4, 0), 1, 1)
        above = pltpu.roll(pltpu.roll(v, 12, 0), 127, 1)
        rows.append(total + weights[0] * v - weights[3] * below - weights[4] * above)
    return rows


def add_faces(partial, inner, outer, weights):
    even = is_even_column()
    before = jnp.where(even, outer[...], inner[...])
    after = jnp.where(even, inner[...], outer[...])
    rows = []
    for elem in range(4):
        left = before if elem == 0 else pltpu.roll(before, 128 - 32 * elem, 1)
        right = after if elem == 3 else pltpu.roll(after, 32 * (3 - elem), 1)
        rows.append(partial[elem] - weights[1] * left - weights[2] * right)
    return rows


def product_sum(first, second):
    total = first[0] * second[0]
    for elem in range(1, 4):
        total = total + first[elem] * second[elem]
    return jnp.sum(total, axis=0, keepdims=True)


def unpack_kernel(chunk, blocks, residual, wide):
    residual[...] = unpack(chunk, blocks, wide)


def solve_kernel(b0, r0, b1, r1, b3, r3, chunk, blocks, residual, values, inner_out, outer_out, row_ref, wide, sems):
    me = lax.axis_index("field")
    copies = []
    for d, source, part in ((0, b0, r0), (1, b1, r1), (3, b3, r3)):
        elem = (me - d) & 3
        residual[elem] = part[...]
        copies.append(pltpu.make_async_copy(source, blocks.at[elem], sems.at[d]))
    for copy in copies:
        copy.start()
    elem = (me - 2) & 3
    residual[elem] = unpack(chunk, blocks.at[elem], wide)
    for copy in copies:
        copy.wait()
    packed = [to_packed(v) for v in line_solve([residual[elem] for elem in range(4)], blocks, row_ref)]
    for elem in range(4):
        values[elem] = packed[elem]
    send_faces(packed, inner_out, outer_out)


def apply_kernel(blocks, p0, p1, p2, p3, vector, weights, partial, row_ref, products):
    me = lax.axis_index("field")
    for d, parts in enumerate((p0, p1, p2, p3)):
        elem = (me - d) & 3
        products[elem] = diagonal_times(parts, vector[elem])
    rows = line_apply([vector[elem] for elem in range(4)], blocks, products, weights, row_ref)
    for elem in range(4):
        partial[elem] = rows[elem]


def join_solve_kernel(blocks, partial, inner, outer, weights, image, values, inner_out, outer_out, row_ref):
    rows = add_faces(partial, inner, outer, weights)
    packed = [to_packed(v) for v in line_solve(rows, blocks, row_ref)]
    for elem in range(4):
        image[elem] = rows[elem]
        values[elem] = packed[elem]
    send_faces(packed, inner_out, outer_out)


def sums_kernel(partial, inner, outer, weights, r, z, w, s, image, sums):
    rows = add_faces(partial, inner, outer, weights)

    def values(ref):
        return [ref[elem] for elem in range(4)]

    z_, w_, s_ = values(z), values(w), values(s)
    seg = segment_of((1, 128))
    total = jnp.zeros((1, 128), f32)
    for index, pair in enumerate(((values(r), z_), (z_, w_), (w_, s_), (s_, rows))):
        total = jnp.where(seg == index, over_segments(product_sum(*pair)), total)
    for elem in range(4):
        image[elem] = rows[elem]
    sums[...] = jnp.broadcast_to(total, sums.shape)


def fold_kernel(rows, total):
    total[...] = jnp.broadcast_to(jnp.sum(rows[...], axis=0), total.shape)


def last_solve_kernel(blocks, z, w, s, t, back0, back1, back2, back3, row_ref, u):
    packed = [to_packed(v) for v in line_solve([t[elem] for elem in range(4)], blocks, row_ref)]
    for elem in range(4):
        u[elem] = packed[elem]
    me = lax.axis_index("field")
    for d, back in enumerate((back0, back1, back2, back3)):
        elem = (me + d) & 3
        for index, ref in enumerate((z, w, s, t, u)):
            back[16 * index : 16 * index + 16, :] = ref[elem]


def final_kernel(s0, s1, s2, s3, rhs, b0, b1, b2, b3, order, solution, residual, precond):
    backs = (b0, b3, b2, b1)
    z, w, s, t, u = (
        jnp.concatenate([b[16 * index : 16 * index + 16, :] for b in backs], axis=1) for index in range(5)
    )
    total = ((s0[...] + s1[...]) + (s2[...] + s3[...]))[0:1]
    totals = [jnp.sum(total[:, 32 * k : 32 * k + 32], axis=1, keepdims=True) for k in range(4)]
    rho, curve, second, third = totals
    alpha = rho / curve
    rho_next = rho - 2.0 * alpha * curve + alpha * alpha * second
    grown = 1.0 + rho_next / rho
    curve_next = grown * grown * curve - 2.0 * alpha * grown * second + alpha * alpha * third
    alpha_next = rho_next / curve_next
    first = alpha + alpha_next * grown
    other = alpha_next * alpha
    combos = [first * z - other * s, other * t - first * w, z - first * s + other * u]
    parts = [part for combo in combos for part in bf16_parts(combo, 3)]
    moved = matmul(jnp.concatenate(parts, axis=0), order[...])
    for index, ref in enumerate((solution, residual, precond)):
        rows = moved[48 * index : 48 * index + 48]
        value = (rows[0:16] + rows[16:32]) + rows[32:48]
        for q in range(4):
            part = value[:, 128 * q : 128 * q + 128]
            if index == 1:
                part = part + rhs[16 * q : 16 * q + 16, :]
            ref[16 * q : 16 * q + 16, :] = part


FACE = jax.ShapeDtypeStruct((16, 128), f32)
VECTOR = jax.ShapeDtypeStruct((4, 16, 128), f32)
BACK = jax.ShapeDtypeStruct((80, 128), f32)
BLOCKS = jax.ShapeDtypeStruct((4, ELEMENT_ROWS, 128), bf16)


def kernel(body, arrays, outs, name, spec=VMEM, scratch=()):
    return pl.pallas_call(
        body,
        out_shape=outs,
        in_specs=spec if isinstance(spec, list) else [spec] * len(arrays),
        out_specs=[VMEM] * len(outs),
        scratch_shapes=list(scratch),
        compiler_params=params(),
        name=name,
    )(*arrays)


def around(value, distance):
    count = lax.axis_size("field")
    return lax.ppermute(value, "field", [(i, (i + distance) % count) for i in range(count)])


def column_swaps(first):
    field, cross = lax.axis_size("field"), lax.axis_size("cross")
    device = {}
    for c in range(cross):
        for f in range(field):
            device[field * c + (f if c % 2 == 0 else field - 1 - f)] = f * cross + c
    pairs = [(device[g], device[g + 1]) for g in range(first, field * cross - 1, 2)]
    return pairs + [(b, a) for a, b in pairs]


def exchange(inner, outer):
    return [lax.ppermute(faces, ("field", "cross"), column_swaps(first)) for first, faces in enumerate((inner, outer))]


def local(rhs, pivot_inverse, line_coupling, element_block, neighbours, face_type):
    matrix, small = pltpu.VMEM((64, 64, 128), bf16), pltpu.VMEM((4, 128), jnp.int32)
    spread, wide = pltpu.VMEM((64, 128), f32), pltpu.VMEM((BLOCK_ROWS + 16, 128), f32)
    shape = jax.ShapeDtypeStruct((64, 128), f32)
    *chunks, place, rhs_here = kernel(
        pack_first_kernel,
        in_hbm(neighbours.T, rhs[0], line_coupling[0], pivot_inverse[0]),
        [jax.ShapeDtypeStruct((FIRST_ROWS, 128), bf16)] * 4 + [jax.ShapeDtypeStruct((8, 128), jnp.int32), shape],
        "pack_first",
        HBM,
        [small, pltpu.VMEM((64, 128), f32), matrix, matrix, pltpu.SemaphoreType.DMA((4,))],
    )
    held = []
    first = {d: around(chunks[d], d) if d else chunks[0] for d in (0, 1, 3, 2)}
    for d in (0, 1, 3):
        last = kernel(
            unpack_kernel,
            [first[d]],
            [jax.ShapeDtypeStruct((ELEMENT_ROWS, 128), bf16), FACE],
            f"unpack_{d}",
            scratch=[wide],
        )
        held += last
        if d == 1:
            *chunks, weights, order = kernel(
                pack_second_kernel,
                in_hbm(element_block[0], face_type.T) + [place, last[1]],
                [jax.ShapeDtypeStruct((SECOND_ROWS, 128), bf16)] * 4
                + [jax.ShapeDtypeStruct((5, 16, 128), f32), jax.ShapeDtypeStruct((512, 512), bf16)],
                "pack_second",
                [HBM, HBM, VMEM, VMEM],
                [matrix, small, pltpu.SemaphoreType.DMA((2,))],
            )
            second = {d: around(chunks[d], d) if d else chunks[0] for d in (0, 1, 3, 2)}
    blocks, r, z, inner, outer = kernel(
        solve_kernel,
        [*held, first[2]],
        [BLOCKS, VECTOR, VECTOR, FACE, FACE],
        "solve_first",
        scratch=[spread, wide, pltpu.SemaphoreType.DMA((4,))],
    )
    inner, outer = exchange(inner, outer)
    parts = [second[d] for d in range(4)]
    products = pltpu.VMEM((4, 16, 128), f32)
    (partial,) = kernel(apply_kernel, [blocks, *parts, z, weights], [VECTOR], "apply_first", scratch=[spread, products])
    w, s, inner, outer = kernel(
        join_solve_kernel,
        [blocks, partial, inner, outer, weights],
        [VECTOR, VECTOR, FACE, FACE],
        "solve_second",
        scratch=[spread],
    )
    inner, outer = exchange(inner, outer)
    (partial,) = kernel(apply_kernel, [blocks, *parts, s, weights], [VECTOR], "apply_second", scratch=[spread, products])
    count = lax.axis_size("cross")
    t, rows = kernel(
        sums_kernel,
        [partial, inner, outer, weights, r, z, w, s],
        [VECTOR, jax.ShapeDtypeStruct((count, 128), f32)],
        "sums",
    )
    rows = lax.all_to_all(rows.reshape(count, 1, 128), "cross", 0, 0)
    backs = kernel(
        last_solve_kernel, [blocks, z, w, s, t], [BACK] * 4, "solve_last", scratch=[spread, pltpu.VMEM((4, 16, 128), f32)]
    )
    returned = [backs[0]] + [around(backs[d], d) for d in (1, 2, 3)]
    (total,) = kernel(fold_kernel, [rows], [jax.ShapeDtypeStruct((8, 128), f32)], "fold")
    totals = [total] + [around(total, d) for d in (1, 2, 3)]
    outs = kernel(final_kernel, [*totals, rhs_here, *returned, order], [shape] * 3, "final")
    return tuple(out[None] for out in outs)


def solution(mesh):
    placed = (
        P("field", None, "cross"),
        P("field", None, None, "cross"),
        P("field", None, None, "cross"),
        P("field", None, None, "cross"),
        P("cross", None),
        P("cross", None),
    )
    return jax.shard_map(
        local,
        mesh=mesh,
        in_specs=placed,
        out_specs=(P("field", None, "cross"), P("field", None, "cross"), P("field", None, "cross")),
        check_vma=False,
    )
```

```python
import jax
import jax.numpy as jnp
from jax import lax
from jax.experimental import pallas as pl
from jax.experimental.pallas import tpu as pltpu
from jax.sharding import PartitionSpec as P


BLOCK_ROWS = 1024
COUPLING, WIDE, SHORT, CORNER, EDGE, RESIDUAL = (0, 1024, 1280, 1408, 1536, 1552)
FIRST_ROWS = 1552 + 32
SECOND_ROWS = RESIDUAL - WIDE
PIVOT = 1024
ELEMENT_ROWS = 2048
VMEM_LIMIT = 24 * 1024 * 1024

VMEM = pl.BlockSpec(memory_space=pltpu.VMEM)
HBM = pl.BlockSpec(memory_space=pltpu.HBM)

f32 = jnp.float32
bf16 = jnp.bfloat16


def params():
    return pltpu.CompilerParams(vmem_limit_bytes=VMEM_LIMIT)


def segment_of(shape):
    return lax.broadcasted_iota(jnp.int32, shape, 1) >> 5


def row_of(shape):
    return lax.broadcasted_iota(jnp.int32, shape, 0)


def matmul(left, right):
    return jnp.dot(left, right, preferred_element_type=f32)


def matmul_nt(left, right):
    return lax.dot_general(left, right, (((1,), (1,)), ((), ())), preferred_element_type=f32)


def bf16_parts(value, count):
    parts = []
    for _ in range(count):
        parts.append(value.astype(bf16))
        value = value - parts[-1].astype(f32)
    return parts


def start_fetch(sources, targets, sems):
    copies = [pltpu.make_async_copy(*pair, sems.at[i]) for i, pair in enumerate(zip(sources, targets, strict=True))]
    for copy in copies:
        copy.start()
    return copies


def send(left, sorting, outs, start, rows):
    result = matmul_nt(left, sorting).astype(bf16)
    for d in range(4):
        outs[d][start : start + rows, :] = result[:, d * 128 : (d + 1) * 128]


def hits_of(position, distance, line):
    return position == ((lax.axis_index("field") + distance) & 3) * 32 + line


def sorting_matrix(position):
    sub = row_of((128, 128))
    rows = []
    for d in range(4):
        hit = hits_of(position, d, sub & 31)
        rows.append(jnp.concatenate([jnp.where(hit & ((sub >> 5) == q), 1.0, 0.0) for q in range(4)], axis=1))
    return jnp.concatenate(rows, axis=0).astype(bf16)


def parts_of(block):
    def part(rows, column):
        return block[rows, 16 * column : 16 * column + 16, :].reshape(-1, 128)

    last, upper, lower = slice(48, 64), slice(32, 40), slice(40, 48)
    wide = [part(last, 0), part(last, 1), part(last, 2), part(slice(16, 32), 0)]
    short = [part(upper, 0), part(upper, 1), part(lower, 0), part(lower, 1)]
    shape = (16, 16, 128)
    major, minor = lax.broadcasted_iota(jnp.int32, shape, 0), lax.broadcasted_iota(jnp.int32, shape, 1)
    corner, edge = [], []
    for q in (0, 2):
        one, other = (
            block[16 * k : 16 * k + 16, 16 * k : 16 * k + 16, :].astype(f32) for k in (q, q + 1)
        )
        pair = jnp.where(minor <= major, one, other).astype(bf16)
        corner += [pair[0:8].reshape(128, 128), pair[8:16].reshape(128, 128)]
        edge += [jnp.zeros((16, 128), bf16), jnp.sum(jnp.where(minor == major, other, 0.0), axis=0).astype(bf16)]
    return [jnp.concatenate(parts, axis=1) for parts in (wide, short, corner, edge)]


def pack_first_kernel(neighbours, rhs, coupling, pivot, out0, out1, out2, out3, place, rhs_out, *scratch):
    *held, sems = scratch
    copies = start_fetch((neighbours, rhs, coupling, pivot), held, sems)
    neighbours, rhs, coupling, pivot = held
    cross = lax.axis_index("cross")
    square = (128, 128)
    lane = lax.broadcasted_iota(jnp.int32, square, 1)
    sub = row_of(square)
    copies[0].wait()

    def step_down(face):
        near = neighbours[face : face + 1, :] - cross * 128
        return jnp.where((near == sub) & (lane != sub), 1.0, 0.0).astype(bf16)

    ones = jnp.ones((16, 128), bf16)
    across = step_down(0)
    once = matmul(ones, across)
    twice = matmul(once.astype(bf16), across)
    column = once + twice + matmul(twice.astype(bf16), across)
    jump = step_down(2)
    row = matmul(ones, jump)
    for turn in range(5):
        row = row + matmul(row.astype(bf16), jump)
        if turn < 4:
            jump = matmul(jump, jump).astype(bf16)
    owner = jnp.where(cross % 2 == 0, column, 3.0 - column)
    position = (owner * 32.0 + row).astype(jnp.int32)[0:1]

    place[...] = jnp.broadcast_to(position, place.shape)

    sorting = sorting_matrix(position)
    outs = (out0, out1, out2, out3)
    copies[2].wait()
    left = [coupling[:, 16 * q : 16 * q + 16, :].reshape(BLOCK_ROWS, 128) for q in range(4)]
    send(jnp.concatenate(left, axis=1), sorting, outs, COUPLING, BLOCK_ROWS)

    copies[1].wait()
    copies[3].wait()
    rhs_out[...] = rhs[...]
    rows = parts_of(pivot)
    for part in bf16_parts(rhs[...], 2):
        rows.append(jnp.concatenate([part[16 * q : 16 * q + 16] for q in range(4)], axis=1))
    send(jnp.concatenate(rows, axis=0), sorting, outs, WIDE, FIRST_ROWS - WIDE)


def pack_second_kernel(diagonal, face_type, place, after, out0, out1, out2, out3, weights, order, held, faces, sems):
    copies = start_fetch((diagonal, face_type), (held, faces), sems)
    sub = row_of((128, 128))
    position = place[0:1, :]
    order[...] = sorting_matrix(position)
    copies[0].wait()
    send(jnp.concatenate(parts_of(held), axis=0), order[...], (out0, out1, out2, out3), 0, SECOND_ROWS)

    copies[1].wait()
    interior = jnp.where(faces[...] == 0, 2.0, 0.0)
    own = interior + jnp.where(faces[...] == 1, 4.0, 0.0)
    table = jnp.concatenate([own, interior, jnp.zeros((8, 128), f32)], axis=0).astype(bf16)
    placed = matmul_nt(table, jnp.where(hits_of(position, 0, sub & 31), 1.0, 0.0).astype(bf16))
    shape = (16, 128)
    seg, m = segment_of(shape), row_of(shape)
    masks = [seg == 0, seg == 3, m < 4, m >= 12]
    total = jnp.zeros(shape, f32)
    for face in range(4):
        total = total + jnp.where(masks[face], placed[face : face + 1], 0.0)
        weights[1 + face] = jnp.where(masks[face], placed[4 + face : 5 + face], 0.0)
    weights[0] = total


def in_hbm(*arrays):
    return [pltpu.with_memory_space_constraint(array, pltpu.HBM) for array in arrays]


def to_packed(spread):
    seg = segment_of((16, 128))
    low = jnp.where(seg == 0, spread[0:16], spread[16:32])
    high = jnp.where(seg == 2, spread[32:48], spread[48:64])
    return jnp.where(seg < 2, low, high)


def to_spread(packed):
    seg = segment_of((16, 128))
    rolled = [packed] + [pltpu.roll(packed, 32 * k, 1) for k in (1, 2, 3)]
    parts = []
    for q in range(4):
        low = jnp.where(seg == 0, rolled[-q % 4], rolled[(1 - q) % 4])
        high = jnp.where(seg == 2, rolled[(2 - q) % 4], rolled[(3 - q) % 4])
        parts.append(jnp.where(seg < 2, low, high))
    return jnp.concatenate(parts, axis=0)


def over_segments(value):
    return (value + pltpu.roll(value, 32, 1)) + (pltpu.roll(value, 64, 1) + pltpu.roll(value, 96, 1))


def transposed_times(blocks, elem, start, spread, row_ref):
    row_ref[...] = spread
    sums = [None] * 4
    for a in range(64):
        term = blocks[elem, start + 16 * a : start + 16 * a + 16, :].astype(f32) * row_ref[a : a + 1, :]
        sums[a % 4] = term if sums[a % 4] is None else sums[a % 4] + term
    return (sums[0] + sums[1]) + (sums[2] + sums[3])


def times(blocks, elem, start, packed):
    block = blocks[elem, start : start + BLOCK_ROWS, :].astype(f32).reshape(64, 16, 128)
    return over_segments(jnp.sum(block * packed[None], axis=1))


def turn_segments(rows):
    seg = segment_of(rows[0].shape)
    rows = list(rows)
    for width, low in ((2, seg < 2), (1, (seg & 1) == 0)):
        for j in range(4):
            if j & width:
                continue
            x, y = rows[j], rows[j + width]
            rows[j] = jnp.where(low, x, pltpu.roll(y, 32 * width, 1))
            rows[j + width] = jnp.where(low, pltpu.roll(x, 128 - 32 * width, 1), y)
    return rows


def corner_row(read, k):
    odd = segment_of((16, 128)) % 2 == 1
    start = CORNER - WIDE + 16 * (k % 8)
    row = read(start, 16)
    if k < 8:
        return jnp.where(odd, pltpu.roll(row, 32, 1), row)
    return jnp.where(odd, row, pltpu.roll(row, 96, 1))


def unpack(chunk, blocks, wide):
    shape = (16, 128)
    seg, m = segment_of(shape), row_of(shape)

    def read(start, rows):
        return chunk[start : start + rows, :].astype(f32)

    blocks[0:BLOCK_ROWS, :] = chunk[COUPLING : COUPLING + BLOCK_ROWS, :]
    for k in range(16):
        corner = corner_row(lambda start, rows: read(WIDE + start, rows), k)
        last = read(WIDE + 16 * k, 16)
        third = read(SHORT + 16 * (k % 8), 16)
        if k >= 8:
            third = pltpu.roll(third, 64, 1)
        wide[16 * k : 16 * k + 16, :] = corner
        wide[256 + 16 * k : 272 + 16 * k, :] = jnp.where(seg == 0, pltpu.roll(last, 32, 1), corner)
        wide[512 + 16 * k : 528 + 16 * k, :] = jnp.where(seg == 2, corner, third)
        wide[768 + 16 * k : 784 + 16 * k, :] = jnp.where(seg == 3, corner, last)
    edge = read(EDGE, 16)
    for k in range(16):
        turned = turn_segments([wide[pl.ds(256 * q + k, 16, stride=16), :] for q in range(4)])
        for q in range(4):
            a = 16 * q + k
            here = (seg < q) | ((seg == q) & ((m <= k) if q % 2 == 0 else (m > k)))
            value = jnp.where(here, wide[16 * a : 16 * a + 16, :], turned[q])
            if q % 2 == 1:
                value = jnp.where((seg == q) & (m == k), edge, value)
            blocks[PIVOT + 16 * a : PIVOT + 16 * a + 16, :] = value.astype(bf16)
    return read(RESIDUAL, 16) + read(RESIDUAL + 16, 16)


def diagonal_times(parts, packed):
    shape = (16, 128)
    seg, m = segment_of(shape), row_of(shape)
    spread = to_spread(packed)
    v0, v1, v2, v3 = (spread[16 * q : 16 * q + 16] for q in range(4))

    def both_ways(block, count, across, along):
        down = [block[k] * across[k : k + 1] for k in range(count)]
        while len(down) > 1:
            down = [x + y for x, y in zip(down[::2], down[1::2], strict=True)]
        return down[0], jnp.sum(block * along[None], axis=1)

    odd = seg % 2 == 1
    diagonal = parts[EDGE - WIDE : EDGE - WIDE + 16, :].astype(f32)
    corner = []
    for k in range(16):
        row = corner_row(lambda start, rows: parts[start : start + rows, :].astype(f32), k)
        diagonal = jnp.where((m == k) & ~odd, row, diagonal)
        corner.append(jnp.where(jnp.where(odd, m - k, k - m) > 0, row, 0.0))
    down, right = both_ways(jnp.concatenate(corner, axis=0).reshape(16, 16, 128), 16, packed, packed)
    total = down + right + diagonal * packed
    wide = parts[0 : SHORT - WIDE, :].astype(f32).reshape(16, 16, 128)
    down, right = both_ways(wide, 16, jnp.where(seg == 3, v1, v3), jnp.where(seg == 3, v0, packed))
    total = total + jnp.where(seg < 3, down, 0.0) + jnp.where(seg == 0, pltpu.roll(down, 32, 1), 0.0)
    turned = [pltpu.roll(right, 32 * k, 1) for k in (1, 2, 3)]
    total = total + jnp.where(seg == 3, (turned[0] + turned[1]) + turned[2], jnp.where(seg == 1, turned[1], 0.0))
    short = parts[SHORT - WIDE : CORNER - WIDE, :].astype(f32).reshape(8, 16, 128)
    down, right = both_ways(short, 8, jnp.where(seg[0:8] < 2, v2[0:8], v2[8:16]), jnp.where(odd, v1, v0))
    total = total + jnp.where(seg < 2, down + pltpu.roll(down, 64, 1), 0.0)
    upper = pltpu.roll(right, 64, 1) + pltpu.roll(right, 32, 1)
    lower = right + pltpu.roll(right, 96, 1)
    return total + jnp.where(seg == 2, jnp.concatenate([upper, lower], axis=0), 0.0)


def line_solve(residual, blocks, row_ref):
    forward = []
    for elem in range(4):
        right = to_spread(residual[elem])
        if elem > 0:
            right = right - times(blocks, elem, COUPLING, forward[-1])
        forward.append(transposed_times(blocks, elem, PIVOT, right, row_ref))
    values = [None] * 4
    carried = None
    for elem in reversed(range(4)):
        value = to_spread(forward[elem])
        if carried is not None:
            value = value - times(blocks, elem, PIVOT, carried)
        values[elem] = value
        if elem > 0:
            carried = transposed_times(blocks, elem, COUPLING, value, row_ref)
    return values


def is_even_column():
    return (lax.axis_index("field") + lax.axis_index("cross")) % 2 == 0


def send_faces(packed, inner, outer):
    seg = segment_of((16, 128))
    to_next, to_before = packed[3], packed[0]
    for elem in range(3):
        to_next = jnp.where(seg == elem, pltpu.roll(packed[elem], 32 * (elem + 1), 1), to_next)
        to_before = jnp.where(seg == elem + 1, pltpu.roll(packed[elem + 1], 32 * (elem + 1), 1), to_before)
    even = is_even_column()
    inner[...] = jnp.where(even, to_next, to_before)
    outer[...] = jnp.where(even, to_before, to_next)


def line_apply(packed, blocks, products, weights, row_ref):
    spread = [to_spread(v) for v in packed]
    rows = []
    for elem in range(4):
        v = packed[elem]
        total = products[elem]
        if elem > 0:
            total = total + to_packed(times(blocks, elem, COUPLING, packed[elem - 1]))
        if elem < 3:
            total = total + transposed_times(blocks, elem + 1, COUPLING, spread[elem + 1], row_ref)
        below = pltpu.roll(pltpu.roll(v, 4, 0), 1, 1)
        above = pltpu.roll(pltpu.roll(v, 12, 0), 127, 1)
        rows.append(total + weights[0] * v - weights[3] * below - weights[4] * above)
    return rows


def add_faces(partial, inner, outer, weights):
    even = is_even_column()
    before = jnp.where(even, outer[...], inner[...])
    after = jnp.where(even, inner[...], outer[...])
    rows = []
    for elem in range(4):
        left = before if elem == 0 else pltpu.roll(before, 128 - 32 * elem, 1)
        right = after if elem == 3 else pltpu.roll(after, 32 * (3 - elem), 1)
        rows.append(partial[elem] - weights[1] * left - weights[2] * right)
    return rows


def product_sum(first, second):
    total = first[0] * second[0]
    for elem in range(1, 4):
        total = total + first[elem] * second[elem]
    return jnp.sum(total, axis=0, keepdims=True)


def unpack_kernel(chunk, blocks, residual, wide):
    residual[...] = unpack(chunk, blocks, wide)


def solve_kernel(b0, r0, b1, r1, b3, r3, chunk, blocks, residual, values, inner_out, outer_out, row_ref, wide, sems):
    me = lax.axis_index("field")
    copies = []
    for d, source, part in ((0, b0, r0), (1, b1, r1), (3, b3, r3)):
        elem = (me - d) & 3
        residual[elem] = part[...]
        copies.append(pltpu.make_async_copy(source, blocks.at[elem], sems.at[d]))
    for copy in copies:
        copy.start()
    elem = (me - 2) & 3
    residual[elem] = unpack(chunk, blocks.at[elem], wide)
    for copy in copies:
        copy.wait()
    packed = [to_packed(v) for v in line_solve([residual[elem] for elem in range(4)], blocks, row_ref)]
    for elem in range(4):
        values[elem] = packed[elem]
    send_faces(packed, inner_out, outer_out)


def apply_kernel(blocks, p0, p1, p2, p3, vector, weights, partial, row_ref, products):
    me = lax.axis_index("field")
    for d, parts in enumerate((p0, p1, p2, p3)):
        elem = (me - d) & 3
        products[elem] = diagonal_times(parts, vector[elem])
    rows = line_apply([vector[elem] for elem in range(4)], blocks, products, weights, row_ref)
    for elem in range(4):
        partial[elem] = rows[elem]


def join_solve_kernel(blocks, partial, inner, outer, weights, image, values, inner_out, outer_out, row_ref):
    rows = add_faces(partial, inner, outer, weights)
    packed = [to_packed(v) for v in line_solve(rows, blocks, row_ref)]
    for elem in range(4):
        image[elem] = rows[elem]
        values[elem] = packed[elem]
    send_faces(packed, inner_out, outer_out)


def sums_kernel(partial, inner, outer, weights, r, z, w, s, image, sums):
    rows = add_faces(partial, inner, outer, weights)

    def values(ref):
        return [ref[elem] for elem in range(4)]

    z_, w_, s_ = values(z), values(w), values(s)
    seg = segment_of((1, 128))
    total = jnp.zeros((1, 128), f32)
    for index, pair in enumerate(((values(r), z_), (z_, w_), (w_, s_), (s_, rows))):
        total = jnp.where(seg == index, over_segments(product_sum(*pair)), total)
    for elem in range(4):
        image[elem] = rows[elem]
    sums[...] = jnp.broadcast_to(total, sums.shape)


def fold_kernel(rows, total):
    total[...] = jnp.broadcast_to(jnp.sum(rows[...], axis=0), total.shape)


def last_solve_kernel(blocks, z, w, s, t, back0, back1, back2, back3, row_ref, u):
    packed = [to_packed(v) for v in line_solve([t[elem] for elem in range(4)], blocks, row_ref)]
    for elem in range(4):
        u[elem] = packed[elem]
    me = lax.axis_index("field")
    for d, back in enumerate((back0, back1, back2, back3)):
        elem = (me + d) & 3
        for index, ref in enumerate((z, w, s, t, u)):
            back[16 * index : 16 * index + 16, :] = ref[elem]


def place_kernel(b0, b1, b2, b3, order, placed):
    vectors = jnp.concatenate([b[...] for b in (b0, b3, b2, b1)], axis=1)
    moved = matmul(jnp.concatenate(bf16_parts(vectors, 3), axis=0), order[...])
    value = (moved[0:80] + moved[80:160]) + moved[160:240]
    for index in range(5):
        for q in range(4):
            start = 64 * index + 16 * q
            placed[start : start + 16, :] = value[16 * index : 16 * index + 16, 128 * q : 128 * q + 128]


def final_kernel(s0, s1, s2, s3, rhs, placed, solution, residual, precond):
    z, w, s, t, u = (placed[64 * index : 64 * index + 64, :] for index in range(5))
    total = ((s0[...] + s1[...]) + (s2[...] + s3[...]))[0:1]
    totals = [jnp.sum(total[:, 32 * k : 32 * k + 32], axis=1, keepdims=True) for k in range(4)]
    rho, curve, second, third = totals
    alpha = rho / curve
    rho_next = rho - 2.0 * alpha * curve + alpha * alpha * second
    grown = 1.0 + rho_next / rho
    curve_next = grown * grown * curve - 2.0 * alpha * grown * second + alpha * alpha * third
    alpha_next = rho_next / curve_next
    first = alpha + alpha_next * grown
    other = alpha_next * alpha
    solution[...] = first * z - other * s
    residual[...] = rhs[...] + (other * t - first * w)
    precond[...] = z - first * s + other * u


FACE = jax.ShapeDtypeStruct((16, 128), f32)
VECTOR = jax.ShapeDtypeStruct((4, 16, 128), f32)
BACK = jax.ShapeDtypeStruct((80, 128), f32)
BLOCKS = jax.ShapeDtypeStruct((4, ELEMENT_ROWS, 128), bf16)


def kernel(body, arrays, outs, name, spec=VMEM, scratch=()):
    return pl.pallas_call(
        body,
        out_shape=outs,
        in_specs=spec if isinstance(spec, list) else [spec] * len(arrays),
        out_specs=[VMEM] * len(outs),
        scratch_shapes=list(scratch),
        compiler_params=params(),
        name=name,
    )(*arrays)


def around(value, distance):
    count = lax.axis_size("field")
    return lax.ppermute(value, "field", [(i, (i + distance) % count) for i in range(count)])


def column_swaps(first):
    field, cross = lax.axis_size("field"), lax.axis_size("cross")
    device = {}
    for c in range(cross):
        for f in range(field):
            device[field * c + (f if c % 2 == 0 else field - 1 - f)] = f * cross + c
    pairs = [(device[g], device[g + 1]) for g in range(first, field * cross - 1, 2)]
    return pairs + [(b, a) for a, b in pairs]


def exchange(inner, outer):
    return [lax.ppermute(faces, ("field", "cross"), column_swaps(first)) for first, faces in enumerate((inner, outer))]


def local(rhs, pivot_inverse, line_coupling, element_block, neighbours, face_type):
    matrix, small = pltpu.VMEM((64, 64, 128), bf16), pltpu.VMEM((4, 128), jnp.int32)
    spread, wide = pltpu.VMEM((64, 128), f32), pltpu.VMEM((BLOCK_ROWS + 16, 128), f32)
    shape = jax.ShapeDtypeStruct((64, 128), f32)
    *chunks, place, rhs_here = kernel(
        pack_first_kernel,
        in_hbm(neighbours.T, rhs[0], line_coupling[0], pivot_inverse[0]),
        [jax.ShapeDtypeStruct((FIRST_ROWS, 128), bf16)] * 4 + [jax.ShapeDtypeStruct((8, 128), jnp.int32), shape],
        "pack_first",
        HBM,
        [small, pltpu.VMEM((64, 128), f32), matrix, matrix, pltpu.SemaphoreType.DMA((4,))],
    )
    held = []
    first = {d: around(chunks[d], d) if d else chunks[0] for d in (0, 1, 3, 2)}
    for d in (0, 1, 3):
        last = kernel(
            unpack_kernel,
            [first[d]],
            [jax.ShapeDtypeStruct((ELEMENT_ROWS, 128), bf16), FACE],
            f"unpack_{d}",
            scratch=[wide],
        )
        held += last
        if d == 1:
            *chunks, weights, order = kernel(
                pack_second_kernel,
                in_hbm(element_block[0], face_type.T) + [place, last[1]],
                [jax.ShapeDtypeStruct((SECOND_ROWS, 128), bf16)] * 4
                + [jax.ShapeDtypeStruct((5, 16, 128), f32), jax.ShapeDtypeStruct((512, 512), bf16)],
                "pack_second",
                [HBM, HBM, VMEM, VMEM],
                [matrix, small, pltpu.SemaphoreType.DMA((2,))],
            )
            second = {d: around(chunks[d], d) if d else chunks[0] for d in (0, 1, 3, 2)}
    blocks, r, z, inner, outer = kernel(
        solve_kernel,
        [*held, first[2]],
        [BLOCKS, VECTOR, VECTOR, FACE, FACE],
        "solve_first",
        scratch=[spread, wide, pltpu.SemaphoreType.DMA((4,))],
    )
    inner, outer = exchange(inner, outer)
    parts = [second[d] for d in range(4)]
    products = pltpu.VMEM((4, 16, 128), f32)
    (partial,) = kernel(apply_kernel, [blocks, *parts, z, weights], [VECTOR], "apply_first", scratch=[spread, products])
    w, s, inner, outer = kernel(
        join_solve_kernel,
        [blocks, partial, inner, outer, weights],
        [VECTOR, VECTOR, FACE, FACE],
        "solve_second",
        scratch=[spread],
    )
    inner, outer = exchange(inner, outer)
    (partial,) = kernel(apply_kernel, [blocks, *parts, s, weights], [VECTOR], "apply_second", scratch=[spread, products])
    count = lax.axis_size("cross")
    t, rows = kernel(
        sums_kernel,
        [partial, inner, outer, weights, r, z, w, s],
        [VECTOR, jax.ShapeDtypeStruct((count, 128), f32)],
        "sums",
    )
    rows = lax.all_to_all(rows.reshape(count, 1, 128), "cross", 0, 0)
    backs = kernel(
        last_solve_kernel, [blocks, z, w, s, t], [BACK] * 4, "solve_last", scratch=[spread, pltpu.VMEM((4, 16, 128), f32)]
    )
    returned = [backs[0]] + [around(backs[d], d) for d in (1, 2, 3)]
    (total,) = kernel(fold_kernel, [rows], [jax.ShapeDtypeStruct((8, 128), f32)], "fold")
    totals = [total] + [around(total, d) for d in (1, 2, 3)]
    (placed,) = kernel(place_kernel, [*returned, order], [jax.ShapeDtypeStruct((320, 128), f32)], "place")
    outs = kernel(final_kernel, [*totals, rhs_here, placed], [shape] * 3, "final")
    return tuple(out[None] for out in outs)


def solution(mesh):
    placed = (
        P("field", None, "cross"),
        P("field", None, None, "cross"),
        P("field", None, None, "cross"),
        P("field", None, None, "cross"),
        P("cross", None),
        P("cross", None),
    )
    return jax.shard_map(
        local,
        mesh=mesh,
        in_specs=placed,
        out_specs=(P("field", None, "cross"), P("field", None, "cross"), P("field", None, "cross")),
        check_vma=False,
    )
```

```python
import jax
import jax.numpy as jnp
from jax import lax
from jax.experimental import pallas as pl
from jax.experimental.pallas import tpu as pltpu
from jax.sharding import PartitionSpec as P


BLOCK_ROWS = 1024
COUPLING, WIDE, SHORT, CORNER, EDGE, RESIDUAL = (0, 1024, 1280, 1408, 1536, 1552)
FIRST_ROWS = 1552 + 32
SECOND_ROWS = RESIDUAL - WIDE
PIVOT = 1024
ELEMENT_ROWS = 2048
VMEM_LIMIT = 24 * 1024 * 1024

VMEM = pl.BlockSpec(memory_space=pltpu.VMEM)
HBM = pl.BlockSpec(memory_space=pltpu.HBM)

f32 = jnp.float32
bf16 = jnp.bfloat16


def params():
    return pltpu.CompilerParams(vmem_limit_bytes=VMEM_LIMIT)


def segment_of(shape):
    return lax.broadcasted_iota(jnp.int32, shape, 1) >> 5


def row_of(shape):
    return lax.broadcasted_iota(jnp.int32, shape, 0)


def matmul(left, right):
    return jnp.dot(left, right, preferred_element_type=f32)


def matmul_nt(left, right):
    return lax.dot_general(left, right, (((1,), (1,)), ((), ())), preferred_element_type=f32)


def bf16_parts(value, count):
    parts = []
    for _ in range(count):
        parts.append(value.astype(bf16))
        value = value - parts[-1].astype(f32)
    return parts


def start_fetch(sources, targets, sems):
    copies = [pltpu.make_async_copy(*pair, sems.at[i]) for i, pair in enumerate(zip(sources, targets, strict=True))]
    for copy in copies:
        copy.start()
    return copies


def send(left, sorting, outs, start, rows):
    result = matmul_nt(left, sorting).astype(bf16)
    for d in range(4):
        outs[d][start : start + rows, :] = result[:, d * 128 : (d + 1) * 128]


def hits_of(position, distance, line):
    return position == ((lax.axis_index("field") + distance) & 3) * 32 + line


def sorting_matrix(position):
    sub = row_of((128, 128))
    rows = []
    for d in range(4):
        hit = hits_of(position, d, sub & 31)
        rows.append(jnp.concatenate([jnp.where(hit & ((sub >> 5) == q), 1.0, 0.0) for q in range(4)], axis=1))
    return jnp.concatenate(rows, axis=0).astype(bf16)


def parts_of(block):
    def part(rows, column):
        return block[rows, 16 * column : 16 * column + 16, :].reshape(-1, 128)

    last, upper, lower = slice(48, 64), slice(32, 40), slice(40, 48)
    wide = [part(last, 0), part(last, 1), part(last, 2), part(slice(16, 32), 0)]
    short = [part(upper, 0), part(upper, 1), part(lower, 0), part(lower, 1)]
    shape = (16, 16, 128)
    major, minor = lax.broadcasted_iota(jnp.int32, shape, 0), lax.broadcasted_iota(jnp.int32, shape, 1)
    corner, edge = [], []
    for q in (0, 2):
        one, other = (
            block[16 * k : 16 * k + 16, 16 * k : 16 * k + 16, :].astype(f32) for k in (q, q + 1)
        )
        pair = jnp.where(minor <= major, one, other).astype(bf16)
        corner += [pair[0:8].reshape(128, 128), pair[8:16].reshape(128, 128)]
        edge += [jnp.zeros((16, 128), bf16), jnp.sum(jnp.where(minor == major, other, 0.0), axis=0).astype(bf16)]
    return [jnp.concatenate(parts, axis=1) for parts in (wide, short, corner, edge)]


def pack_first_kernel(neighbours, rhs, coupling, pivot, out0, out1, out2, out3, place, rhs_out, *scratch):
    *held, sems = scratch
    copies = start_fetch((neighbours, rhs, coupling, pivot), held, sems)
    neighbours, rhs, coupling, pivot = held
    cross = lax.axis_index("cross")
    square = (128, 128)
    lane = lax.broadcasted_iota(jnp.int32, square, 1)
    sub = row_of(square)
    copies[0].wait()

    def step_down(face):
        near = neighbours[face : face + 1, :] - cross * 128
        return jnp.where((near == sub) & (lane != sub), 1.0, 0.0).astype(bf16)

    ones = jnp.ones((16, 128), bf16)
    across = step_down(0)
    once = matmul(ones, across)
    twice = matmul(once.astype(bf16), across)
    column = once + twice + matmul(twice.astype(bf16), across)
    steps = []
    for face in (2, 3):
        jump = step_down(face)
        row = matmul(ones, jump)
        for turn in range(4):
            row = row + matmul(row.astype(bf16), jump)
            if turn < 3:
                jump = matmul(jump, jump).astype(bf16)
        steps.append(row)
    row = jnp.where(steps[0] < 16.0, steps[0], 31.0 - steps[1])
    owner = jnp.where(cross % 2 == 0, column, 3.0 - column)
    position = (owner * 32.0 + row).astype(jnp.int32)[0:1]

    place[...] = jnp.broadcast_to(position, place.shape)

    sorting = sorting_matrix(position)
    outs = (out0, out1, out2, out3)
    copies[2].wait()
    left = [coupling[:, 16 * q : 16 * q + 16, :].reshape(BLOCK_ROWS, 128) for q in range(4)]
    send(jnp.concatenate(left, axis=1), sorting, outs, COUPLING, BLOCK_ROWS)

    copies[1].wait()
    copies[3].wait()
    rhs_out[...] = rhs[...]
    rows = parts_of(pivot)
    for part in bf16_parts(rhs[...], 2):
        rows.append(jnp.concatenate([part[16 * q : 16 * q + 16] for q in range(4)], axis=1))
    send(jnp.concatenate(rows, axis=0), sorting, outs, WIDE, FIRST_ROWS - WIDE)


def pack_second_kernel(diagonal, face_type, place, after, out0, out1, out2, out3, weights, order, held, faces, sems):
    copies = start_fetch((diagonal, face_type), (held, faces), sems)
    sub = row_of((128, 128))
    position = place[0:1, :]
    order[...] = sorting_matrix(position)
    copies[0].wait()
    send(jnp.concatenate(parts_of(held), axis=0), order[...], (out0, out1, out2, out3), 0, SECOND_ROWS)

    copies[1].wait()
    interior = jnp.where(faces[...] == 0, 2.0, 0.0)
    own = interior + jnp.where(faces[...] == 1, 4.0, 0.0)
    table = jnp.concatenate([own, interior, jnp.zeros((8, 128), f32)], axis=0).astype(bf16)
    placed = matmul_nt(table, jnp.where(hits_of(position, 0, sub & 31), 1.0, 0.0).astype(bf16))
    shape = (16, 128)
    seg, m = segment_of(shape), row_of(shape)
    masks = [seg == 0, seg == 3, m < 4, m >= 12]
    total = jnp.zeros(shape, f32)
    for face in range(4):
        total = total + jnp.where(masks[face], placed[face : face + 1], 0.0)
        weights[1 + face] = jnp.where(masks[face], placed[4 + face : 5 + face], 0.0)
    weights[0] = total


def in_hbm(*arrays):
    return [pltpu.with_memory_space_constraint(array, pltpu.HBM) for array in arrays]


def to_packed(spread):
    seg = segment_of((16, 128))
    low = jnp.where(seg == 0, spread[0:16], spread[16:32])
    high = jnp.where(seg == 2, spread[32:48], spread[48:64])
    return jnp.where(seg < 2, low, high)


def to_spread(packed):
    seg = segment_of((16, 128))
    rolled = [packed] + [pltpu.roll(packed, 32 * k, 1) for k in (1, 2, 3)]
    parts = []
    for q in range(4):
        low = jnp.where(seg == 0, rolled[-q % 4], rolled[(1 - q) % 4])
        high = jnp.where(seg == 2, rolled[(2 - q) % 4], rolled[(3 - q) % 4])
        parts.append(jnp.where(seg < 2, low, high))
    return jnp.concatenate(parts, axis=0)


def over_segments(value):
    return (value + pltpu.roll(value, 32, 1)) + (pltpu.roll(value, 64, 1) + pltpu.roll(value, 96, 1))


def transposed_times(blocks, elem, start, spread, row_ref):
    row_ref[...] = spread
    sums = [None] * 4
    for a in range(64):
        term = blocks[elem, start + 16 * a : start + 16 * a + 16, :].astype(f32) * row_ref[a : a + 1, :]
        sums[a % 4] = term if sums[a % 4] is None else sums[a % 4] + term
    return (sums[0] + sums[1]) + (sums[2] + sums[3])


def times(blocks, elem, start, packed):
    block = blocks[elem, start : start + BLOCK_ROWS, :].astype(f32).reshape(64, 16, 128)
    return over_segments(jnp.sum(block * packed[None], axis=1))


def turn_segments(rows):
    seg = segment_of(rows[0].shape)
    rows = list(rows)
    for width, low in ((2, seg < 2), (1, (seg & 1) == 0)):
        for j in range(4):
            if j & width:
                continue
            x, y = rows[j], rows[j + width]
            rows[j] = jnp.where(low, x, pltpu.roll(y, 32 * width, 1))
            rows[j + width] = jnp.where(low, pltpu.roll(x, 128 - 32 * width, 1), y)
    return rows


def corner_row(read, k):
    odd = segment_of((16, 128)) % 2 == 1
    start = CORNER - WIDE + 16 * (k % 8)
    row = read(start, 16)
    if k < 8:
        return jnp.where(odd, pltpu.roll(row, 32, 1), row)
    return jnp.where(odd, row, pltpu.roll(row, 96, 1))


def unpack(chunk, blocks, wide):
    shape = (16, 128)
    seg, m = segment_of(shape), row_of(shape)

    def read(start, rows):
        return chunk[start : start + rows, :].astype(f32)

    blocks[0:BLOCK_ROWS, :] = chunk[COUPLING : COUPLING + BLOCK_ROWS, :]
    for k in range(16):
        corner = corner_row(lambda start, rows: read(WIDE + start, rows), k)
        last = read(WIDE + 16 * k, 16)
        third = read(SHORT + 16 * (k % 8), 16)
        if k >= 8:
            third = pltpu.roll(third, 64, 1)
        wide[16 * k : 16 * k + 16, :] = corner
        wide[256 + 16 * k : 272 + 16 * k, :] = jnp.where(seg == 0, pltpu.roll(last, 32, 1), corner)
        wide[512 + 16 * k : 528 + 16 * k, :] = jnp.where(seg == 2, corner, third)
        wide[768 + 16 * k : 784 + 16 * k, :] = jnp.where(seg == 3, corner, last)
    edge = read(EDGE, 16)
    for k in range(16):
        turned = turn_segments([wide[pl.ds(256 * q + k, 16, stride=16), :] for q in range(4)])
        for q in range(4):
            a = 16 * q + k
            here = (seg < q) | ((seg == q) & ((m <= k) if q % 2 == 0 else (m > k)))
            value = jnp.where(here, wide[16 * a : 16 * a + 16, :], turned[q])
            if q % 2 == 1:
                value = jnp.where((seg == q) & (m == k), edge, value)
            blocks[PIVOT + 16 * a : PIVOT + 16 * a + 16, :] = value.astype(bf16)
    return read(RESIDUAL, 16) + read(RESIDUAL + 16, 16)


def diagonal_times(parts, packed):
    shape = (16, 128)
    seg, m = segment_of(shape), row_of(shape)
    spread = to_spread(packed)
    v0, v1, v2, v3 = (spread[16 * q : 16 * q + 16] for q in range(4))

    def both_ways(block, count, across, along):
        down = [block[k] * across[k : k + 1] for k in range(count)]
        while len(down) > 1:
            down = [x + y for x, y in zip(down[::2], down[1::2], strict=True)]
        return down[0], jnp.sum(block * along[None], axis=1)

    odd = seg % 2 == 1
    diagonal = parts[EDGE - WIDE : EDGE - WIDE + 16, :].astype(f32)
    corner = []
    for k in range(16):
        row = corner_row(lambda start, rows: parts[start : start + rows, :].astype(f32), k)
        diagonal = jnp.where((m == k) & ~odd, row, diagonal)
        corner.append(jnp.where(jnp.where(odd, m - k, k - m) > 0, row, 0.0))
    down, right = both_ways(jnp.concatenate(corner, axis=0).reshape(16, 16, 128), 16, packed, packed)
    total = down + right + diagonal * packed
    wide = parts[0 : SHORT - WIDE, :].astype(f32).reshape(16, 16, 128)
    down, right = both_ways(wide, 16, jnp.where(seg == 3, v1, v3), jnp.where(seg == 3, v0, packed))
    total = total + jnp.where(seg < 3, down, 0.0) + jnp.where(seg == 0, pltpu.roll(down, 32, 1), 0.0)
    turned = [pltpu.roll(right, 32 * k, 1) for k in (1, 2, 3)]
    total = total + jnp.where(seg == 3, (turned[0] + turned[1]) + turned[2], jnp.where(seg == 1, turned[1], 0.0))
    short = parts[SHORT - WIDE : CORNER - WIDE, :].astype(f32).reshape(8, 16, 128)
    down, right = both_ways(short, 8, jnp.where(seg[0:8] < 2, v2[0:8], v2[8:16]), jnp.where(odd, v1, v0))
    total = total + jnp.where(seg < 2, down + pltpu.roll(down, 64, 1), 0.0)
    upper = pltpu.roll(right, 64, 1) + pltpu.roll(right, 32, 1)
    lower = right + pltpu.roll(right, 96, 1)
    return total + jnp.where(seg == 2, jnp.concatenate([upper, lower], axis=0), 0.0)


def line_solve(residual, blocks, row_ref):
    forward = []
    for elem in range(4):
        right = to_spread(residual[elem])
        if elem > 0:
            right = right - times(blocks, elem, COUPLING, forward[-1])
        forward.append(transposed_times(blocks, elem, PIVOT, right, row_ref))
    values = [None] * 4
    carried = None
    for elem in reversed(range(4)):
        value = to_spread(forward[elem])
        if carried is not None:
            value = value - times(blocks, elem, PIVOT, carried)
        values[elem] = value
        if elem > 0:
            carried = transposed_times(blocks, elem, COUPLING, value, row_ref)
    return values


def is_even_column():
    return (lax.axis_index("field") + lax.axis_index("cross")) % 2 == 0


def send_faces(packed, inner, outer):
    seg = segment_of((16, 128))
    to_next, to_before = packed[3], packed[0]
    for elem in range(3):
        to_next = jnp.where(seg == elem, pltpu.roll(packed[elem], 32 * (elem + 1), 1), to_next)
        to_before = jnp.where(seg == elem + 1, pltpu.roll(packed[elem + 1], 32 * (elem + 1), 1), to_before)
    even = is_even_column()
    inner[...] = jnp.where(even, to_next, to_before)
    outer[...] = jnp.where(even, to_before, to_next)


def line_apply(packed, blocks, products, weights, row_ref):
    spread = [to_spread(v) for v in packed]
    rows = []
    for elem in range(4):
        v = packed[elem]
        total = products[elem]
        if elem > 0:
            total = total + to_packed(times(blocks, elem, COUPLING, packed[elem - 1]))
        if elem < 3:
            total = total + transposed_times(blocks, elem + 1, COUPLING, spread[elem + 1], row_ref)
        below = pltpu.roll(pltpu.roll(v, 4, 0), 1, 1)
        above = pltpu.roll(pltpu.roll(v, 12, 0), 127, 1)
        rows.append(total + weights[0] * v - weights[3] * below - weights[4] * above)
    return rows


def add_faces(partial, inner, outer, weights):
    even = is_even_column()
    before = jnp.where(even, outer[...], inner[...])
    after = jnp.where(even, inner[...], outer[...])
    rows = []
    for elem in range(4):
        left = before if elem == 0 else pltpu.roll(before, 128 - 32 * elem, 1)
        right = after if elem == 3 else pltpu.roll(after, 32 * (3 - elem), 1)
        rows.append(partial[elem] - weights[1] * left - weights[2] * right)
    return rows


def product_sum(first, second):
    total = first[0] * second[0]
    for elem in range(1, 4):
        total = total + first[elem] * second[elem]
    return jnp.sum(total, axis=0, keepdims=True)


def unpack_kernel(chunk, blocks, residual, wide):
    residual[...] = unpack(chunk, blocks, wide)


def solve_kernel(b0, r0, b1, r1, b3, r3, chunk, blocks, residual, values, inner_out, outer_out, row_ref, wide, sems):
    me = lax.axis_index("field")
    copies = []
    for d, source, part in ((0, b0, r0), (1, b1, r1), (3, b3, r3)):
        elem = (me - d) & 3
        residual[elem] = part[...]
        copies.append(pltpu.make_async_copy(source, blocks.at[elem], sems.at[d]))
    for copy in copies:
        copy.start()
    elem = (me - 2) & 3
    residual[elem] = unpack(chunk, blocks.at[elem], wide)
    for copy in copies:
        copy.wait()
    packed = [to_packed(v) for v in line_solve([residual[elem] for elem in range(4)], blocks, row_ref)]
    for elem in range(4):
        values[elem] = packed[elem]
    send_faces(packed, inner_out, outer_out)


def apply_kernel(blocks, p0, p1, p2, p3, vector, weights, partial, row_ref, products):
    me = lax.axis_index("field")
    for d, parts in enumerate((p0, p1, p2, p3)):
        elem = (me - d) & 3
        products[elem] = diagonal_times(parts, vector[elem])
    rows = line_apply([vector[elem] for elem in range(4)], blocks, products, weights, row_ref)
    for elem in range(4):
        partial[elem] = rows[elem]


def join_solve_kernel(blocks, partial, inner, outer, weights, image, values, inner_out, outer_out, row_ref):
    rows = add_faces(partial, inner, outer, weights)
    packed = [to_packed(v) for v in line_solve(rows, blocks, row_ref)]
    for elem in range(4):
        image[elem] = rows[elem]
        values[elem] = packed[elem]
    send_faces(packed, inner_out, outer_out)


def sums_kernel(partial, inner, outer, weights, r, z, w, s, image, sums):
    rows = add_faces(partial, inner, outer, weights)

    def values(ref):
        return [ref[elem] for elem in range(4)]

    z_, w_, s_ = values(z), values(w), values(s)
    seg = segment_of((1, 128))
    total = jnp.zeros((1, 128), f32)
    for index, pair in enumerate(((values(r), z_), (z_, w_), (w_, s_), (s_, rows))):
        total = jnp.where(seg == index, over_segments(product_sum(*pair)), total)
    for elem in range(4):
        image[elem] = rows[elem]
    sums[...] = jnp.broadcast_to(total, sums.shape)


def fold_kernel(rows, total):
    total[...] = jnp.broadcast_to(jnp.sum(rows[...], axis=0), total.shape)


def last_solve_kernel(blocks, z, w, s, t, back0, back1, back2, back3, row_ref, u):
    packed = [to_packed(v) for v in line_solve([t[elem] for elem in range(4)], blocks, row_ref)]
    for elem in range(4):
        u[elem] = packed[elem]
    me = lax.axis_index("field")
    for d, back in enumerate((back0, back1, back2, back3)):
        elem = (me + d) & 3
        for index, ref in enumerate((z, w, s, t, u)):
            back[16 * index : 16 * index + 16, :] = ref[elem]


def place_kernel(b0, b1, b2, b3, order, placed):
    vectors = jnp.concatenate([b[...] for b in (b0, b3, b2, b1)], axis=1)
    moved = matmul(jnp.concatenate(bf16_parts(vectors, 3), axis=0), order[...])
    value = (moved[0:80] + moved[80:160]) + moved[160:240]
    for index in range(5):
        for q in range(4):
            start = 64 * index + 16 * q
            placed[start : start + 16, :] = value[16 * index : 16 * index + 16, 128 * q : 128 * q + 128]


def final_kernel(s0, s1, s2, s3, rhs, placed, solution, residual, precond):
    z, w, s, t, u = (placed[64 * index : 64 * index + 64, :] for index in range(5))
    total = ((s0[...] + s1[...]) + (s2[...] + s3[...]))[0:1]
    totals = [jnp.sum(total[:, 32 * k : 32 * k + 32], axis=1, keepdims=True) for k in range(4)]
    rho, curve, second, third = totals
    alpha = rho / curve
    rho_next = rho - 2.0 * alpha * curve + alpha * alpha * second
    grown = 1.0 + rho_next / rho
    curve_next = grown * grown * curve - 2.0 * alpha * grown * second + alpha * alpha * third
    alpha_next = rho_next / curve_next
    first = alpha + alpha_next * grown
    other = alpha_next * alpha
    solution[...] = first * z - other * s
    residual[...] = rhs[...] + (other * t - first * w)
    precond[...] = z - first * s + other * u


FACE = jax.ShapeDtypeStruct((16, 128), f32)
VECTOR = jax.ShapeDtypeStruct((4, 16, 128), f32)
BACK = jax.ShapeDtypeStruct((80, 128), f32)
BLOCKS = jax.ShapeDtypeStruct((4, ELEMENT_ROWS, 128), bf16)


def kernel(body, arrays, outs, name, spec=VMEM, scratch=()):
    return pl.pallas_call(
        body,
        out_shape=outs,
        in_specs=spec if isinstance(spec, list) else [spec] * len(arrays),
        out_specs=[VMEM] * len(outs),
        scratch_shapes=list(scratch),
        compiler_params=params(),
        name=name,
    )(*arrays)


def around(value, distance):
    count = lax.axis_size("field")
    return lax.ppermute(value, "field", [(i, (i + distance) % count) for i in range(count)])


def column_swaps(first):
    field, cross = lax.axis_size("field"), lax.axis_size("cross")
    device = {}
    for c in range(cross):
        for f in range(field):
            device[field * c + (f if c % 2 == 0 else field - 1 - f)] = f * cross + c
    pairs = [(device[g], device[g + 1]) for g in range(first, field * cross - 1, 2)]
    return pairs + [(b, a) for a, b in pairs]


def exchange(inner, outer):
    return [lax.ppermute(faces, ("field", "cross"), column_swaps(first)) for first, faces in enumerate((inner, outer))]


def local(rhs, pivot_inverse, line_coupling, element_block, neighbours, face_type):
    matrix, small = pltpu.VMEM((64, 64, 128), bf16), pltpu.VMEM((4, 128), jnp.int32)
    spread, wide = pltpu.VMEM((64, 128), f32), pltpu.VMEM((BLOCK_ROWS + 16, 128), f32)
    shape = jax.ShapeDtypeStruct((64, 128), f32)
    *chunks, place, rhs_here = kernel(
        pack_first_kernel,
        in_hbm(neighbours.T, rhs[0], line_coupling[0], pivot_inverse[0]),
        [jax.ShapeDtypeStruct((FIRST_ROWS, 128), bf16)] * 4 + [jax.ShapeDtypeStruct((8, 128), jnp.int32), shape],
        "pack_first",
        HBM,
        [small, pltpu.VMEM((64, 128), f32), matrix, matrix, pltpu.SemaphoreType.DMA((4,))],
    )
    held = []
    first = {d: around(chunks[d], d) if d else chunks[0] for d in (0, 1, 3, 2)}
    for d in (0, 1, 3):
        last = kernel(
            unpack_kernel,
            [first[d]],
            [jax.ShapeDtypeStruct((ELEMENT_ROWS, 128), bf16), FACE],
            f"unpack_{d}",
            scratch=[wide],
        )
        held += last
        if d == 1:
            *chunks, weights, order = kernel(
                pack_second_kernel,
                in_hbm(element_block[0], face_type.T) + [place, last[1]],
                [jax.ShapeDtypeStruct((SECOND_ROWS, 128), bf16)] * 4
                + [jax.ShapeDtypeStruct((5, 16, 128), f32), jax.ShapeDtypeStruct((512, 512), bf16)],
                "pack_second",
                [HBM, HBM, VMEM, VMEM],
                [matrix, small, pltpu.SemaphoreType.DMA((2,))],
            )
            second = {d: around(chunks[d], d) if d else chunks[0] for d in (0, 1, 3, 2)}
    blocks, r, z, inner, outer = kernel(
        solve_kernel,
        [*held, first[2]],
        [BLOCKS, VECTOR, VECTOR, FACE, FACE],
        "solve_first",
        scratch=[spread, wide, pltpu.SemaphoreType.DMA((4,))],
    )
    inner, outer = exchange(inner, outer)
    parts = [second[d] for d in range(4)]
    products = pltpu.VMEM((4, 16, 128), f32)
    (partial,) = kernel(apply_kernel, [blocks, *parts, z, weights], [VECTOR], "apply_first", scratch=[spread, products])
    w, s, inner, outer = kernel(
        join_solve_kernel,
        [blocks, partial, inner, outer, weights],
        [VECTOR, VECTOR, FACE, FACE],
        "solve_second",
        scratch=[spread],
    )
    inner, outer = exchange(inner, outer)
    (partial,) = kernel(apply_kernel, [blocks, *parts, s, weights], [VECTOR], "apply_second", scratch=[spread, products])
    count = lax.axis_size("cross")
    t, rows = kernel(
        sums_kernel,
        [partial, inner, outer, weights, r, z, w, s],
        [VECTOR, jax.ShapeDtypeStruct((count, 128), f32)],
        "sums",
    )
    rows = lax.all_to_all(rows.reshape(count, 1, 128), "cross", 0, 0)
    backs = kernel(
        last_solve_kernel, [blocks, z, w, s, t], [BACK] * 4, "solve_last", scratch=[spread, pltpu.VMEM((4, 16, 128), f32)]
    )
    returned = [backs[0]] + [around(backs[d], d) for d in (1, 2, 3)]
    (total,) = kernel(fold_kernel, [rows], [jax.ShapeDtypeStruct((8, 128), f32)], "fold")
    totals = [total] + [around(total, d) for d in (1, 2, 3)]
    (placed,) = kernel(place_kernel, [*returned, order], [jax.ShapeDtypeStruct((320, 128), f32)], "place")
    outs = kernel(final_kernel, [*totals, rhs_here, placed], [shape] * 3, "final")
    return tuple(out[None] for out in outs)


def solution(mesh):
    placed = (
        P("field", None, "cross"),
        P("field", None, None, "cross"),
        P("field", None, None, "cross"),
        P("field", None, None, "cross"),
        P("cross", None),
        P("cross", None),
    )
    return jax.shard_map(
        local,
        mesh=mesh,
        in_specs=placed,
        out_specs=(P("field", None, "cross"), P("field", None, "cross"), P("field", None, "cross")),
        check_vma=False,
    )
```
